32 devices in a mesh: seq: 4 (over z), fsdp: 8 (over y, x, core).
Axes of the slice: x: 2, y: 2, z: 4, core: 2. Of those that a mesh axis runs over, the one named last changes fastest.
Arguments:
- tokens: bfloat16 [4096, 1024], P(('fsdp', 'seq')), may hold values from -6 to 6
- cotangent: bfloat16 [4096, 1024], P(('fsdp', 'seq')), may hold values from -6 to 6
- doc_starts: int32 [8], replicated, may hold values from 0 to 4095, as said below
- variate_ids: int32 [4096], replicated, may hold values from 0 to 7, as said below
- time_ids: int32 [4096], replicated, may hold values from 0 to 63, as said below
- gain_attn: float32 [1024], replicated, may hold values from 0.5 to 1.5
- w_attn: bfloat16 [1024, 3072], P('fsdp'), may hold values from -0.1875 to 0.1875
- gain_query: float32 [64], replicated, may hold values from 0.5 to 1.5
- gain_key: float32 [64], replicated, may hold values from 0.5 to 1.5
- variate_bias: float32 [16, 2], replicated, may hold values from -3 to 3
- w_output: bfloat16 [1024, 1024], P('fsdp'), may hold values from -3 to 3
- gain_feed: float32 [1024], replicated, may hold values from 0.5 to 1.5
- w_gate: bfloat16 [1024, 4096], P('fsdp'), may hold values from -0.1875 to 0.1875
- w_up: bfloat16 [1024, 4096], P('fsdp'), may hold values from -0.1875 to 0.1875
- w_down: bfloat16 [4096, 1024], P('fsdp'), may hold values from -0.09375 to 0.09375
Outputs:
- layer_out: bfloat16 [4096, 1024], P(('fsdp', 'seq'))
- tokens_grad: float32 [4096, 1024], P(('fsdp', 'seq'))
- attn_grad: float32 [1024, 3072], P(('seq', 'fsdp'))
- output_grad: float32 [1024, 1024], P(('seq', 'fsdp'))
- gate_grad: float32 [1024, 4096], P(('seq', 'fsdp'))
- up_grad: float32 [1024, 4096], P(('seq', 'fsdp'))
- down_grad: float32 [4096, 1024], P(('seq', 'fsdp'))
- attn_gain_grad: float32 [1024], P(('seq', 'fsdp'))
- feed_gain_grad: float32 [1024], P(('seq', 'fsdp'))
- query_gain_grad: float32 [64], replicated
- key_gain_grad: float32 [64], replicated
- bias_grad: float32 [16, 2], replicated
The draws below stay inside these ranges and needn't reach their ends.
Inputs may be any that keep to these rules, and one draw needn't show every extreme that they name: `doc_starts`: non-decreasing, the first entry is 0. `variate_ids`: only compared for equality within a document. `time_ids`: a time index modulo 64; token 0 has 63.
All inputs are finite; a program needn't handle non-finite values.
Results may differ from the reference program's by a relative error of at most 0.038.
Values may be sent and summed in bfloat16 or wider, within the bound.
A program may use at most 256 MiB of HBM per device.

```python
import jax
import jax.numpy as jnp
from jax import lax

D = 1024
HEADS = 16
HEAD_DIM = 64
FF = 4096
DOCS = 8
GROUP = 512
TOKENS = 4096


def layout(key):
    positions = jnp.arange(TOKENS, dtype=jnp.int32)
    streams = jax.random.split(key, 6)
    opening = jax.random.randint(streams[0], (), 1, GROUP)
    closing = jax.random.randint(streams[1], (), TOKENS - GROUP + 1, TOKENS)
    pick_values = jax.random.randint(streams[2], (DOCS - 3,), 0, 1 << 20)
    side_coins = jax.random.randint(streams[3], (DOCS - 3,), 0, 2)
    early_pos = 1 + pick_values % jnp.maximum(opening - 1, 1)
    late_pos = closing + 1 + pick_values % jnp.maximum(TOKENS - closing - 1, 1)
    can_early = opening > 1
    can_late = closing < TOKENS - 1
    pick_late = jnp.logical_and(can_late, jnp.logical_or(side_coins == 1, jnp.logical_not(can_early)))
    chosen = jnp.where(pick_late, late_pos, jnp.where(can_early, early_pos, 0))
    starts = jnp.sort(jnp.concatenate([jnp.zeros((1,), jnp.int32), jnp.stack([opening, closing]), chosen]))
    breaks = jax.random.randint(streams[4], (TOKENS,), 0, max(GROUP // 2, 2)) == 0
    at_start = jnp.any(positions[:, None] == starts[None, :], axis=1)
    breaks = jnp.logical_or(breaks, at_start)
    breaks = jnp.logical_or(breaks, positions % (TOKENS // 8) == 0)
    run_ids = jnp.cumsum(breaks.astype(jnp.int32)) - 1
    run_first = lax.cummax(jnp.where(breaks, positions, 0), axis=0)
    offsets = jax.random.randint(streams[5], (TOKENS,), 0, 64)
    offsets = offsets.at[0].set(63)
    time_values = (positions - run_first + offsets[run_first]) % 64
    return (starts, run_ids % 8, time_values)


def draw_doc_starts(key, part):
    shared = layout(key)
    return shared[0]


def draw_variate_ids(key, part):
    shared = layout(key)
    return shared[1]


def draw_time_ids(key, part):
    shared = layout(key)
    return shared[2]


def steps_of(rng, dims, pieces, least, high):
    def one(dim, shards_of):
        draws = jax.random.uniform(jax.random.fold_in(jax.random.fold_in(rng, 6), dim), (shards_of,), jnp.float32, least / len(pieces), high / len(pieces))
        return jnp.repeat(jnp.exp(draws), dims[dim] // shards_of).reshape((-1,) + (1,) * (len(dims) - dim - 1))

    level = one(*pieces[0])
    for cut in pieces[1:]:
        level = level * one(*cut)
    return level


def noise(stream_key, extent, deviation, limit, cuts=(), kind=jnp.bfloat16):
    factor_of = steps_of(stream_key, extent, cuts, -0.22, 0.18) if cuts else 1.0
    drawn = jax.random.normal(stream_key, extent, jnp.float32) * deviation * factor_of
    return jnp.minimum(jnp.maximum(drawn, -limit), limit).astype(kind)


def setup_inputs(seed: int = 0) -> dict:
    keys = jax.random.split(jax.random.key(seed), 16)
    return {
        "tokens": noise(keys[0], (TOKENS, D), 1.0, 6.0, ((0, 32),)),
        "cotangent": noise(keys[1], (TOKENS, D), 1.0, 6.0, ((0, 32),)),
        "doc_starts": draw_doc_starts(jax.random.fold_in(keys[15], 71), 0),
        "variate_ids": draw_variate_ids(jax.random.fold_in(keys[15], 71), 0),
        "time_ids": draw_time_ids(jax.random.fold_in(keys[15], 71), 0),
        "gain_attn": jnp.clip(1.0 + 0.1 * jax.random.normal(keys[5], (D,), jnp.float32), 0.5, 1.5),
        "w_attn": noise(keys[6], (D, 3 * HEADS * HEAD_DIM), D ** -0.5, 0.1875, ((0, 8),)),
        "gain_query": jnp.clip(1.0 + 0.1 * jax.random.normal(keys[7], (HEAD_DIM,), jnp.float32), 0.5, 1.5),
        "gain_key": jnp.clip(1.0 + 0.1 * jax.random.normal(keys[8], (HEAD_DIM,), jnp.float32), 0.5, 1.5),
        "variate_bias": noise(keys[9], (HEADS, 2), 1.0, 3.0, (), jnp.float32),
        "w_output": noise(keys[10], (HEADS * HEAD_DIM, D), (max(1, (HEADS * HEAD_DIM * 16) // TOKENS)) ** -0.5, 3.0, ((0, 8),)),
        "gain_feed": jnp.clip(1.0 + 0.1 * jax.random.normal(keys[11], (D,), jnp.float32), 0.5, 1.5),
        "w_gate": noise(keys[12], (D, FF), D ** -0.5, 0.1875, ((0, 8),)),
        "w_up": noise(keys[13], (D, FF), D ** -0.5, 0.1875, ((0, 8),)),
        "w_down": noise(keys[14], (FF, D), FF ** -0.5, 0.09375, ((0, 8),)),
    }


EPSILON = 1e-06
NEG_FILL = -1e+30
FULL_PRECISION = lax.Precision.HIGHEST

@jax.custom_vjp
def low(v):
    return lax.optimization_barrier(v.astype(jnp.bfloat16)).astype(jnp.float32)

@jax.custom_vjp
def low_back(v):
    return v

def low_keep(v):
    return (low(v), None)

def low_pass(kept, grad):
    return (grad,)

def back_keep(v):
    return (v, None)

def back_low(kept, grad):
    return (low(grad),)
low.defvjp(low_keep, low_pass)
low_back.defvjp(back_keep, back_low)

def rms_scale(vector, gain):
    return vector * lax.rsqrt(lax.optimization_barrier(jnp.mean(vector * vector, axis=-1, keepdims=True)) + EPSILON) * gain

def rotate(vector, angles):
    half_width = vector.shape[-1] // 2
    front_half = vector[..., :half_width]
    back_half = vector[..., half_width:]
    cosine = jnp.cos(angles)
    sine_part = jnp.sin(angles)
    return jnp.concatenate([front_half * cosine - back_half * sine_part, front_half * sine_part + back_half * cosine], axis=-1)

def angle_table(times, width):
    half_width = width // 2
    frequency = 10000.0 ** (-2.0 * jnp.arange(half_width, dtype=jnp.float32) / width)
    return times.astype(jnp.float32)[:, None, None] * frequency

def doc_index(positions, starts):
    return lax.optimization_barrier(jnp.sum((starts[None, :] <= positions[:, None]).astype(jnp.int32), axis=1)) - 1

def head_attention(queries, key_rows, values, bias_pair, doc_ids, variates):
    score_scale = HEAD_DIM ** (-0.5)

    def one_block(block_inputs):
        query_block, query_docs, query_vars = block_inputs
        scores = jnp.dot(query_block, key_rows.T, precision=FULL_PRECISION) * score_scale
        scores = scores + jnp.where(query_vars[:, None] == variates[None, :], bias_pair[0], bias_pair[1])
        scores = jnp.where(query_docs[:, None] == doc_ids[None, :], scores, NEG_FILL)
        scores = low_back(scores)
        row_top = lax.optimization_barrier(jnp.max(scores, axis=1, keepdims=True))
        weights = jnp.exp(scores - row_top)
        soft_probs = weights / lax.optimization_barrier(jnp.sum(weights, axis=1, keepdims=True))
        return jnp.dot(low(soft_probs), values, precision=FULL_PRECISION)
    block_count = queries.shape[0] // 512
    results = lax.map(jax.checkpoint(one_block), (queries.reshape(block_count, 512, -1), doc_ids.reshape(block_count, 512), variates.reshape(block_count, 512)))
    return results.reshape(queries.shape)

def attention(queries, key_rows, values, variate_bias, doc_ids, variates):

    def one_head(head_inputs):
        return head_attention(head_inputs[0], head_inputs[1], head_inputs[2], head_inputs[3], doc_ids, variates)
    results = lax.map(one_head, (jnp.transpose(queries, (1, 0, 2)), jnp.transpose(key_rows, (1, 0, 2)), jnp.transpose(values, (1, 0, 2)), variate_bias))
    return jnp.transpose(results, (1, 0, 2))

def reference(tokens, cotangent, doc_starts, variate_ids, time_ids, gain_attn, w_attn, gain_query, gain_key, variate_bias, w_output, gain_feed, w_gate, w_up, w_down):
    positions = jnp.arange(TOKENS, dtype=jnp.int32)
    doc_ids = doc_index(positions, doc_starts)
    angles = angle_table(time_ids, HEAD_DIM)

    def layer_forward(inputs, g_attn, m_attn, g_query, g_key, bias_table, m_output, g_feed, m_gate, m_up, m_down):
        normed = low(rms_scale(inputs, g_attn))
        projected = low_back(jnp.dot(normed, m_attn, precision=FULL_PRECISION)).reshape(TOKENS, 3, HEADS, HEAD_DIM)
        queries = low_back(low(rotate(rms_scale(projected[:, 0], g_query), angles)))
        key_rows = low_back(low(rotate(rms_scale(projected[:, 1], g_key), angles)))
        values = low_back(low(projected[:, 2]))
        attended = attention(queries, key_rows, values, bias_table, doc_ids, variate_ids)
        heads_out = low_back(low(attended.reshape(TOKENS, HEADS * HEAD_DIM)))
        middle = inputs + low_back(jnp.dot(heads_out, m_output, precision=FULL_PRECISION))
        normed_mid = low(rms_scale(middle, g_feed))
        gate_act = low_back(jnp.dot(normed_mid, m_gate, precision=FULL_PRECISION))
        up_act = low_back(jnp.dot(normed_mid, m_up, precision=FULL_PRECISION))
        hidden = low(jax.nn.silu(gate_act) * up_act)
        return middle + low_back(jnp.dot(hidden, m_down, precision=FULL_PRECISION))
    result, pull_back = jax.vjp(layer_forward, tokens.astype(jnp.float32), gain_attn, w_attn.astype(jnp.float32), gain_query, gain_key, variate_bias, w_output.astype(jnp.float32), gain_feed, w_gate.astype(jnp.float32), w_up.astype(jnp.float32), w_down.astype(jnp.float32))
    gradients = pull_back(cotangent.astype(jnp.float32))
    return (result.astype(jnp.bfloat16), gradients[0], gradients[2], gradients[6], gradients[8], gradients[9], gradients[10], gradients[1], gradients[7], gradients[3], gradients[4], gradients[5])
```

```python
import functools

import jax
import jax.numpy as jnp
from jax import lax
from jax.experimental import pallas as pl
from jax.experimental.pallas import tpu as pltpu
from jax.sharding import PartitionSpec as P

EPSILON = 1e-06
F32, BF16 = jnp.float32, jnp.bfloat16
VARIATES = 8
AWAY = 1024.0
QUERY_BLOCK = 256
LSE_ROW, VAR_ROW = 32, 40
MESH = pl.DeviceIdType.MESH
ANY = pl.BlockSpec(memory_space=pl.ANY)
VMEM = pl.BlockSpec(memory_space=pltpu.VMEM)
VMEM_BYTES = 48 * 2**20


def nn(a, b):
    return jnp.dot(a, b, preferred_element_type=F32)


def nt(a, b):
    return lax.dot_general(a, b, (((1,), (1,)), ((), ())), preferred_element_type=F32)


def tn(a, b):
    return lax.dot_general(a, b, (((0,), (0,)), ((), ())), preferred_element_type=F32)


def pieces(values):
    high = values.astype(BF16).astype(F32)
    middle = (values - high).astype(BF16).astype(F32)
    return high, middle, (values - high - middle).astype(BF16).astype(F32)


def send_all(plan, send_sems, recv_sems, local_sems):
    remote, local = plan
    copies = []
    for n, (src, dst, device, may_send, may_receive) in enumerate(remote):
        copy = pltpu.make_async_remote_copy(
            src_ref=src,
            dst_ref=dst,
            send_sem=send_sems.at[n],
            recv_sem=recv_sems.at[n],
            device_id=device,
            device_id_type=MESH,
        )
        when(may_send, copy.start)
        copies.append((copy, may_send, may_receive))
    locals_ = []
    for n, (src, dst, may) in enumerate(local):
        copy = pltpu.make_async_copy(src, dst, local_sems.at[n])
        when(may, copy.start)
        locals_.append((copy, may))

    def finish():
        for copy, may in locals_:
            when(may, copy.wait)
        for copy, may_send, may_receive in copies:
            when(may_send, copy.wait_send)
            when(may_receive, copy.wait_recv)

    return finish


def when(condition, action):
    if condition is None:
        action()
    else:
        pl.when(condition)(action)


def greet(devices):
    barrier = pltpu.get_barrier_semaphore()
    for device in devices:
        pl.semaphore_signal(barrier, inc=1, device_id=device, device_id_type=MESH)
    pl.semaphore_wait(barrier, len(devices))


def exchange(number, inputs, out_shapes, make_plan, peers, counts):
    def kernel(*refs):
        ins = refs[: len(inputs)]
        outs = refs[len(inputs) : len(inputs) + len(out_shapes)]
        send_sems, recv_sems, local_sems = refs[-3:]
        s, f = lax.axis_index("seq"), lax.axis_index("fsdp")
        greet(peers(s, f))
        send_all(make_plan(s, f, ins, outs), send_sems, recv_sems, local_sems)()

    return pl.pallas_call(
        kernel,
        in_specs=[ANY] * len(inputs),
        out_specs=[ANY] * len(out_shapes),
        out_shape=out_shapes,
        scratch_shapes=[
            pltpu.SemaphoreType.DMA((counts[0],)),
            pltpu.SemaphoreType.DMA((counts[0],)),
            pltpu.SemaphoreType.DMA((max(counts[1], 1),)),
        ],
        compiler_params=pltpu.CompilerParams(collective_id=number, has_side_effects=True),
    )(*inputs)


def shape(dims, dtype=BF16):
    return jax.ShapeDtypeStruct(tuple(dims), dtype)


def join(a, b):
    return jnp.concatenate([a, b], axis=0)


def forward_kernel(q_ref, kv_ref, qa_ref, ka_ref, o_ref, att_ref, lse_ref):
    width, rows = q_ref.shape[1:]
    blocks = rows // QUERY_BLOCK

    def block(i, _):
        j = i // blocks
        cols = pl.ds(pl.multiple_of((i % blocks) * QUERY_BLOCK, QUERY_BLOCK), QUERY_BLOCK)
        queries = join(q_ref[j, :, cols], qa_ref[j, :, cols]).T
        total = jnp.zeros((QUERY_BLOCK, 2 * width), F32)
        for g in range(kv_ref.shape[0]):
            keys = join(kv_ref[g, :width, :], ka_ref[g])
            values = join(kv_ref[g, width:, :], jnp.ones((width, rows), BF16))
            weights = jnp.exp(nn(queries, keys)).astype(BF16)
            total += nt(weights, values)
        total = total.T
        weight_sum = total[width : width + 1]
        attended = total[:width] / weight_sum
        att_ref[j, :, cols] = attended
        o_ref[j, :, cols] = attended.astype(BF16)
        lse_ref[j, :, cols] = jnp.log(weight_sum)
        return 0

    lax.fori_loop(0, q_ref.shape[0] * blocks, block, 0)


def attention_forward(q, kv, qa, ka):
    groups, width, rows = q.shape
    return pl.pallas_call(
        forward_kernel,
        in_specs=[VMEM] * 4,
        out_specs=[VMEM] * 3,
        out_shape=[shape(q.shape), shape(q.shape, F32), shape((groups, 1, rows), F32)],
        compiler_params=pltpu.CompilerParams(vmem_limit_bytes=VMEM_BYTES),
        cost_estimate=pl.CostEstimate(
            flops=groups * rows * kv.shape[0] * rows * 8 * width,
            bytes_accessed=8 * 2**20,
            transcendentals=groups * rows * kv.shape[0] * rows,
        ),
    )(q, kv, qa, ka)


def with_rows(base, first, rows):
    index = lax.broadcasted_iota(jnp.int32, base.shape, 0)
    for n, row in enumerate(rows):
        base = jnp.where(index == first + n, row, base)
    return base


def backward_body(q_ref, kv_ref, qa_ref, ka_ref, do_ref, att_ref, lse_ref, dq_ref, dkv_ref, bias_ref, sum_ref):
    width, rows = q_ref.shape[1:]
    blocks = rows // QUERY_BLOCK
    parts = do_ref.shape[1]
    span = rows // parts
    sum_ref[...] = jnp.zeros_like(sum_ref)
    bias_ref[...] = jnp.zeros_like(bias_ref)

    def block(i, _):
        j = i // blocks
        first = (i % blocks) * QUERY_BLOCK
        cols = pl.ds(pl.multiple_of(first, QUERY_BLOCK), QUERY_BLOCK)
        q_t = q_ref[j, :, cols]
        marks = qa_ref[j, :, cols].astype(F32)
        extra = with_rows(marks, LSE_ROW, pieces(-lse_ref[j, :, cols])).astype(BF16)
        queries = join(q_t, extra).T
        grad_t = jnp.concatenate(
            [do_ref[j, first // span + n] for n in range(QUERY_BLOCK // span)], axis=1
        )
        delta = jnp.sum(grad_t.astype(F32) * att_ref[j, :, cols], axis=0, keepdims=True)
        extra = with_rows(jnp.zeros((width, QUERY_BLOCK), F32), 0, pieces(-delta)).astype(BF16)
        grads = join(grad_t, extra).T
        query_sum = jnp.zeros((QUERY_BLOCK, 2 * width), F32)
        for g in range(kv_ref.shape[0]):
            keys = join(kv_ref[g, :width, :], ka_ref[g])
            values = join(kv_ref[g, width:, :], jnp.ones((width, rows), BF16))
            probs = jnp.exp(nn(queries, keys))
            score_grad = (probs * nn(grads, values)).astype(BF16)
            sum_ref[g, width:, :] += nn(grad_t, probs.astype(BF16))
            sum_ref[g, :width, :] += nn(q_t, score_grad)
            query_sum += nt(score_grad, keys)
        query_sum = query_sum.T
        dq_ref[j, :, cols] = (query_sum[:width] * width**-0.5).astype(BF16)
        by_variate = query_sum[width : width + VARIATES]
        bias_ref[0] += by_variate * marks[VAR_ROW : VAR_ROW + VARIATES]
        bias_ref[1] += by_variate
        return 0

    lax.fori_loop(0, q_ref.shape[0] * blocks, block, 0)
    dkv_ref[...] = sum_ref[...].astype(BF16)


def rms_scale(vector, gain, axis=-1):
    return vector * lax.rsqrt(jnp.mean(vector * vector, axis=axis, keepdims=True) + EPSILON) * gain


def norm_back(grad, vector, gain):
    inverse = lax.rsqrt(jnp.mean(vector * vector, axis=-1, keepdims=True) + EPSILON)
    scaled = grad * gain
    mean = jnp.mean(scaled * vector, axis=-1, keepdims=True)
    return inverse * scaled - vector * (inverse**3 * mean), jnp.sum(grad * vector * inverse, axis=0)


def per_device(
    tokens,
    cotangent,
    doc_starts,
    variate_ids,
    time_ids,
    gain_attn,
    w_attn,
    gain_query,
    gain_key,
    variate_bias,
    w_output,
    gain_feed,
    w_gate,
    w_up,
    w_down,
):
    S, F = lax.axis_size("seq"), lax.axis_size("fsdp")
    s, f = lax.axis_index("seq"), lax.axis_index("fsdp")
    rows, width = tokens.shape
    heads = variate_bias.shape[0]
    dim = gain_query.shape[0]
    own_heads = heads // S
    splits = F // own_heads
    group = rows * S
    groups = F // splits
    hidden = w_down.shape[0] * F // S
    half = F // 2
    cut = width // (S * F)
    lanes = own_heads * dim

    def along_seq(s, f):
        return [(lax.rem(s + d, S), f) for d in range(1, S)]

    def along_fsdp(s, f):
        return [(s, lax.rem(f + d, F)) for d in range(1, F)]

    def along_both(s, f):
        return along_seq(s, f) + along_fsdp(s, f)

    def like_parts(s, f):
        return [
            (lax.rem(s + a, S), lax.rem(f + b * splits, F))
            for a in range(S)
            for b in range(groups)
            if a or b
        ]

    def everyone(s, f):
        return [(lax.rem(s + a, S), lax.rem(f + b, F)) for a in range(S) for b in range(F) if a or b]

    def seq_swap(s, f, src, dst):
        remote = [(src.at[t[0]], dst.at[s], t, None, None) for t in along_seq(s, f)]
        return remote, [(src.at[s], dst.at[s], None)]

    w_heads = lax.dynamic_slice_in_dim(
        w_attn.reshape(-1, 3, S, lanes), s, 1, 2
    ).reshape(-1, 3 * lanes)
    per_plane = F // S
    down_rows = w_down.shape[0] // S

    def plan_a(s, f, ins, outs):
        x, w, down = ins
        xs, ws, mine = outs
        remote = [(x, xs.at[s], t, None, None) for t in along_seq(s, f)]
        remote += [(w, ws.at[f], t, None, None) for t in along_fsdp(s, f)]
        local = [(x, xs.at[s], None), (w, ws.at[f], None)]
        holds = f // per_plane == s
        source = s * per_plane + f // S
        for i in range(S):
            to = lax.rem(f, per_plane) * S + i
            send = jnp.logical_and(holds, to != f)
            if i == 0:
                get = source != f
            else:
                get = False
            remote.append((down.at[i], mine, (s, to), send, get))
            local.append((down.at[i], mine, jnp.logical_and(holds, to == f)))
        return remote, local

    x_parts, w_parts, down_mine = exchange_a(
        [tokens, w_heads, w_down.reshape(S, down_rows, width)],
        [shape((S, rows, width)), shape((F,) + w_heads.shape), shape((down_rows, width))],
        plan_a,
        along_both,
        (S - 1) + (F - 1),
        S,
    )
    w_qkv = w_parts.reshape(width, 3 * lanes)
    inputs = x_parts.reshape(group, width).astype(F32)

    packed = jnp.concatenate(
        [
            lax.dynamic_slice_in_dim(w_gate, s * hidden, hidden, 1),
            lax.dynamic_slice_in_dim(w_up, s * hidden, hidden, 1),
            w_output,
            down_mine.reshape(w_gate.shape[0], hidden),
        ],
        axis=1,
    )
    gathered = lax.all_gather(packed, "fsdp", axis=0, tiled=True)
    later_cot, _ = lax.optimization_barrier((cotangent, x_parts))
    cot_group = lax.all_gather(later_cot, "seq", axis=0, tiled=True)

    normed = rms_scale(inputs, gain_attn).astype(BF16)
    projected = lax.dot_general(
        w_qkv, normed, (((0,), (1,)), ((), ())), preferred_element_type=F32
    ).reshape(3, own_heads, dim, group)
    times = lax.dynamic_slice_in_dim(time_ids, f * group, group).astype(F32)
    frequency = 10000.0 ** (-2.0 * jnp.arange(dim // 2, dtype=F32) / dim)
    angles = frequency[:, None] * times[None, :]
    cosine, sine = jnp.cos(angles), jnp.sin(angles)

    def prepare(raw, gain):
        front, back = jnp.split(rms_scale(raw, gain[:, None], axis=1), 2, axis=1)
        return jnp.concatenate([front * cosine - back * sine, front * sine + back * cosine], axis=1)

    queries, query_pull = jax.vjp(prepare, projected[0], gain_query)
    key_rows, key_pull = jax.vjp(prepare, projected[1], gain_key)
    queries = queries.astype(BF16) * dim**-0.5
    kv = jnp.concatenate([key_rows, projected[2]], axis=1).astype(BF16)

    def plan_b(s, f, ins, outs):
        q, kv = ins
        qs, kvs = outs
        remote, local = [], [(kv.at[f // splits], kvs.at[f], None), (q.at[f // splits], qs.at[f // splits], None)]
        for d in range(1, F):
            to = lax.rem(f + d, F)
            remote.append((kv.at[to // splits], kvs.at[f], (s, to), None, None))
            if d % splits == 0:
                remote.append((q.at[to // splits], qs.at[f // splits], (s, to), None, None))
        return remote, local

    q_all, kv_all = exchange(
        1,
        [queries, kv],
        [shape((groups, dim, group)), shape((F, 2 * dim, group))],
        plan_b,
        along_fsdp,
        (F - 1 + groups - 1, 2),
    )

    head = s * own_heads + f // splits
    part = lax.rem(f, splits)
    total = F * group
    positions = jnp.arange(total, dtype=jnp.int32)
    docs = jnp.sum((doc_starts[:, None] <= positions[None, :]).astype(jnp.int32), axis=0) - 1
    doc_marks = (docs[None, :] == jnp.arange(doc_starts.shape[0])[:, None]).astype(F32)
    var_marks = (variate_ids[None, :] == jnp.arange(VARIATES)[:, None]).astype(F32)
    nothing = jnp.zeros((dim - LSE_ROW - 3, total), F32)
    key_marks = jnp.concatenate(
        [var_marks, var_marks, var_marks, 1.0 - doc_marks, jnp.ones((3, total), F32), nothing]
    ).astype(BF16)
    key_marks = key_marks.reshape(dim, F, group).transpose(1, 0, 2)
    my_bias = lax.dynamic_slice_in_dim(variate_bias, head, 1, 0)[0]
    high, middle_, low = pieces(my_bias[0] - my_bias[1])

    def mine(marks):
        marks = marks.reshape(-1, groups, splits, group)
        return lax.dynamic_slice_in_dim(marks, part, 1, 2)[:, :, 0]

    var_mine, doc_mine = mine(var_marks), mine(doc_marks)
    query_marks = jnp.concatenate(
        [
            var_mine * high,
            var_mine * middle_,
            var_mine * low,
            doc_mine * -AWAY,
            jnp.zeros((VAR_ROW - LSE_ROW, groups, group), F32),
            var_mine,
            jnp.zeros((dim - VAR_ROW - VARIATES, groups, group), F32),
        ]
    ).astype(BF16)
    query_marks = query_marks.transpose(1, 0, 2)

    attended_low, attended, log_sum = attention_forward(q_all, kv_all, query_marks, key_marks)

    def plan_d(s, f, ins, outs):
        (o,), (all_heads,) = ins, outs
        own = s * own_heads + f // splits
        remote = [
            (o.at[t[1] // splits], all_heads.at[own], t, None, None) for t in like_parts(s, f)
        ]
        return remote, [(o.at[f // splits], all_heads.at[own], None)]

    heads_t = exchange(
        2,
        [attended_low],
        [shape((heads, dim, group))],
        plan_d,
        like_parts,
        (S * groups - 1, 1),
    )[0].reshape(heads * dim, group)

    gate_full, up_full, output_full, down_full = jnp.split(
        gathered, [hidden, 2 * hidden, 2 * hidden + width], axis=1
    )
    down_full = down_full.reshape(hidden, width)
    middle = inputs + tn(heads_t, output_full)
    normed_mid = rms_scale(middle, gain_feed).astype(BF16)
    gate_act, up_act = nn(normed_mid, gate_full), nn(normed_mid, up_full)
    hidden_grad = nt(cot_group, down_full)
    sigmoid = jax.nn.sigmoid(gate_act)
    silu = gate_act * sigmoid
    hidden_low = (silu * up_act).astype(BF16)
    gate_low = (hidden_grad * up_act * sigmoid * (1.0 + gate_act * (1.0 - sigmoid))).astype(BF16)
    up_low = (hidden_grad * silu).astype(BF16)
    mid_part = (nt(gate_low, gate_full) + nt(up_low, up_full)).astype(BF16)
    out_part = nn(hidden_low, down_full).astype(BF16)
    by_owner = (S, half, 2, cut)
    gate_part = tn(normed_mid, gate_low).astype(BF16).reshape(by_owner + (hidden,))
    up_part = tn(normed_mid, up_low).astype(BF16).reshape(by_owner + (hidden,))
    down_part = tn(hidden_low, cot_group).astype(BF16).reshape(half, 2, down_rows, width)

    def pair(s, f):
        return (s, f + 1 - 2 * lax.rem(f, 2))

    def plan_e(s, f, ins, outs):
        u, gate, up, down = ins
        us, gates, ups, downs = outs
        remote, local = seq_swap(s, f, u, us)
        other = 1 - lax.rem(f, 2)
        for src, dst in ((gate.at[:, :, other], gates), (up.at[:, :, other], ups), (down.at[:, other], downs)):
            remote.append((src, dst, pair(s, f), None, None))
        return remote, local

    mid_terms, gate_other, up_other, down_other = exchange(
        3,
        [mid_part.reshape(S, rows, width), gate_part, up_part, down_part],
        [
            shape((S, rows, width)),
            shape((S, half, cut, hidden)),
            shape((S, half, cut, hidden)),
            shape((half, down_rows, width)),
        ],
        plan_e,
        lambda s, f: along_seq(s, f) + [pair(s, f)],
        (S - 1 + 3, 1),
    )
    parity = lax.rem(f, 2)

    def halves(own, other, axis):
        own = lax.dynamic_index_in_dim(own, parity, axis, keepdims=False)
        return (own.astype(F32) + other.astype(F32)).astype(BF16)

    own_middle = lax.dynamic_slice_in_dim(middle, s * rows, rows, 0)
    mid_grad, feed_gain = norm_back(jnp.sum(mid_terms.astype(F32), axis=0), own_middle, gain_feed)
    middle_grad = cotangent.astype(F32) + mid_grad
    middle_low = middle_grad.astype(BF16)
    heads_grad = nt(output_full, middle_low).astype(BF16).reshape(heads, dim, rows)
    own_heads_t = lax.dynamic_slice_in_dim(heads_t, s * rows, rows, 1)
    output_part = nn(own_heads_t, middle_low).astype(BF16).reshape(by_owner + (width,))

    def plan_f(s, f, ins, outs):
        grad, out = ins
        grads, outs_ = outs
        place = grads.at[f // splits, s]
        remote = [
            (grad.at[t[0] * own_heads + t[1] // splits], place, t, None, None)
            for t in like_parts(s, f)
        ]
        remote.append((out.at[:, :, 1 - lax.rem(f, 2)], outs_, pair(s, f), None, None))
        return remote, [(grad.at[s * own_heads + f // splits], place, None)]

    grad_heads, output_other = exchange(
        4,
        [heads_grad, output_part],
        [shape((groups, S, dim, rows)), shape((S, half, cut, width))],
        plan_f,
        lambda s, f: like_parts(s, f) + [pair(s, f)],
        (S * groups - 1 + 1, 1),
    )
    gate_half = halves(gate_part, gate_other, 2)
    up_half = halves(up_part, up_other, 2)
    down_half = halves(down_part, down_other, 1)
    output_half = halves(output_part, output_other, 2)

    def same_parity(s, f):
        return [(s, lax.rem(f + 2 * d, F)) for d in range(1, half)]

    def kernel_g(*refs):
        ins, sends, outs, gots = refs[:7], refs[7:12], refs[12:15], refs[15:20]
        sum_ref, send_sems, recv_sems, local_sems = refs[20:]
        s, f = lax.axis_index("seq"), lax.axis_index("fsdp")
        greet(along_seq(s, f) + same_parity(s, f))
        remote, local = seq_swap(s, f, sends[4], gots[4])
        for src, dst in zip(sends[:3], gots[:3]):
            for t in same_parity(s, f):
                remote.append((src.at[:, t[1] // 2], dst.at[f // 2], t, None, None))
            local.append((src.at[:, f // 2], dst.at[f // 2], None))
        for t in same_parity(s, f):
            remote.append((sends[3].at[t[1] // 2], gots[3].at[f // 2], t, None, None))
        local.append((sends[3].at[f // 2], gots[3].at[f // 2], None))
        finish = send_all((remote, local), send_sems, recv_sems, local_sems)
        backward_body(*ins, *outs, sum_ref)
        finish()

    copies = S - 1 + 4 * (half - 1)
    owned = (half, S, cut)
    query_grad, kv_grad, bias_terms, gate_got, up_got, output_got, down_got, out_terms = pl.pallas_call(
        kernel_g,
        in_specs=[VMEM] * 7 + [ANY] * 5,
        out_specs=[VMEM] * 3 + [ANY] * 5,
        out_shape=[
            shape(q_all.shape),
            shape(kv_all.shape),
            shape((2, VARIATES, QUERY_BLOCK), F32),
            shape(owned + (hidden,)),
            shape(owned + (hidden,)),
            shape(owned + (width,)),
            shape((half, down_rows, width)),
            shape((S, rows, width)),
        ],
        scratch_shapes=[
            pltpu.VMEM(kv_all.shape, F32),
            pltpu.SemaphoreType.DMA((copies,)),
            pltpu.SemaphoreType.DMA((copies,)),
            pltpu.SemaphoreType.DMA((5,)),
        ],
        compiler_params=pltpu.CompilerParams(
            collective_id=5, has_side_effects=True, vmem_limit_bytes=VMEM_BYTES
        ),
    )(
        q_all,
        kv_all,
        query_marks,
        key_marks,
        grad_heads,
        attended,
        log_sum,
        gate_half,
        up_half,
        output_half,
        down_half,
        out_part.reshape(S, rows, width),
    )
    layer_out = (own_middle + jnp.sum(out_terms.astype(F32), axis=0)).astype(BF16)
    down_grad = jnp.sum(down_got.astype(F32), axis=0)

    def over_pairs(got):
        return jnp.sum(got.astype(F32), axis=0).astype(BF16)

    def plan_h(s, f, ins, outs):
        dq, dkv, *sums = ins
        dqs, dkvs, *gots = outs
        own = f // splits
        remote, local = [], [(dkv.at[f], dkvs.at[f], None), (dq.at[own], dqs.at[own], None)]
        for d in range(1, F):
            to = lax.rem(f + d, F)
            remote.append((dkv.at[to], dkvs.at[f], (s, to), None, None))
            if d % splits == 0:
                remote.append((dq.at[to // splits], dqs.at[own], (s, to), None, None))
        for src, dst in zip(sums, gots):
            more, also = seq_swap(s, f, src, dst)
            remote += more
            local += also
        return remote, local

    wide = shape((S, cut, hidden))
    query_got, kv_got, gate_rows, up_rows, output_rows = exchange(
        6,
        [query_grad, kv_grad, over_pairs(gate_got), over_pairs(up_got), over_pairs(output_got)],
        [shape((own_heads, dim, group)), shape((F, 2 * dim, group)), wide, wide, shape((S, cut, width))],
        plan_h,
        along_both,
        (F - 1 + groups - 1 + 3 * (S - 1), 5),
    )
    gate_grad = gate_rows.astype(F32).transpose(1, 0, 2).reshape(cut, S * hidden)
    up_grad = up_rows.astype(F32).transpose(1, 0, 2).reshape(cut, S * hidden)
    output_grad = jnp.sum(output_rows.astype(F32), axis=0)

    kv_sum = jnp.sum(kv_got.astype(F32).reshape(own_heads, splits, 2 * dim, group), axis=1)
    kv_low = kv_sum.astype(BF16).astype(F32)
    query_raw, query_gain = query_pull(query_got.astype(F32))
    key_raw, key_gain = key_pull(kv_low[:, :dim])
    projected_grad = (
        jnp.stack([query_raw, key_raw, kv_low[:, dim:]]).astype(BF16).reshape(3 * lanes, group)
    )
    normed_part = lax.dot_general(
        projected_grad, w_qkv, (((0,), (1,)), ((), ())), preferred_element_type=F32
    ).astype(BF16)
    attn_part = lax.dot_general(
        normed, projected_grad, (((0,), (1,)), ((), ())), preferred_element_type=F32
    ).astype(BF16)

    def plan_i(s, f, ins, outs):
        u, w = ins
        us, ws = outs
        remote, local = seq_swap(s, f, u, us)
        for t in along_fsdp(s, f):
            remote.append((w.at[:, t[1]], ws.at[f], t, None, None))
        local.append((w.at[:, f], ws.at[f], None))
        return remote, local

    normed_terms, attn_got = exchange(
        7,
        [normed_part.reshape(S, rows, width), attn_part.reshape(S, F, cut, 3 * lanes)],
        [shape((S, rows, width)), shape((F, S, cut, 3 * lanes))],
        plan_i,
        along_both,
        (S - 1 + F - 1, 2),
    )
    input_grad, attn_gain = norm_back(
        jnp.sum(normed_terms.astype(F32), axis=0), tokens.astype(F32), gain_attn
    )
    tokens_grad = middle_grad + input_grad

    bias_sums = jnp.sum(bias_terms, axis=(1, 2))
    bias_pair = jnp.stack([bias_sums[0], bias_sums[1] - bias_sums[0]])
    bias_full = lax.dynamic_update_slice_in_dim(
        jnp.zeros((heads, 2), F32), bias_pair[None], head, 0
    )
    count = S * F
    small = jnp.zeros((count, 8, 128), F32)
    small = small.at[:, 0, :cut].set(attn_gain.reshape(count, cut))
    small = small.at[:, 1, :cut].set(feed_gain.reshape(count, cut))
    small = small.at[:, 2, :dim].set(query_gain)
    small = small.at[:, 3, :dim].set(key_gain)
    small = small.at[:, 4, : 2 * heads].set(bias_full.reshape(-1))

    def plan_j(s, f, ins, outs):
        w, vectors = ins
        ws, got = outs
        remote, local = seq_swap(s, f, w, ws)
        own = s * F + f
        remote += [(vectors.at[t[0] * F + t[1]], got.at[own], t, None, None) for t in everyone(s, f)]
        local.append((vectors.at[own], got.at[own], None))
        return remote, local

    attn_rows, small_got = exchange(
        8,
        [over_pairs(attn_got), small],
        [shape((S, cut, 3 * lanes)), shape((count, 8, 128), F32)],
        plan_j,
        everyone,
        (S - 1 + count - 1, 2),
    )
    attn_grad = (
        attn_rows.astype(F32).reshape(S, cut, 3, lanes).transpose(1, 2, 0, 3).reshape(cut, 3 * heads * dim)
    )
    sums = jnp.sum(small_got, axis=0)
    return (
        layer_out,
        tokens_grad,
        attn_grad,
        output_grad,
        gate_grad,
        up_grad,
        down_grad,
        sums[0, :cut],
        sums[1, :cut],
        sums[2, :dim],
        sums[3, :dim],
        sums[4, : 2 * heads].reshape(heads, 2),
    )


def exchange_a(inputs, out_shapes, make_plan, peers, plain, conditional):
    def kernel(*refs):
        ins, outs = refs[: len(inputs)], refs[len(inputs) : len(inputs) + len(out_shapes)]
        send_sems, recv_sems, local_sems = refs[-3:]
        s, f = lax.axis_index("seq"), lax.axis_index("fsdp")
        greet(peers(s, f))
        remote, local = make_plan(s, f, ins, outs)
        finish = send_all((remote[:plain], local), send_sems, recv_sems, local_sems)
        copies = []
        for n, (src, dst, device, may_send, may_receive) in enumerate(remote[plain:]):
            copy = pltpu.make_async_remote_copy(
                src_ref=src,
                dst_ref=dst,
                send_sem=send_sems.at[plain + n],
                recv_sem=recv_sems.at[plain],
                device_id=device,
                device_id_type=MESH,
            )
            when(may_send, copy.start)
            copies.append((copy, may_send))
        finish()
        for copy, may_send in copies:
            when(may_send, copy.wait_send)
        when(remote[plain][4], copies[0][0].wait_recv)

    return pl.pallas_call(
        kernel,
        in_specs=[ANY] * len(inputs),
        out_specs=[ANY] * len(out_shapes),
        out_shape=out_shapes,
        scratch_shapes=[
            pltpu.SemaphoreType.DMA((plain + conditional,)),
            pltpu.SemaphoreType.DMA((plain + 1,)),
            pltpu.SemaphoreType.DMA((2 + conditional,)),
        ],
        compiler_params=pltpu.CompilerParams(collective_id=0, has_side_effects=True),
    )(*inputs)


def solution(mesh):
    by_token, by_fsdp, by_owner = P(("fsdp", "seq"), None), P("fsdp", None), P(("seq", "fsdp"), None)
    in_specs = (
        by_token,
        by_token,
        P(),
        P(),
        P(),
        P(),
        by_fsdp,
        P(),
        P(),
        P(),
        by_fsdp,
        P(),
        by_fsdp,
        by_fsdp,
        by_fsdp,
    )
    out_specs = (
        (by_token, by_token) + (by_owner,) * 5 + (P(("seq", "fsdp")),) * 2 + (P(),) * 3
    )
    return jax.shard_map(
        per_device, mesh=mesh, in_specs=in_specs, out_specs=out_specs, check_vma=False
    )
```

```python
import functools

import jax
import jax.numpy as jnp
from jax import lax
from jax.experimental import pallas as pl
from jax.experimental.pallas import tpu as pltpu
from jax.sharding import PartitionSpec as P

EPSILON = 1e-06
F32, BF16 = jnp.float32, jnp.bfloat16
VARIATES = 8
AWAY = 1024.0
QUERY_BLOCK = 256
LSE_ROW, VAR_ROW = 32, 40
MESH = pl.DeviceIdType.MESH
ANY = pl.BlockSpec(memory_space=pl.ANY)
VMEM = pl.BlockSpec(memory_space=pltpu.VMEM)
VMEM_BYTES = 48 * 2**20


def nn(a, b):
    return jnp.dot(a, b, preferred_element_type=F32)


def nt(a, b):
    return lax.dot_general(a, b, (((1,), (1,)), ((), ())), preferred_element_type=F32)


def tn(a, b):
    return lax.dot_general(a, b, (((0,), (0,)), ((), ())), preferred_element_type=F32)


def pieces(values):
    high = values.astype(BF16).astype(F32)
    middle = (values - high).astype(BF16).astype(F32)
    return high, middle, (values - high - middle).astype(BF16).astype(F32)


def send_all(plan, send_sems, recv_sems, local_sems):
    remote, local = plan
    copies = []
    for n, (src, dst, device, may_send, may_receive) in enumerate(remote):
        copy = pltpu.make_async_remote_copy(
            src_ref=src,
            dst_ref=dst,
            send_sem=send_sems.at[n],
            recv_sem=recv_sems.at[n],
            device_id=device,
            device_id_type=MESH,
        )
        when(may_send, copy.start)
        copies.append((copy, may_send, may_receive))
    locals_ = []
    for n, (src, dst, may) in enumerate(local):
        copy = pltpu.make_async_copy(src, dst, local_sems.at[n])
        when(may, copy.start)
        locals_.append((copy, may))

    def finish():
        for copy, may in locals_:
            when(may, copy.wait)
        for copy, may_send, may_receive in copies:
            when(may_send, copy.wait_send)
            when(may_receive, copy.wait_recv)

    return finish


def when(condition, action):
    if condition is None:
        action()
    else:
        pl.when(condition)(action)


def greet(devices):
    barrier = pltpu.get_barrier_semaphore()
    for device in devices:
        pl.semaphore_signal(barrier, inc=1, device_id=device, device_id_type=MESH)
    pl.semaphore_wait(barrier, len(devices))


def exchange(number, inputs, out_shapes, make_plan, peers, counts):
    def kernel(*refs):
        ins = refs[: len(inputs)]
        outs = refs[len(inputs) : len(inputs) + len(out_shapes)]
        send_sems, recv_sems, local_sems = refs[-3:]
        s, f = lax.axis_index("seq"), lax.axis_index("fsdp")
        greet(peers(s, f))
        send_all(make_plan(s, f, ins, outs), send_sems, recv_sems, local_sems)()

    return pl.pallas_call(
        kernel,
        in_specs=[ANY] * len(inputs),
        out_specs=[ANY] * len(out_shapes),
        out_shape=out_shapes,
        scratch_shapes=[
            pltpu.SemaphoreType.DMA((counts[0],)),
            pltpu.SemaphoreType.DMA((counts[0],)),
            pltpu.SemaphoreType.DMA((max(counts[1], 1),)),
        ],
        compiler_params=pltpu.CompilerParams(collective_id=number, has_side_effects=True),
    )(*inputs)


class Line:
    def __init__(self, block, sems, s, f, S):
        self.block, (self.sent, self.got) = block, sems
        self.s, self.f, self.S = s, f, S

    def hop(self, plane, slot, step):
        ref = self.block(plane, slot)
        return pltpu.make_async_remote_copy(
            src_ref=ref,
            dst_ref=ref,
            send_sem=self.sent.at[plane, slot, int(step > 0)],
            recv_sem=self.got.at[plane, slot],
            device_id=(self.s + step, self.f),
            device_id_type=MESH,
        )

    def each_hop(self, slot, distance, action):
        s, S = self.s, self.S
        pl.when((s - distance + 1) * (S - 1 - s) > 0)(
            lambda: action(self.hop(s - distance, slot, 1))
        )
        pl.when((S - s - distance) * s > 0)(lambda: action(self.hop(s + distance, slot, -1)))

    def send(self, slot):
        self.each_hop(slot, 0, lambda hop: hop.start())

    def arrive(self, slot, distance):
        s, S = self.s, self.S
        pl.when(s - distance >= 0)(lambda: self.hop(s - distance, slot, 1).wait_recv())
        pl.when(s + distance < S)(lambda: self.hop(s + distance, slot, -1).wait_recv())
        self.each_hop(slot, distance, lambda hop: hop.start())

    def drain(self, slot):
        for distance in range(self.S):
            self.each_hop(slot, distance, lambda hop: hop.wait_send())


def line_sems(S, slots):
    return [pltpu.SemaphoreType.DMA((S, slots, 2)), pltpu.SemaphoreType.DMA((S, slots))]


def flipped(f, bit):
    step = 2**bit
    return f + step - 2 * step * lax.rem(f // step, 2)


class CubeGather:
    def __init__(self, block, own, sems, s, f, F):
        self.block, self.own, (self.sent, self.shared, self.got) = block, own, sems
        self.s, self.f, self.F = s, f, F
        bits = list(range(1, F.bit_length() - 1))
        self.orders = (bits, bits[::-1])

    def copy(self, g, half, sem, to, own=False):
        ref = self.block(g, half)
        return pltpu.make_async_remote_copy(
            src_ref=self.own(half) if own else ref,
            dst_ref=ref,
            send_sem=sem,
            recv_sem=self.got.at[g, half],
            device_id=(self.s, to),
            device_id_type=MESH,
        )

    def held(self, half, rounds):
        masks = [((), 0)]
        for n, bit in enumerate(self.orders[half][:rounds]):
            masks += [(mask + (bit,), n + 1) for mask, _ in list(masks)]
        return masks

    def device(self, mask):
        g = self.f
        for bit in mask:
            g = flipped(g, bit)
        return g

    def sends(self, half, since):
        rounds = len(self.orders[half])
        out = []
        for place, (mask, came) in enumerate(self.held(half, rounds)):
            for n in range(came, rounds):
                if came == since:
                    out.append((n, place, mask))
        return out

    def send(self, half, n, place, mask):
        bit = self.orders[half][n]
        sem = self.sent.at[half, n, place]
        return self.copy(self.device(mask), half, sem, flipped(self.f, bit), not mask)

    def shares(self, half, since):
        return [
            self.copy(
                self.device(mask), half, self.shared.at[half, place], flipped(self.f, 0), not mask
            )
            for place, (mask, came) in enumerate(self.held(half, len(self.orders[half])))
            if came == since
        ]

    @property
    def rounds(self):
        return len(self.orders[0])

    def start(self):
        for half in range(2):
            self.send(half, 0, 0, ()).start()
        for half in range(2):
            self.shares(half, 0)[0].start()

    def step(self, number):
        for half in range(2):
            shares = self.shares(half, number)
            for share in shares:
                share.wait_recv()
            if number < self.rounds:
                for which in self.sends(half, number) + self.sends(half, 0)[number : number + 1]:
                    if which[0] == number or which[1]:
                        self.send(half, *which).start()
            for share in shares:
                share.start()

    def finish(self):
        for half in range(2):
            for place, (mask, _) in enumerate(self.held(half, self.rounds)):
                g = flipped(self.device(mask), 0)
                self.copy(g, half, self.shared.at[half, place], self.f).wait_recv()

    def drain(self):
        for half in range(2):
            for number in range(self.rounds + 1):
                for which in self.sends(half, number):
                    self.send(half, *which).wait_send()
                for share in self.shares(half, number):
                    share.wait_send()


def cube_sems(F):
    rounds = F.bit_length() - 2
    return [
        pltpu.SemaphoreType.DMA((2, rounds, F // 4)),
        pltpu.SemaphoreType.DMA((2, F // 2)),
        pltpu.SemaphoreType.DMA((F, 2)),
    ]


def shape(dims, dtype=BF16):
    return jax.ShapeDtypeStruct(tuple(dims), dtype)


def join(a, b):
    return jnp.concatenate([a, b], axis=0)


def side_by_side(ref, *index):
    return jnp.concatenate([ref[(*index, n)] for n in range(ref.shape[len(index)])], axis=1)


def forward_group(j, q_ref, kv_ref, qa_ref, ka_ref, att_ref, lse_ref, o_ref):
    width, rows = att_ref.shape[1:]
    span = q_ref.shape[-1]
    sub = QUERY_BLOCK // span

    def block(i, _):
        cols = pl.ds(pl.multiple_of(i * QUERY_BLOCK, QUERY_BLOCK), QUERY_BLOCK)
        q_t = jnp.concatenate([q_ref[j, i * sub + n] for n in range(sub)], axis=1)
        queries = join(q_t, qa_ref[j, :, cols]).T
        total = jnp.zeros((QUERY_BLOCK, 2 * width), F32)
        for g in range(kv_ref.shape[0]):
            kv = side_by_side(kv_ref, g)
            keys = join(kv[:width], ka_ref[g])
            values = join(kv[width:], jnp.ones((width, rows), BF16))
            weights = jnp.exp(nn(queries, keys)).astype(BF16)
            total += nt(weights, values)
        total = total.T
        weight_sum = total[width : width + 1]
        attended = total[:width] / weight_sum
        att_ref[j, :, cols] = attended
        o_ref[j, :, cols] = attended.astype(BF16)
        lse_ref[j, :, cols] = jnp.log(weight_sum)
        return 0

    lax.fori_loop(0, rows // QUERY_BLOCK, block, 0)


def with_rows(base, first, rows):
    index = lax.broadcasted_iota(jnp.int32, base.shape, 0)
    for n, row in enumerate(rows):
        base = jnp.where(index == first + n, row, base)
    return base


def backward_body(q_ref, kv_ref, qa_ref, ka_ref, do_ref, att_ref, lse_ref, dq_ref, dkv_ref, bias_ref, sum_ref):
    width, rows = att_ref.shape[1:]
    blocks = rows // QUERY_BLOCK
    span = q_ref.shape[-1]
    sub = QUERY_BLOCK // span
    sum_ref[...] = jnp.zeros_like(sum_ref)
    bias_ref[...] = jnp.zeros_like(bias_ref)

    def block(i, _):
        j = i // blocks
        first = (i % blocks) * sub
        cols = pl.ds(pl.multiple_of((i % blocks) * QUERY_BLOCK, QUERY_BLOCK), QUERY_BLOCK)
        q_t = jnp.concatenate([q_ref[j, first + n] for n in range(sub)], axis=1)
        marks = qa_ref[j, :, cols].astype(F32)
        extra = with_rows(marks, LSE_ROW, pieces(-lse_ref[j, :, cols])).astype(BF16)
        queries = join(q_t, extra).T
        grad_t = jnp.concatenate([do_ref[j, first + n] for n in range(sub)], axis=1)
        delta = jnp.sum(grad_t.astype(F32) * att_ref[j, :, cols], axis=0, keepdims=True)
        extra = with_rows(jnp.zeros((width, QUERY_BLOCK), F32), 0, pieces(-delta)).astype(BF16)
        grads = join(grad_t, extra).T
        query_sum = jnp.zeros((QUERY_BLOCK, 2 * width), F32)
        for g in range(kv_ref.shape[0]):
            kv = side_by_side(kv_ref, g)
            keys = join(kv[:width], ka_ref[g])
            values = join(kv[width:], jnp.ones((width, rows), BF16))
            probs = jnp.exp(nn(queries, keys))
            score_grad = (probs * nn(grads, values)).astype(BF16)
            sum_ref[g, width:, :] += nn(grad_t, probs.astype(BF16))
            sum_ref[g, :width, :] += nn(q_t, score_grad)
            query_sum += nt(score_grad, keys)
        query_sum = query_sum.T
        dq_ref[j, :, cols] = (query_sum[:width] * width**-0.5).astype(BF16)
        by_variate = query_sum[width : width + VARIATES]
        bias_ref[0] += by_variate * marks[VAR_ROW : VAR_ROW + VARIATES]
        bias_ref[1] += by_variate
        return 0

    lax.fori_loop(0, q_ref.shape[0] * blocks, block, 0)
    dkv_ref[...] = sum_ref[...].astype(BF16)


def rms_scale(vector, gain, axis=-1):
    return vector * lax.rsqrt(jnp.mean(vector * vector, axis=axis, keepdims=True) + EPSILON) * gain


def norm_back(grad, vector, gain):
    inverse = lax.rsqrt(jnp.mean(vector * vector, axis=-1, keepdims=True) + EPSILON)
    scaled = grad * gain
    mean = jnp.mean(scaled * vector, axis=-1, keepdims=True)
    return inverse * scaled - vector * (inverse**3 * mean), jnp.sum(grad * vector * inverse, axis=0)


def per_device(
    tokens,
    cotangent,
    doc_starts,
    variate_ids,
    time_ids,
    gain_attn,
    w_attn,
    gain_query,
    gain_key,
    variate_bias,
    w_output,
    gain_feed,
    w_gate,
    w_up,
    w_down,
):
    S, F = lax.axis_size("seq"), lax.axis_size("fsdp")
    s, f = lax.axis_index("seq"), lax.axis_index("fsdp")
    rows, width = tokens.shape
    heads = variate_bias.shape[0]
    dim = gain_query.shape[0]
    own_heads = heads // S
    splits = F // own_heads
    group = rows * S
    groups = F // splits
    hidden = w_down.shape[0] * F // S
    half = F // 2
    cut = width // (S * F)
    lanes = own_heads * dim

    def along_seq(s, f):
        return [(lax.rem(s + d, S), f) for d in range(1, S)]

    def along_fsdp(s, f):
        return [(s, lax.rem(f + d, F)) for d in range(1, F)]

    def along_both(s, f):
        return along_seq(s, f) + along_fsdp(s, f)

    def like_parts(s, f):
        return [
            (lax.rem(s + a, S), lax.rem(f + b * splits, F))
            for a in range(S)
            for b in range(groups)
            if a or b
        ]

    def everyone(s, f):
        return [(lax.rem(s + a, S), lax.rem(f + b, F)) for a in range(S) for b in range(F) if a or b]

    def seq_swap(s, f, src, dst):
        remote = [(src.at[t[0]], dst.at[s], t, None, None) for t in along_seq(s, f)]
        return remote, [(src.at[s], dst.at[s], None)]

    frequency = (10000.0 ** (-2.0 * jnp.arange(dim // 2, dtype=F32) / dim))[:, None]
    per_plane = F // S
    down_rows = w_down.shape[0] // S
    local_rows = w_attn.shape[0]
    total = F * group

    def peers_a(s, f):
        return [(lax.rem(s + 1, S), f), (lax.rem(s + S - 1, S), f)] + along_fsdp(s, f)

    def kernel_a(
        x_ref, w_ref, wo_ref, cot_ref, times_ref, freq_ref, gain_ref, gain_q_ref, gain_k_ref, ids_ref, ids_mine_ref,
        starts_ref, bias_ref,
        xs_ref, ws_ref, raw_ref, cots_ref, cos_ref, sin_ref, ka_ref, qa_ref, q_ref, kv_ref, wos_ref,
        q_out, kv_out, w_sem, x_sent, x_got, c_sent, c_got, pair_sent, pair_shared, pair_got,
        wo_sent, wo_shared, wo_got, kv_sent, kv_shared, kv_got, q_sent, q_got, own_sem,
    ):
        s, f = lax.axis_index("seq"), lax.axis_index("fsdp")
        loads = []
        for n in range(3):
            src = w_ref.at[:, pl.ds(pl.multiple_of(n * S * lanes + s * lanes, 128), lanes)]
            dst = ws_ref.at[pl.ds(f * local_rows, local_rows), pl.ds(n * lanes, lanes)]
            loads.append(pltpu.make_async_copy(src, dst, w_sem.at[n]))
        for load in loads:
            load.start()
        wo_here = pltpu.make_async_copy(wo_ref, wos_ref.at[pl.ds(f * local_rows, local_rows)], w_sem.at[3])
        wo_here.start()
        xs_ref[s] = x_ref[...]
        cots_ref[s] = cot_ref[...]
        greet(peers_a(s, f))
        xs = Line(lambda plane, slot: xs_ref.at[plane], (x_sent, x_got), s, f, S)
        xs.send(0)
        for load in loads:
            load.wait()

        def rows_of(ref):
            size = local_rows // 2
            return lambda g, half: ref.at[pl.ds(g * local_rows + half * size, size)]

        def half_of(ref):
            size = local_rows // 2
            return lambda half: ref.at[pl.ds(half * size, size)]

        ws = CubeGather(
            rows_of(ws_ref), lambda half: rows_of(ws_ref)(f, half), (pair_sent, pair_shared, pair_got), s, f, F
        )
        wos = CubeGather(rows_of(wos_ref), half_of(wo_ref), (wo_sent, wo_shared, wo_got), s, f, F)
        ws.start()

        angles = freq_ref[...] * times_ref[...].astype(F32)
        cos_ref[...] = jnp.cos(angles)
        sin_ref[...] = jnp.sin(angles)
        pair = [bias_ref[s * own_heads + f // splits, n] for n in range(2)]
        difference = pieces(jnp.full((VARIATES, group), pair[0] - pair[1], F32))
        index = lax.broadcasted_iota(jnp.int32, (VARIATES, group), 0)

        def marks(g, ids):
            positions = g * group + lax.broadcasted_iota(jnp.int32, (VARIATES, group), 1)
            docs = jnp.zeros((VARIATES, group), jnp.int32) - 1
            for n in range(doc_starts.shape[0]):
                docs = docs + (starts_ref[n] <= positions).astype(jnp.int32)
            return (docs == index).astype(F32), (ids == index).astype(F32)

        for g in range(F):
            doc, var = marks(g, ids_ref[g])
            tail = (index < 3).astype(F32)
            none = jnp.zeros((dim - LSE_ROW - VARIATES, group), F32)
            ka_ref[g] = jnp.concatenate([var, var, var, 1.0 - doc, tail, none]).astype(BF16)
        for j in range(groups):
            doc, var = marks(j * splits + lax.rem(f, splits), ids_mine_ref[j])
            none = jnp.zeros((VARIATES, group), F32)
            rest = jnp.zeros((dim - VAR_ROW - VARIATES, group), F32)
            scaled = [var * part for part in difference]
            qa_ref[j] = jnp.concatenate([*scaled, doc * -AWAY, none, var, rest]).astype(BF16)

        def kv_copy(g, b, src, sem, to):
            return pltpu.make_async_remote_copy(
                src_ref=src, dst_ref=kv_ref.at[g, b], send_sem=sem, recv_sem=kv_got.at[g, b],
                device_id=(s, to), device_id_type=MESH,
            )

        def to_heads(b, d):
            to = lax.rem(f + 2 * d, F)
            return kv_copy(f, b, kv_out.at[b, to // splits], kv_sent.at[b, d], to)

        def to_neighbour(b, d):
            g = lax.rem(f + 2 * d, F)
            src = kv_ref.at[g, b] if d else kv_out.at[b, f // splits]
            return kv_copy(g, b, src, kv_shared.at[b, d], flipped(f, 0))

        def queries_to_heads(b, d):
            to = lax.rem(f + d * splits, F)
            return pltpu.make_async_remote_copy(
                src_ref=q_out.at[b, to // splits], dst_ref=q_ref.at[f // splits, b], send_sem=q_sent.at[b, d],
                recv_sem=q_got.at[f // splits, b], device_id=(s, to), device_id_type=MESH,
            )

        def own_copies(b):
            return (
                pltpu.make_async_copy(kv_out.at[b, f // splits], kv_ref.at[f, b], own_sem.at[b, 0]),
                pltpu.make_async_copy(q_out.at[b, f // splits], q_ref.at[f // splits, b], own_sem.at[b, 1]),
            )

        def project(b):
            normed = rms_scale(xs_ref[b].astype(F32), gain_ref[...]).astype(BF16)
            projected = nn(normed, ws_ref[...]).T.reshape(3, own_heads, dim, rows)
            cols = pl.ds(pl.multiple_of(b * rows, rows), rows)
            cosine, sine = cos_ref[:, cols], sin_ref[:, cols]

            def turned(raw, gain):
                raw = rms_scale(raw, gain, axis=1)
                front, back = raw[:, : dim // 2], raw[:, dim // 2 :]
                return jnp.concatenate(
                    [front * cosine - back * sine, front * sine + back * cosine], axis=1
                )

            raw_ref[0, :, :, cols] = projected[0]
            raw_ref[1, :, :, cols] = projected[1]
            q_out[b] = (turned(projected[0], gain_q_ref[...]).astype(BF16).astype(F32) * dim**-0.5).astype(BF16)
            kv_out[b, :, :dim] = turned(projected[1], gain_k_ref[...]).astype(BF16)
            kv_out[b, :, dim:] = projected[2].astype(BF16)
            for d in range(1, half):
                to_heads(b, d).start()
            for d in range(1, groups):
                queries_to_heads(b, d).start()
            to_neighbour(b, 0).start()
            for copy in own_copies(b):
                copy.start()

        def share(b):
            for d in range(1, half):
                to_neighbour(b, d).wait_recv()
                to_neighbour(b, d).start()

        for number in range(1, ws.rounds + 1):
            ws.step(number)
        wos.start()
        ws.finish()
        project(s)
        cots = Line(lambda plane, slot: cots_ref.at[plane], (c_sent, c_got), s, f, S)
        for distance in range(1, S):
            xs.arrive(0, distance)
            if distance == min(2, S - 1):
                cots.send(0)
            pl.when(s - distance >= 0)(lambda distance=distance: project(s - distance))
            pl.when(s + distance < S)(lambda distance=distance: project(s + distance))
            if distance < S - 1 and distance < wos.rounds:
                wos.step(distance)

        def share_all(b, _):
            share(b)
            return 0

        lax.fori_loop(0, S, share_all, 0)
        for number in range(min(S - 1, wos.rounds), wos.rounds + 1):
            wos.step(number)
        for distance in range(1, S):
            cots.arrive(0, distance)

        def last(b, _):
            for copy in own_copies(b):
                copy.wait()
            for d in range(half):
                if d:
                    to_heads(b, d).wait_send()
                to_neighbour(b, d).wait_send()
                g = lax.rem(flipped(f, 0) + 2 * d, F)
                kv_copy(g, b, kv_ref.at[g, b], kv_shared.at[b, d], f).wait_recv()
            for d in range(1, groups):
                queries_to_heads(b, d).wait_send()
                g = lax.rem(f + d * splits, F)
                pltpu.make_async_remote_copy(
                    src_ref=q_out.at[b, 0], dst_ref=q_ref.at[g // splits, b], send_sem=q_sent.at[b, d],
                    recv_sem=q_got.at[g // splits, b], device_id=(s, g), device_id_type=MESH,
                ).wait_recv()
            return 0

        lax.fori_loop(0, S, last, 0)
        for line in (xs, cots):
            line.drain(0)
        wos.finish()
        wo_here.wait()
        ws.drain()
        wos.drain()

    smem = pl.BlockSpec(memory_space=pltpu.SMEM)
    ids = variate_ids.reshape(F, 1, group)
    ids_mine = lax.dynamic_index_in_dim(
        ids.reshape(groups, splits, 1, group), lax.rem(f, splits), 1, keepdims=False
    )
    x_parts, w_qkv, raw, cot_parts, cosine, sine, key_marks, query_marks, q_all, kv_all, output_full = pl.pallas_call(
        kernel_a,
        in_specs=[VMEM, ANY, ANY] + [VMEM] * 8 + [smem] * 2,
        out_specs=[VMEM] * 8 + [ANY] * 3,
        out_shape=[
            shape((S, rows, width)),
            shape((width, 3 * lanes)),
            shape((2, own_heads, dim, group), F32),
            shape((S, rows, width)),
            shape((dim // 2, group), F32),
            shape((dim // 2, group), F32),
            shape((F, dim, group)),
            shape((groups, dim, group)),
            shape((groups, S, dim, rows)),
            shape((F, S, 2 * dim, rows)),
            shape((heads * dim, width)),
        ],
        scratch_shapes=[
            pltpu.VMEM((S, own_heads, dim, rows), BF16),
            pltpu.VMEM((S, own_heads, 2 * dim, rows), BF16),
            pltpu.SemaphoreType.DMA((4,)),
            *line_sems(S, 1),
            *line_sems(S, 1),
            *cube_sems(F),
            *cube_sems(F),
            pltpu.SemaphoreType.DMA((S, half)),
            pltpu.SemaphoreType.DMA((S, half)),
            pltpu.SemaphoreType.DMA((F, S)),
            pltpu.SemaphoreType.DMA((S, groups)),
            pltpu.SemaphoreType.DMA((groups, S)),
            pltpu.SemaphoreType.DMA((S, 2)),
        ],
        compiler_params=pltpu.CompilerParams(
            collective_id=0, has_side_effects=True, vmem_limit_bytes=VMEM_BYTES
        ),
        cost_estimate=pl.CostEstimate(flops=10**9, bytes_accessed=10**8, transcendentals=0),
    )(
        tokens,
        w_attn,
        w_output,
        cotangent,
        lax.dynamic_slice_in_dim(time_ids, f * group, group)[None, :],
        frequency,
        gain_attn[None, :],
        gain_query[:, None],
        gain_key[:, None],
        ids,
        ids_mine,
        doc_starts,
        variate_bias,
    )
    inputs = x_parts.reshape(group, width).astype(F32)
    head = s * own_heads + f // splits

    def unit_place(s, f):
        return lax.rem(f, per_plane) * S + lax.rem(f // per_plane + s, S)

    def unit_block(s, g):
        holder = lax.rem(lax.rem(g, S) - s + S, S) * per_plane + g // S
        return holder * S + lax.rem(g, S)

    def units(w):
        if down_rows % 128 == 0:
            return w
        blocks = w.reshape(w.shape[0], S * F, down_rows)
        return jnp.concatenate(
            [lax.dynamic_index_in_dim(blocks, unit_block(s, g), 1, False) for g in range(F)], axis=1
        )

    def kernel_b(
        q_ref, kv_ref, qa_ref, ka_ref, wd_ref, wg_ref, wu_ref,
        att_ref, lse_ref, heads_ref, downs_ref, gates_ref, ups_ref,
        o_ref, gate_own, up_own, o_sent, h_sent, h_got, w_sem, here_sem, *cube_refs,
    ):
        s, f = lax.axis_index("seq"), lax.axis_index("fsdp")
        column, part = f // splits, lax.rem(f, splits)
        down_own = wd_ref.at[lax.rem(f // per_plane + s, S)]
        loads = []
        for n, (src, dst) in enumerate(((wg_ref, gate_own), (wu_ref, up_own))):
            if down_rows % 128:
                loads.append(pltpu.make_async_copy(src, dst, w_sem.at[n, 0]))
                continue
            for g in range(F):
                cols = pl.ds(pl.multiple_of(unit_block(s, g) * down_rows, 128), down_rows)
                place = pl.ds(g * down_rows, down_rows)
                loads.append(pltpu.make_async_copy(src.at[:, cols], dst.at[:, place], w_sem.at[n, g]))
        for load in loads:
            load.start()
        greet(along_both(s, f))
        for load in loads:
            load.wait()
        mine = pl.ds(f * local_rows, local_rows)
        here = [
            pltpu.make_async_copy(gate_own, gates_ref.at[mine], here_sem.at[0]),
            pltpu.make_async_copy(up_own, ups_ref.at[mine], here_sem.at[1]),
            pltpu.make_async_copy(
                down_own, downs_ref.at[pl.ds(unit_place(s, f) * down_rows, down_rows)], here_sem.at[2]
            ),
        ]
        for copy in here:
            copy.start()

        def rows_of(ref, size, place=lambda g: g):
            return lambda g, half: ref.at[pl.ds(place(g) * size + half * (size // 2), size // 2)]

        def half_of(ref, size):
            return lambda half: ref.at[pl.ds(half * (size // 2), size // 2)]

        blocks = (
            (rows_of(gates_ref, local_rows), half_of(gate_own, local_rows)),
            (rows_of(ups_ref, local_rows), half_of(up_own, local_rows)),
            (rows_of(downs_ref, down_rows, lambda g: unit_place(s, g)), half_of(down_own, down_rows)),
        )
        gathers = [
            CubeGather(block, mine, cube_refs[3 * n : 3 * n + 3], s, f, F)
            for n, (block, mine) in enumerate(blocks)
        ]
        for gather in gathers:
            gather.start()

        own = s * own_heads + column

        def to_column(turn):
            j = lax.rem(column + turn, groups)
            return pltpu.make_async_remote_copy(
                src_ref=o_ref.at[j], dst_ref=heads_ref.at[own], send_sem=o_sent.at[turn], recv_sem=h_got.at[turn, 0],
                device_id=(s, j * splits + part), device_id_type=MESH,
            )

        def along(turn, d):
            ref = heads_ref.at[s * own_heads + lax.rem(column - turn + groups, groups)]
            return pltpu.make_async_remote_copy(
                src_ref=ref, dst_ref=ref, send_sem=h_sent.at[turn, d], recv_sem=h_got.at[turn, d],
                device_id=(lax.rem(s + d, S), f), device_id_type=MESH,
            )

        for turn in range(groups + 1):
            if turn < groups:
                j = lax.rem(column + turn, groups)
                forward_group(j, q_ref, kv_ref, qa_ref, ka_ref, att_ref, lse_ref, o_ref)
                if turn:
                    to_column(turn).start()
                else:
                    heads_ref[own] = o_ref[j]
            if turn != 1:
                came = max(turn - 1, 0)
                if came:
                    to_column(came).wait_recv()
                for d in range(1, S):
                    along(came, d).start()
        for number in range(1, gathers[0].rounds + 1):
            for gather in gathers:
                gather.step(number)
        for turn in range(groups):
            if turn:
                to_column(turn).wait_send()
            for d in range(1, S):
                along(turn, d).wait()
        for copy in here:
            copy.wait()
        for gather in gathers:
            gather.finish()
            gather.drain()

    attended, log_sum, heads_t, down_full, gate_full, up_full = pl.pallas_call(
        kernel_b,
        in_specs=[VMEM] * 4 + [ANY] * 3,
        out_specs=[VMEM] * 3 + [ANY] * 3,
        out_shape=[
            shape((groups, dim, group), F32),
            shape((groups, 1, group), F32),
            shape((heads, dim, group)),
            shape((hidden, width)),
            shape((width, hidden)),
            shape((width, hidden)),
        ],
        scratch_shapes=[
            pltpu.VMEM((groups, dim, group), BF16),
            pltpu.VMEM((local_rows, hidden), BF16),
            pltpu.VMEM((local_rows, hidden), BF16),
            pltpu.SemaphoreType.DMA((groups,)),
            *[pltpu.SemaphoreType.DMA((groups, S))] * 2,
            pltpu.SemaphoreType.DMA((2, F)),
            pltpu.SemaphoreType.DMA((3,)),
            *cube_sems(F),
            *cube_sems(F),
            *cube_sems(F),
        ],
        compiler_params=pltpu.CompilerParams(
            collective_id=1, has_side_effects=True, vmem_limit_bytes=VMEM_BYTES
        ),
        cost_estimate=pl.CostEstimate(flops=2 * 10**10, bytes_accessed=10**8, transcendentals=10**7),
    )(
        q_all, kv_all, query_marks, key_marks, w_down.reshape(S, down_rows, width), units(w_gate), units(w_up)
    )
    heads_t = heads_t.reshape(heads * dim, group)
    cot_group = cot_parts.reshape(group, width)

    middle = inputs + tn(heads_t, output_full)
    normed_mid = rms_scale(middle, gain_feed).astype(BF16)
    gate_act, up_act = nn(normed_mid, gate_full), nn(normed_mid, up_full)
    hidden_grad = nt(cot_group, down_full)
    sigmoid = jax.nn.sigmoid(gate_act)
    silu = gate_act * sigmoid
    hidden_low = (silu * up_act).astype(BF16)
    gate_low = (hidden_grad * up_act * sigmoid * (1.0 + gate_act * (1.0 - sigmoid))).astype(BF16)
    up_low = (hidden_grad * silu).astype(BF16)
    mid_part = (nt(gate_low, gate_full) + nt(up_low, up_full)).astype(BF16)
    out_part = nn(hidden_low, down_full).astype(BF16)
    by_owner = (S, half, 2, cut)
    gate_part = tn(normed_mid, gate_low).astype(BF16).reshape(by_owner + (hidden,))
    up_part = tn(normed_mid, up_low).astype(BF16).reshape(by_owner + (hidden,))
    down_part = tn(hidden_low, cot_group).astype(BF16).reshape(half, 2, down_rows, width)

    def pair(s, f):
        return (s, f + 1 - 2 * lax.rem(f, 2))

    def plan_e(s, f, ins, outs):
        u, gate, up, down = ins
        us, gates, ups, downs = outs
        remote, local = seq_swap(s, f, u, us)
        other = 1 - lax.rem(f, 2)
        for src, dst in ((gate.at[:, :, other], gates), (up.at[:, :, other], ups), (down.at[:, other], downs)):
            remote.append((src, dst, pair(s, f), None, None))
        return remote, local

    mid_terms, gate_other, up_other, down_other = exchange(
        3,
        [mid_part.reshape(S, rows, width), gate_part, up_part, down_part],
        [
            shape((S, rows, width)),
            shape((S, half, cut, hidden)),
            shape((S, half, cut, hidden)),
            shape((half, down_rows, width)),
        ],
        plan_e,
        lambda s, f: along_seq(s, f) + [pair(s, f)],
        (S - 1 + 3, 1),
    )
    parity = lax.rem(f, 2)

    def halves(own, other, axis):
        own = lax.dynamic_index_in_dim(own, parity, axis, keepdims=False)
        return (own.astype(F32) + other.astype(F32)).astype(BF16)

    own_middle = lax.dynamic_slice_in_dim(middle, s * rows, rows, 0)
    mid_grad, feed_gain = norm_back(jnp.sum(mid_terms.astype(F32), axis=0), own_middle, gain_feed)
    middle_grad = cotangent.astype(F32) + mid_grad
    middle_low = middle_grad.astype(BF16)
    heads_grad = nt(output_full, middle_low).astype(BF16).reshape(heads, dim, rows)
    own_heads_t = lax.dynamic_slice_in_dim(heads_t, s * rows, rows, 1)
    output_part = nn(own_heads_t, middle_low).astype(BF16).reshape(by_owner + (width,))

    def plan_f(s, f, ins, outs):
        grad, out = ins
        grads, outs_ = outs
        place = grads.at[f // splits, s]
        remote = [
            (grad.at[t[0] * own_heads + t[1] // splits], place, t, None, None)
            for t in like_parts(s, f)
        ]
        remote.append((out.at[:, :, 1 - lax.rem(f, 2)], outs_, pair(s, f), None, None))
        return remote, [(grad.at[s * own_heads + f // splits], place, None)]

    grad_heads, output_other = exchange(
        4,
        [heads_grad, output_part],
        [shape((groups, S, dim, rows)), shape((S, half, cut, width))],
        plan_f,
        lambda s, f: like_parts(s, f) + [pair(s, f)],
        (S * groups - 1 + 1, 1),
    )
    gate_half = halves(gate_part, gate_other, 2)
    up_half = halves(up_part, up_other, 2)
    down_half = halves(down_part, down_other, 1)
    output_half = halves(output_part, output_other, 2)

    def same_parity(s, f):
        return [(s, lax.rem(f + 2 * d, F)) for d in range(1, half)]

    def kernel_g(*refs):
        ins, sends, outs, gots = refs[:7], refs[7:12], refs[12:15], refs[15:20]
        sum_ref, send_sems, recv_sems, local_sems = refs[20:]
        s, f = lax.axis_index("seq"), lax.axis_index("fsdp")
        greet(along_seq(s, f) + same_parity(s, f))
        remote, local = seq_swap(s, f, sends[4], gots[4])
        for src, dst in zip(sends[:3], gots[:3]):
            for t in same_parity(s, f):
                remote.append((src.at[:, t[1] // 2], dst.at[f // 2], t, None, None))
            local.append((src.at[:, f // 2], dst.at[f // 2], None))
        for t in same_parity(s, f):
            remote.append((sends[3].at[t[1] // 2], gots[3].at[f // 2], t, None, None))
        local.append((sends[3].at[f // 2], gots[3].at[f // 2], None))
        finish = send_all((remote, local), send_sems, recv_sems, local_sems)
        backward_body(*ins, *outs, sum_ref)
        finish()

    copies = S - 1 + 4 * (half - 1)
    owned = (half, S, cut)
    query_grad, kv_grad, bias_terms, gate_got, up_got, output_got, down_got, out_terms = pl.pallas_call(
        kernel_g,
        in_specs=[VMEM] * 7 + [ANY] * 5,
        out_specs=[VMEM] * 3 + [ANY] * 5,
        out_shape=[
            shape((groups, dim, group)),
            shape((F, 2 * dim, group)),
            shape((2, VARIATES, QUERY_BLOCK), F32),
            shape(owned + (hidden,)),
            shape(owned + (hidden,)),
            shape(owned + (width,)),
            shape((half, down_rows, width)),
            shape((S, rows, width)),
        ],
        scratch_shapes=[
            pltpu.VMEM((F, 2 * dim, group), F32),
            pltpu.SemaphoreType.DMA((copies,)),
            pltpu.SemaphoreType.DMA((copies,)),
            pltpu.SemaphoreType.DMA((5,)),
        ],
        compiler_params=pltpu.CompilerParams(
            collective_id=5, has_side_effects=True, vmem_limit_bytes=VMEM_BYTES
        ),
    )(
        q_all,
        kv_all,
        query_marks,
        key_marks,
        grad_heads,
        attended,
        log_sum,
        gate_half,
        up_half,
        output_half,
        down_half,
        out_part.reshape(S, rows, width),
    )

    bias_sums = jnp.sum(bias_terms, axis=(1, 2))
    bias_pair = jnp.stack([bias_sums[0], bias_sums[1] - bias_sums[0]])
    bias_row = lax.dynamic_update_slice_in_dim(jnp.zeros((heads, 2), F32), bias_pair[None], head, 0)
    bias_row = jnp.pad(bias_row.reshape(1, 2 * heads), ((0, 0), (0, 128 - 2 * heads)))
    count = S * F
    chunks = width // 128

    def kernel_h(
        dq_ref, dkv_ref, gate_got, up_got, out_got, down_got, out_terms, middle_ref, mid_grad_ref, raw_ref, cos_ref,
        sin_ref, gain_q_ref, gain_k_ref, gain_ref, ws_ref, xs_ref, feed_ref, bias_ref,
        layer_ref, tokens_ref, attn_ref, output_ref, gate_ref, up_ref, down_ref, sums_ref,
        dqs, dkvs, gate_sum, up_sum, out_sum, gate_rows, up_rows, out_rows, down_sum, down_rows_ref, down_sent, down_arrived, pg_ref, u_ref, from_left, from_right,
        w_part, w_got, w_sum, w_rows, vec, vec_got,
        dq_sent, dq_got, dkv_sent, dkv_got, own_sem, swap_sent, swap_got, u_right, u_left, got_right, got_left,
        w_sent, w_arrived, rows_sent, rows_got, vec_sent, vec_arrived,
    ):
        s, f = lax.axis_index("seq"), lax.axis_index("fsdp")
        own = f // splits

        def copy(src, dst, sent, got, to):
            return pltpu.make_async_remote_copy(
                src_ref=src, dst_ref=dst, send_sem=sent, recv_sem=got, device_id=to, device_id_type=MESH
            )

        greet(everyone(s, f))
        pending = []
        here = [
            pltpu.make_async_copy(dkv_ref.at[f], dkvs.at[f], own_sem.at[0]),
            pltpu.make_async_copy(dq_ref.at[own], dqs.at[own], own_sem.at[1]),
        ]
        for load in here:
            load.start()
        for d in range(1, F):
            to, source = lax.rem(f + d, F), lax.rem(f + F - d, F)
            if d % splits == 0:
                send = copy(dq_ref.at[to // splits], dqs.at[own], dq_sent.at[d // splits], dq_got.at[d // splits], (s, to))
                send.start()
                pending.append(send)
            send = copy(dkv_ref.at[to], dkvs.at[f], dkv_sent.at[d], dkv_got.at[d], (s, to))
            send.start()
            pending.append(send)

        swaps = []
        for n, (got, total, rows_ref) in enumerate(
            ((gate_got, gate_sum, gate_rows), (up_got, up_sum, up_rows), (out_got, out_sum, out_rows))
        ):
            total[...] = jnp.sum(got[...].astype(F32), axis=0).astype(BF16)
            rows_ref[s] = total[s]
            for d in range(1, S):
                to = lax.rem(s + d, S)
                send = copy(total.at[to], rows_ref.at[s], swap_sent.at[n, d], swap_got.at[n, d], (to, f))
                send.start()
                swaps.append(send)
        layer_ref[...] = (middle_ref[...] + jnp.sum(out_terms[...].astype(F32), axis=0)).astype(BF16)
        to_plane = lax.rem(lax.rem(f, S) - s + S, S)
        down_sum[...] = jnp.sum(down_got[...].astype(F32), axis=0).astype(BF16)
        down_move = copy(down_sum, down_rows_ref, down_sent, down_arrived, (to_plane, f))
        pl.when(to_plane != s)(down_move.start)

        for load in here:
            load.wait()
        for send in pending:
            send.wait_recv()

        cosine, sine = cos_ref[...], sin_ref[...]

        def prepare_back(grad, raw, gain):
            front, back = grad[: dim // 2], grad[dim // 2 :]
            grad = join(front * cosine + back * sine, back * cosine - front * sine)
            inverse = lax.rsqrt(jnp.mean(raw * raw, axis=0, keepdims=True) + EPSILON)
            scaled = grad * gain
            mean = jnp.mean(scaled * raw, axis=0, keepdims=True)
            return inverse * scaled - raw * (inverse**3 * mean), grad * raw * inverse

        def gain_row(terms):
            folded = terms[:, :128]
            for n in range(1, group // 128):
                folded = folded + terms[:, n * 128 : (n + 1) * 128]
            return jnp.sum(folded.T, axis=0, keepdims=True)

        gain_terms = [jnp.zeros((dim, group), F32), jnp.zeros((dim, group), F32)]
        for h in range(own_heads):
            kv_sum = dkvs[h * splits].astype(F32)
            for n in range(1, splits):
                kv_sum = kv_sum + dkvs[h * splits + n].astype(F32)
            kv_sum = kv_sum.astype(BF16).astype(F32)
            for n, (grad, gain) in enumerate(
                ((dqs[h].astype(F32), gain_q_ref[...]), (kv_sum[:dim], gain_k_ref[...]))
            ):
                back, terms = prepare_back(grad, raw_ref[n, h], gain)
                gain_terms[n] += terms
                pg_ref[:, pl.ds(n * lanes + h * dim, dim)] = back.T.astype(BF16)
            pg_ref[:, pl.ds(2 * lanes + h * dim, dim)] = kv_sum[dim:].T.astype(BF16)

        attn_gain = jnp.zeros((1, width), F32)
        for b in range(S):
            grad = nt(pg_ref[pl.ds(b * rows, rows), :], ws_ref[...])
            x = xs_ref[b].astype(F32)
            inverse = lax.rsqrt(jnp.mean(x * x, axis=1, keepdims=True) + EPSILON)
            attn_gain += jnp.sum(grad * x * inverse, axis=0, keepdims=True)
            u_ref[b] = grad.astype(BF16)

        def right(t):
            return copy(u_ref.at[t], from_left.at[t], u_right.at[t], got_right.at[t], (s + 1, f))

        def left(t):
            return copy(u_ref.at[t], from_right.at[t], u_left.at[t], got_left.at[t], (s - 1, f))

        def take(t, buffer, hop):
            hop(t).wait_recv()
            u_ref[t] = (u_ref[t].astype(F32) + buffer[t].astype(F32)).astype(BF16)

        def pass_on(time):
            n = time - s
            pl.when((n >= 0) & (s >= 1))(lambda: take(S - 1 - n, from_left, right))
            pl.when((n >= 0) & (S - 1 - n > s))(lambda: right(S - 1 - n).start())
            m = time - (S - 1 - s)
            pl.when((m >= 0) & (s < S - 1))(lambda: take(m, from_right, left))
            pl.when((m >= 0) & (m < s))(lambda: left(m).start())

        pass_on(0)

        gains = jnp.concatenate([gain_row(gain_terms[0]), gain_row(gain_terms[1])], axis=1)
        gains = jnp.concatenate([gains, jnp.zeros((1, 256 - 2 * dim), F32)], axis=1)[:, :128]
        for n in range(chunks):
            part = slice(n * 128, (n + 1) * 128)
            vec[n] = jnp.concatenate(
                [attn_gain[:, part], feed_ref[:, part], gains, bias_ref[...], jnp.zeros((4, 128), F32)]
            )
        me = s * F + f
        vec_got[me] = vec[me * cut // 128]
        small = []
        for a in range(S):
            for b in range(F):
                if a or b:
                    to = (lax.rem(s + a, S), lax.rem(f + b, F))
                    chunk = (to[0] * F + to[1]) * cut // 128
                    small.append(
                        copy(vec.at[chunk], vec_got.at[me], vec_sent.at[a * F + b], vec_arrived.at[a * F + b], to)
                    )
                    small[-1].start()

        for b in range(S):
            normed = rms_scale(xs_ref[b].astype(F32), gain_ref[...]).astype(BF16)
            u_terms = tn(normed, pg_ref[pl.ds(b * rows, rows), :])
            if b == 0:
                total = u_terms
            else:
                total = total + u_terms
        w_part[...] = total.astype(BF16).reshape(S, F, cut, 3 * lanes)
        w_got[f] = w_part[:, f]
        for d in range(1, F):
            to = lax.rem(f + d, F)
            send = copy(w_part.at[:, to], w_got.at[f], w_sent.at[d], w_arrived.at[d], (s, to))
            send.start()
            swaps.append(send)
        attn_sends = swaps[-(F - 1) :]
        for n in range(1, S - 1):
            pass_on(n)
        for send in attn_sends:
            send.wait_recv()
        w_sum[...] = jnp.sum(w_got[...].astype(F32), axis=0).astype(BF16)
        w_rows[s] = w_sum[s]
        last = []
        for d in range(1, S):
            to = lax.rem(s + d, S)
            last.append(copy(w_sum.at[to], w_rows.at[s], rows_sent.at[d], rows_got.at[d], (to, f)))
            last[-1].start()

        for send in swaps[: 3 * (S - 1)]:
            send.wait_recv()
        for n in range(S):
            for g in range(F):
                holder = (g % S - n) % S * per_plane + g // S
                place = (holder * S + g % S) * down_rows
                part = slice(g * down_rows, (g + 1) * down_rows)
                gate_ref[:, place : place + down_rows] = gate_rows[n, :, part].astype(F32)
                up_ref[:, place : place + down_rows] = up_rows[n, :, part].astype(F32)
        output_ref[...] = jnp.sum(out_rows[...].astype(F32), axis=0)
        pl.when(to_plane != s)(down_move.wait)

        @pl.when(to_plane != s)
        def _():
            down_ref[...] = down_rows_ref[...].astype(F32)

        @pl.when(to_plane == s)
        def _():
            down_ref[...] = down_sum[...].astype(F32)

        for send in small:
            send.wait_recv()
        sums_ref[...] = jnp.sum(vec_got[...], axis=0)

        pass_on(S - 1)
        grad = u_ref[s].astype(F32)
        x = xs_ref[s].astype(F32)
        inverse = lax.rsqrt(jnp.mean(x * x, axis=1, keepdims=True) + EPSILON)
        scaled = grad * gain_ref[...]
        mean = jnp.mean(scaled * x, axis=1, keepdims=True)
        tokens_ref[...] = mid_grad_ref[...] + inverse * scaled - x * (inverse**3 * mean)

        for send in last:
            send.wait_recv()
        for n in range(S):
            for part in range(3):
                place = part * S * lanes + n * lanes
                attn_ref[:, place : place + lanes] = w_rows[n][:, part * lanes : (part + 1) * lanes].astype(F32)
        for t in range(S):
            pl.when(s < t)(lambda t=t: right(t).wait_send())
            pl.when(s > t)(lambda t=t: left(t).wait_send())
        for send in pending + swaps + small + last:
            send.wait_send()

    dma = pltpu.SemaphoreType.DMA
    layer_out, tokens_grad, attn_grad, output_grad, gate_grad, up_grad, down_grad, sums = pl.pallas_call(
        kernel_h,
        in_specs=[ANY] * 2 + [VMEM] * 17,
        out_specs=[VMEM] * 8,
        out_shape=[
            shape((rows, width)),
            shape((rows, width), F32),
            shape((cut, 3 * S * lanes), F32),
            shape((cut, width), F32),
            shape((cut, S * hidden), F32),
            shape((cut, S * hidden), F32),
            shape((down_rows, width), F32),
            shape((8, 128), F32),
        ],
        scratch_shapes=[
            pltpu.VMEM((own_heads, dim, group), BF16),
            pltpu.VMEM((F, 2 * dim, group), BF16),
            pltpu.VMEM((S, cut, hidden), BF16),
            pltpu.VMEM((S, cut, hidden), BF16),
            pltpu.VMEM((S, cut, width), BF16),
            pltpu.VMEM((S, cut, hidden), BF16),
            pltpu.VMEM((S, cut, hidden), BF16),
            pltpu.VMEM((S, cut, width), BF16),
            pltpu.VMEM((down_rows, width), BF16),
            pltpu.VMEM((down_rows, width), BF16),
            dma,
            dma,
            pltpu.VMEM((group, 3 * lanes), BF16),
            pltpu.VMEM((S, rows, width), BF16),
            pltpu.VMEM((S, rows, width), BF16),
            pltpu.VMEM((S, rows, width), BF16),
            pltpu.VMEM((S, F, cut, 3 * lanes), BF16),
            pltpu.VMEM((F, S, cut, 3 * lanes), BF16),
            pltpu.VMEM((S, cut, 3 * lanes), BF16),
            pltpu.VMEM((S, cut, 3 * lanes), BF16),
            pltpu.VMEM((chunks, 8, 128), F32),
            pltpu.VMEM((count, 8, 128), F32),
            *[dma((groups,))] * 2,
            *[dma((F,))] * 2,
            dma((2,)),
            *[dma((3, S))] * 2,
            *[dma((S,))] * 4,
            *[dma((F,))] * 2,
            *[dma((S,))] * 2,
            *[dma((count,))] * 2,
        ],
        compiler_params=pltpu.CompilerParams(
            collective_id=6, has_side_effects=True, vmem_limit_bytes=VMEM_BYTES
        ),
    )(
        query_grad, kv_grad, gate_got, up_got, output_got, down_got, out_terms, own_middle, middle_grad, raw, cosine, sine,
        gain_query[:, None], gain_key[:, None], gain_attn[None, :], w_qkv, x_parts, feed_gain[None, :], bias_row,
    )
    place = lax.rem((s * F + f) * cut, 128)
    return (
        layer_out,
        tokens_grad,
        attn_grad,
        output_grad,
        gate_grad,
        up_grad,
        down_grad,
        lax.dynamic_slice_in_dim(sums[0], place, cut),
        lax.dynamic_slice_in_dim(sums[1], place, cut),
        sums[2, :dim],
        sums[2, dim : 2 * dim],
        sums[3, : 2 * heads].reshape(heads, 2),
    )


def solution(mesh):
    by_token, by_fsdp, by_owner = P(("fsdp", "seq"), None), P("fsdp", None), P(("seq", "fsdp"), None)
    in_specs = (
        by_token,
        by_token,
        P(),
        P(),
        P(),
        P(),
        by_fsdp,
        P(),
        P(),
        P(),
        by_fsdp,
        P(),
        by_fsdp,
        by_fsdp,
        by_fsdp,
    )
    out_specs = (
        (by_token, by_token) + (by_owner,) * 5 + (P(("seq", "fsdp")),) * 2 + (P(),) * 3
    )
    return jax.shard_map(
        per_device, mesh=mesh, in_specs=in_specs, out_specs=out_specs, check_vma=False
    )
```

```python
import functools

import jax
import jax.numpy as jnp
from jax import lax
from jax.experimental import pallas as pl
from jax.experimental.pallas import tpu as pltpu
from jax.sharding import PartitionSpec as P

EPSILON = 1e-06
F32, BF16 = jnp.float32, jnp.bfloat16
VARIATES = 8
AWAY = 1024.0
QUERY_BLOCK = 256
LSE_ROW, VAR_ROW = 32, 40
MESH = pl.DeviceIdType.MESH
ANY = pl.BlockSpec(memory_space=pl.ANY)
VMEM = pl.BlockSpec(memory_space=pltpu.VMEM)
VMEM_BYTES = 56 * 2**20


def nn(a, b):
    return jnp.dot(a, b, preferred_element_type=F32)


def nt(a, b):
    return lax.dot_general(a, b, (((1,), (1,)), ((), ())), preferred_element_type=F32)


def tn(a, b):
    return lax.dot_general(a, b, (((0,), (0,)), ((), ())), preferred_element_type=F32)


def pieces(values):
    high = values.astype(BF16).astype(F32)
    middle = (values - high).astype(BF16).astype(F32)
    return high, middle, (values - high - middle).astype(BF16).astype(F32)


def send_all(plan, send_sems, recv_sems, local_sems):
    remote, local = plan
    copies = []
    for n, (src, dst, device, may_send, may_receive) in enumerate(remote):
        copy = pltpu.make_async_remote_copy(
            src_ref=src,
            dst_ref=dst,
            send_sem=send_sems.at[n],
            recv_sem=recv_sems.at[n],
            device_id=device,
            device_id_type=MESH,
        )
        when(may_send, copy.start)
        copies.append((copy, may_send, may_receive))
    locals_ = []
    for n, (src, dst, may) in enumerate(local):
        copy = pltpu.make_async_copy(src, dst, local_sems.at[n])
        when(may, copy.start)
        locals_.append((copy, may))

    def finish():
        for copy, may in locals_:
            when(may, copy.wait)
        for copy, may_send, may_receive in copies:
            when(may_send, copy.wait_send)
            when(may_receive, copy.wait_recv)

    return finish


def when(condition, action):
    if condition is None:
        action()
    else:
        pl.when(condition)(action)


def greet(devices):
    barrier = pltpu.get_barrier_semaphore()
    for device in devices:
        pl.semaphore_signal(barrier, inc=1, device_id=device, device_id_type=MESH)
    pl.semaphore_wait(barrier, len(devices))


class Line:
    def __init__(self, block, sems, s, f, S):
        self.block, (self.sent, self.got) = block, sems
        self.s, self.f, self.S = s, f, S

    def hop(self, plane, slot, step):
        ref = self.block(plane, slot)
        return pltpu.make_async_remote_copy(
            src_ref=ref,
            dst_ref=ref,
            send_sem=self.sent.at[plane, slot, int(step > 0)],
            recv_sem=self.got.at[plane, slot],
            device_id=(self.s + step, self.f),
            device_id_type=MESH,
        )

    def each_hop(self, slot, distance, action):
        s, S = self.s, self.S
        pl.when((s - distance + 1) * (S - 1 - s) > 0)(
            lambda: action(self.hop(s - distance, slot, 1))
        )
        pl.when((S - s - distance) * s > 0)(lambda: action(self.hop(s + distance, slot, -1)))

    def send(self, slot):
        self.each_hop(slot, 0, lambda hop: hop.start())

    def arrive(self, slot, distance):
        s, S = self.s, self.S
        pl.when(s - distance >= 0)(lambda: self.hop(s - distance, slot, 1).wait_recv())
        pl.when(s + distance < S)(lambda: self.hop(s + distance, slot, -1).wait_recv())
        self.each_hop(slot, distance, lambda hop: hop.start())

    def drain(self, slot):
        for distance in range(self.S):
            self.each_hop(slot, distance, lambda hop: hop.wait_send())


def line_sems(S, slots):
    return [pltpu.SemaphoreType.DMA((S, slots, 2)), pltpu.SemaphoreType.DMA((S, slots))]


class LineSum:
    def __init__(self, terms, from_left, from_right, sems, s, f, S):
        self.terms, self.from_left, self.from_right = terms, from_left, from_right
        self.sent, self.got = sems
        self.s, self.f, self.S = s, f, S

    def hop(self, t, to_right):
        return pltpu.make_async_remote_copy(
            src_ref=self.terms.at[t],
            dst_ref=(self.from_left if to_right else self.from_right).at[t],
            send_sem=self.sent.at[int(to_right), t],
            recv_sem=self.got.at[int(to_right), t],
            device_id=(self.s + (1 if to_right else -1), self.f),
            device_id_type=MESH,
        )

    def take(self, t, to_right):
        self.hop(t, to_right).wait_recv()
        came = (self.from_left if to_right else self.from_right)[t]
        self.terms[t] = (self.terms[t].astype(F32) + came.astype(F32)).astype(BF16)

    def step(self, time):
        s, S = self.s, self.S
        n = time - s
        pl.when((n >= 0) & (s >= 1))(lambda: self.take(S - 1 - n, True))
        pl.when((n >= 0) & (S - 1 - n > s))(lambda: self.hop(S - 1 - n, True).start())
        m = time - (S - 1 - s)
        pl.when((m >= 0) & (s < S - 1))(lambda: self.take(m, False))
        pl.when((m >= 0) & (m < s))(lambda: self.hop(m, False).start())

    def drain(self):
        for t in range(self.S):
            pl.when(self.s < t)(lambda t=t: self.hop(t, True).wait_send())
            pl.when(self.s > t)(lambda t=t: self.hop(t, False).wait_send())


def flipped(f, bit):
    step = 2**bit
    return f + step - 2 * step * lax.rem(f // step, 2)


class CubeGather:
    def __init__(self, block, own, sems, s, f, F):
        self.block, self.own, (self.sent, self.shared, self.got) = block, own, sems
        self.s, self.f, self.F = s, f, F
        bits = list(range(1, F.bit_length() - 1))
        self.orders = (bits, bits[::-1])

    def copy(self, g, half, sem, to, own=False):
        ref = self.block(g, half)
        return pltpu.make_async_remote_copy(
            src_ref=self.own(half) if own else ref,
            dst_ref=ref,
            send_sem=sem,
            recv_sem=self.got.at[g, half],
            device_id=(self.s, to),
            device_id_type=MESH,
        )

    def held(self, half, rounds):
        masks = [((), 0)]
        for n, bit in enumerate(self.orders[half][:rounds]):
            masks += [(mask + (bit,), n + 1) for mask, _ in list(masks)]
        return masks

    def device(self, mask):
        g = self.f
        for bit in mask:
            g = flipped(g, bit)
        return g

    def sends(self, half, since):
        rounds = len(self.orders[half])
        out = []
        for place, (mask, came) in enumerate(self.held(half, rounds)):
            for n in range(came, rounds):
                if came == since:
                    out.append((n, place, mask))
        return out

    def send(self, half, n, place, mask):
        bit = self.orders[half][n]
        sem = self.sent.at[half, n, place]
        return self.copy(self.device(mask), half, sem, flipped(self.f, bit), not mask)

    def shares(self, half, since):
        return [
            self.copy(
                self.device(mask), half, self.shared.at[half, place], flipped(self.f, 0), not mask
            )
            for place, (mask, came) in enumerate(self.held(half, len(self.orders[half])))
            if came == since
        ]

    @property
    def rounds(self):
        return len(self.orders[0])

    def start(self):
        for half in range(2):
            self.send(half, 0, 0, ()).start()
        for half in range(2):
            self.shares(half, 0)[0].start()

    def step(self, number):
        for half in range(2):
            shares = self.shares(half, number)
            for share in shares:
                share.wait_recv()
            if number < self.rounds:
                for which in self.sends(half, number) + self.sends(half, 0)[number : number + 1]:
                    if which[0] == number or which[1]:
                        self.send(half, *which).start()
            for share in shares:
                share.start()

    def finish(self):
        for half in range(2):
            for place, (mask, _) in enumerate(self.held(half, self.rounds)):
                g = flipped(self.device(mask), 0)
                self.copy(g, half, self.shared.at[half, place], self.f).wait_recv()

    def drain(self):
        for half in range(2):
            for number in range(self.rounds + 1):
                for which in self.sends(half, number):
                    self.send(half, *which).wait_send()
                for share in self.shares(half, number):
                    share.wait_send()


def cube_sems(F):
    rounds = F.bit_length() - 2
    return [
        pltpu.SemaphoreType.DMA((2, rounds, F // 4)),
        pltpu.SemaphoreType.DMA((2, F // 2)),
        pltpu.SemaphoreType.DMA((F, 2)),
    ]


def shape(dims, dtype=BF16):
    return jax.ShapeDtypeStruct(tuple(dims), dtype)


def join(a, b):
    return jnp.concatenate([a, b], axis=0)


def side_by_side(ref, *index):
    return jnp.concatenate([ref[(*index, n)] for n in range(ref.shape[len(index)])], axis=1)


def forward_group(j, q_ref, kv_ref, qa_ref, ka_ref, att_ref, lse_ref, o_ref):
    width, rows = att_ref.shape[1:]
    span = q_ref.shape[-1]
    sub = QUERY_BLOCK // span

    def block(i, _):
        cols = pl.ds(pl.multiple_of(i * QUERY_BLOCK, QUERY_BLOCK), QUERY_BLOCK)
        q_t = jnp.concatenate([q_ref[j, i * sub + n] for n in range(sub)], axis=1)
        queries = join(q_t, qa_ref[j, :, cols]).T
        total = jnp.zeros((QUERY_BLOCK, 2 * width), F32)
        for g in range(kv_ref.shape[0]):
            kv = side_by_side(kv_ref, g)
            keys = join(kv[:width], ka_ref[g])
            values = join(kv[width:], jnp.ones((width, rows), BF16))
            weights = jnp.exp(nn(queries, keys)).astype(BF16)
            total += nt(weights, values)
        total = total.T
        weight_sum = total[width : width + 1]
        attended = total[:width] / weight_sum
        att_ref[j, :, cols] = attended
        o_ref[j, :, cols] = attended.astype(BF16)
        lse_ref[j, :, cols] = jnp.log(weight_sum)
        return 0

    lax.fori_loop(0, rows // QUERY_BLOCK, block, 0)


def with_rows(base, first, rows):
    index = lax.broadcasted_iota(jnp.int32, base.shape, 0)
    for n, row in enumerate(rows):
        base = jnp.where(index == first + n, row, base)
    return base


def backward_body(q_ref, kv_ref, qa_ref, ka_ref, do_ref, att_ref, lse_ref, dq_ref, dkv_ref, bias_ref, sum_ref):
    width, rows = att_ref.shape[1:]
    blocks = rows // QUERY_BLOCK
    span = q_ref.shape[-1]
    sub = QUERY_BLOCK // span
    sum_ref[...] = jnp.zeros_like(sum_ref)
    bias_ref[...] = jnp.zeros_like(bias_ref)

    def block(i, _):
        j = i // blocks
        first = (i % blocks) * sub
        cols = pl.ds(pl.multiple_of((i % blocks) * QUERY_BLOCK, QUERY_BLOCK), QUERY_BLOCK)
        q_t = jnp.concatenate([q_ref[j, first + n] for n in range(sub)], axis=1)
        marks = qa_ref[j, :, cols].astype(F32)
        extra = with_rows(marks, LSE_ROW, pieces(-lse_ref[j, :, cols])).astype(BF16)
        queries = join(q_t, extra).T
        grad_t = jnp.concatenate([do_ref[j, first + n] for n in range(sub)], axis=1)
        delta = jnp.sum(grad_t.astype(F32) * att_ref[j, :, cols], axis=0, keepdims=True)
        extra = with_rows(jnp.zeros((width, QUERY_BLOCK), F32), 0, pieces(-delta)).astype(BF16)
        grads = join(grad_t, extra).T
        query_sum = jnp.zeros((QUERY_BLOCK, 2 * width), F32)
        for g in range(kv_ref.shape[0]):
            kv = side_by_side(kv_ref, g)
            keys = join(kv[:width], ka_ref[g])
            values = join(kv[width:], jnp.ones((width, rows), BF16))
            probs = jnp.exp(nn(queries, keys))
            score_grad = (probs * nn(grads, values)).astype(BF16)
            sum_ref[g, width:, :] += nn(grad_t, probs.astype(BF16))
            sum_ref[g, :width, :] += nn(q_t, score_grad)
            query_sum += nt(score_grad, keys)
        query_sum = query_sum.T
        dq_ref[j, :, cols] = (query_sum[:width] * width**-0.5).astype(BF16)
        by_variate = query_sum[width : width + VARIATES]
        bias_ref[0] += by_variate * marks[VAR_ROW : VAR_ROW + VARIATES]
        bias_ref[1] += by_variate
        return 0

    lax.fori_loop(0, q_ref.shape[0] * blocks, block, 0)
    dkv_ref[...] = sum_ref[...].astype(BF16)


def rms_scale(vector, gain, axis=-1):
    return vector * lax.rsqrt(jnp.mean(vector * vector, axis=axis, keepdims=True) + EPSILON) * gain


def per_device(
    tokens,
    cotangent,
    doc_starts,
    variate_ids,
    time_ids,
    gain_attn,
    w_attn,
    gain_query,
    gain_key,
    variate_bias,
    w_output,
    gain_feed,
    w_gate,
    w_up,
    w_down,
):
    S, F = lax.axis_size("seq"), lax.axis_size("fsdp")
    s, f = lax.axis_index("seq"), lax.axis_index("fsdp")
    rows, width = tokens.shape
    heads = variate_bias.shape[0]
    dim = gain_query.shape[0]
    own_heads = heads // S
    splits = F // own_heads
    group = rows * S
    groups = F // splits
    hidden = w_down.shape[0] * F // S
    half = F // 2
    cut = width // (S * F)
    lanes = own_heads * dim

    def along_seq(s, f):
        return [(lax.rem(s + d, S), f) for d in range(1, S)]

    def along_fsdp(s, f):
        return [(s, lax.rem(f + d, F)) for d in range(1, F)]

    def along_both(s, f):
        return along_seq(s, f) + along_fsdp(s, f)

    def like_parts(s, f):
        return [
            (lax.rem(s + a, S), lax.rem(f + b * splits, F))
            for a in range(S)
            for b in range(groups)
            if a or b
        ]

    def everyone(s, f):
        return [(lax.rem(s + a, S), lax.rem(f + b, F)) for a in range(S) for b in range(F) if a or b]

    def seq_swap(s, f, src, dst):
        remote = [(src.at[t[0]], dst.at[s], t, None, None) for t in along_seq(s, f)]
        return remote, [(src.at[s], dst.at[s], None)]

    frequency = (10000.0 ** (-2.0 * jnp.arange(dim // 2, dtype=F32) / dim))[:, None]
    per_plane = F // S
    down_rows = w_down.shape[0] // S
    local_rows = w_attn.shape[0]
    total = F * group

    def peers_a(s, f):
        return [(lax.rem(s + 1, S), f), (lax.rem(s + S - 1, S), f)] + along_fsdp(s, f)

    def kernel_a(
        x_ref, w_ref, wo_ref, cot_ref, times_ref, freq_ref, gain_ref, gain_q_ref, gain_k_ref, ids_ref, ids_mine_ref,
        starts_ref, bias_ref,
        xs_ref, ws_ref, raw_ref, cots_ref, cos_ref, sin_ref, ka_ref, qa_ref, q_ref, kv_ref, wos_ref,
        q_out, kv_out, w_sem, x_sent, x_got, c_sent, c_got, pair_sent, pair_shared, pair_got,
        wo_sent, wo_shared, wo_got, kv_sent, kv_shared, kv_got, q_sent, q_got, own_sem,
    ):
        s, f = lax.axis_index("seq"), lax.axis_index("fsdp")
        loads = []
        for n in range(3):
            src = w_ref.at[:, pl.ds(pl.multiple_of(n * S * lanes + s * lanes, 128), lanes)]
            dst = ws_ref.at[pl.ds(f * local_rows, local_rows), pl.ds(n * lanes, lanes)]
            loads.append(pltpu.make_async_copy(src, dst, w_sem.at[n]))
        for load in loads:
            load.start()
        wo_here = pltpu.make_async_copy(wo_ref, wos_ref.at[pl.ds(f * local_rows, local_rows)], w_sem.at[3])
        wo_here.start()
        xs_ref[s] = x_ref[...]
        cots_ref[s] = cot_ref[...]
        greet(peers_a(s, f))
        xs = Line(lambda plane, slot: xs_ref.at[plane], (x_sent, x_got), s, f, S)
        xs.send(0)
        for load in loads:
            load.wait()

        def rows_of(ref):
            size = local_rows // 2
            return lambda g, half: ref.at[pl.ds(g * local_rows + half * size, size)]

        def half_of(ref):
            size = local_rows // 2
            return lambda half: ref.at[pl.ds(half * size, size)]

        ws = CubeGather(
            rows_of(ws_ref), lambda half: rows_of(ws_ref)(f, half), (pair_sent, pair_shared, pair_got), s, f, F
        )
        wos = CubeGather(rows_of(wos_ref), half_of(wo_ref), (wo_sent, wo_shared, wo_got), s, f, F)
        ws.start()

        angles = freq_ref[...] * times_ref[...].astype(F32)
        cos_ref[...] = jnp.cos(angles)
        sin_ref[...] = jnp.sin(angles)
        pair = [bias_ref[s * own_heads + f // splits, n] for n in range(2)]
        difference = pieces(jnp.full((VARIATES, group), pair[0] - pair[1], F32))
        index = lax.broadcasted_iota(jnp.int32, (VARIATES, group), 0)

        def marks(g, ids):
            positions = g * group + lax.broadcasted_iota(jnp.int32, (VARIATES, group), 1)
            docs = jnp.zeros((VARIATES, group), jnp.int32) - 1
            for n in range(doc_starts.shape[0]):
                docs = docs + (starts_ref[n] <= positions).astype(jnp.int32)
            return (docs == index).astype(F32), (ids == index).astype(F32)

        for g in range(F):
            doc, var = marks(g, ids_ref[g])
            tail = (index < 3).astype(F32)
            none = jnp.zeros((dim - LSE_ROW - VARIATES, group), F32)
            ka_ref[g] = jnp.concatenate([var, var, var, 1.0 - doc, tail, none]).astype(BF16)
        for j in range(groups):
            doc, var = marks(j * splits + lax.rem(f, splits), ids_mine_ref[j])
            none = jnp.zeros((VARIATES, group), F32)
            rest = jnp.zeros((dim - VAR_ROW - VARIATES, group), F32)
            scaled = [var * part for part in difference]
            qa_ref[j] = jnp.concatenate([*scaled, doc * -AWAY, none, var, rest]).astype(BF16)

        def kv_copy(g, b, src, sem, to):
            return pltpu.make_async_remote_copy(
                src_ref=src, dst_ref=kv_ref.at[g, b], send_sem=sem, recv_sem=kv_got.at[g, b],
                device_id=(s, to), device_id_type=MESH,
            )

        def to_heads(b, d):
            to = lax.rem(f + 2 * d, F)
            return kv_copy(f, b, kv_out.at[b, to // splits], kv_sent.at[b, d], to)

        def to_neighbour(b, d):
            g = lax.rem(f + 2 * d, F)
            src = kv_ref.at[g, b] if d else kv_out.at[b, f // splits]
            return kv_copy(g, b, src, kv_shared.at[b, d], flipped(f, 0))

        def queries_to_heads(b, d):
            to = lax.rem(f + d * splits, F)
            return pltpu.make_async_remote_copy(
                src_ref=q_out.at[b, to // splits], dst_ref=q_ref.at[f // splits, b], send_sem=q_sent.at[b, d],
                recv_sem=q_got.at[f // splits, b], device_id=(s, to), device_id_type=MESH,
            )

        def own_copies(b):
            return (
                pltpu.make_async_copy(kv_out.at[b, f // splits], kv_ref.at[f, b], own_sem.at[b, 0]),
                pltpu.make_async_copy(q_out.at[b, f // splits], q_ref.at[f // splits, b], own_sem.at[b, 1]),
            )

        def project(b):
            normed = rms_scale(xs_ref[b].astype(F32), gain_ref[...]).astype(BF16)
            projected = nn(normed, ws_ref[...]).T.reshape(3, own_heads, dim, rows)
            cols = pl.ds(pl.multiple_of(b * rows, rows), rows)
            cosine, sine = cos_ref[:, cols], sin_ref[:, cols]

            def turned(raw, gain):
                raw = rms_scale(raw, gain, axis=1)
                front, back = raw[:, : dim // 2], raw[:, dim // 2 :]
                return jnp.concatenate(
                    [front * cosine - back * sine, front * sine + back * cosine], axis=1
                )

            raw_ref[0, :, :, cols] = projected[0]
            raw_ref[1, :, :, cols] = projected[1]
            q_out[b] = (turned(projected[0], gain_q_ref[...]).astype(BF16).astype(F32) * dim**-0.5).astype(BF16)
            kv_out[b, :, :dim] = turned(projected[1], gain_k_ref[...]).astype(BF16)
            kv_out[b, :, dim:] = projected[2].astype(BF16)
            for d in range(1, half):
                to_heads(b, d).start()
            for d in range(1, groups):
                queries_to_heads(b, d).start()
            to_neighbour(b, 0).start()
            for copy in own_copies(b):
                copy.start()

        def share(b):
            for d in range(1, half):
                to_neighbour(b, d).wait_recv()
                to_neighbour(b, d).start()

        for number in range(1, ws.rounds + 1):
            ws.step(number)
        wos.start()
        ws.finish()
        project(s)
        cots = Line(lambda plane, slot: cots_ref.at[plane], (c_sent, c_got), s, f, S)
        for distance in range(1, S):
            xs.arrive(0, distance)
            if distance == min(2, S - 1):
                cots.send(0)
            pl.when(s - distance >= 0)(lambda distance=distance: project(s - distance))
            pl.when(s + distance < S)(lambda distance=distance: project(s + distance))
            if distance < S - 1 and distance < wos.rounds:
                wos.step(distance)

        def share_all(b, _):
            share(b)
            return 0

        lax.fori_loop(0, S, share_all, 0)
        for number in range(min(S - 1, wos.rounds), wos.rounds + 1):
            wos.step(number)
        for distance in range(1, S):
            cots.arrive(0, distance)

        def last(b, _):
            for copy in own_copies(b):
                copy.wait()
            for d in range(half):
                if d:
                    to_heads(b, d).wait_send()
                to_neighbour(b, d).wait_send()
                g = lax.rem(flipped(f, 0) + 2 * d, F)
                kv_copy(g, b, kv_ref.at[g, b], kv_shared.at[b, d], f).wait_recv()
            for d in range(1, groups):
                queries_to_heads(b, d).wait_send()
                g = lax.rem(f + d * splits, F)
                pltpu.make_async_remote_copy(
                    src_ref=q_out.at[b, 0], dst_ref=q_ref.at[g // splits, b], send_sem=q_sent.at[b, d],
                    recv_sem=q_got.at[g // splits, b], device_id=(s, g), device_id_type=MESH,
                ).wait_recv()
            return 0

        lax.fori_loop(0, S, last, 0)
        for line in (xs, cots):
            line.drain(0)
        wos.finish()
        wo_here.wait()
        ws.drain()
        wos.drain()

    smem = pl.BlockSpec(memory_space=pltpu.SMEM)
    ids = variate_ids.reshape(F, 1, group)
    ids_mine = lax.dynamic_index_in_dim(
        ids.reshape(groups, splits, 1, group), lax.rem(f, splits), 1, keepdims=False
    )
    x_parts, w_qkv, raw, cot_parts, cosine, sine, key_marks, query_marks, q_all, kv_all, output_full = pl.pallas_call(
        kernel_a,
        in_specs=[VMEM, ANY, ANY] + [VMEM] * 8 + [smem] * 2,
        out_specs=[VMEM] * 8 + [ANY] * 3,
        out_shape=[
            shape((S, rows, width)),
            shape((width, 3 * lanes)),
            shape((2, own_heads, dim, group), F32),
            shape((S, rows, width)),
            shape((dim // 2, group), F32),
            shape((dim // 2, group), F32),
            shape((F, dim, group)),
            shape((groups, dim, group)),
            shape((groups, S, dim, rows)),
            shape((F, S, 2 * dim, rows)),
            shape((heads * dim, width)),
        ],
        scratch_shapes=[
            pltpu.VMEM((S, own_heads, dim, rows), BF16),
            pltpu.VMEM((S, own_heads, 2 * dim, rows), BF16),
            pltpu.SemaphoreType.DMA((4,)),
            *line_sems(S, 1),
            *line_sems(S, 1),
            *cube_sems(F),
            *cube_sems(F),
            pltpu.SemaphoreType.DMA((S, half)),
            pltpu.SemaphoreType.DMA((S, half)),
            pltpu.SemaphoreType.DMA((F, S)),
            pltpu.SemaphoreType.DMA((S, groups)),
            pltpu.SemaphoreType.DMA((groups, S)),
            pltpu.SemaphoreType.DMA((S, 2)),
        ],
        compiler_params=pltpu.CompilerParams(
            collective_id=0, has_side_effects=True, vmem_limit_bytes=VMEM_BYTES
        ),
        cost_estimate=pl.CostEstimate(flops=10**9, bytes_accessed=10**8, transcendentals=0),
    )(
        tokens,
        w_attn,
        w_output,
        cotangent,
        lax.dynamic_slice_in_dim(time_ids, f * group, group)[None, :],
        frequency,
        gain_attn[None, :],
        gain_query[:, None],
        gain_key[:, None],
        ids,
        ids_mine,
        doc_starts,
        variate_bias,
    )
    head = s * own_heads + f // splits

    def unit_place(s, f):
        return lax.rem(f, per_plane) * S + lax.rem(f // per_plane + s, S)

    def unit_block(s, g):
        holder = lax.rem(lax.rem(g, S) - s + S, S) * per_plane + g // S
        return holder * S + lax.rem(g, S)

    def units(w):
        if down_rows % 128 == 0:
            return w
        blocks = w.reshape(w.shape[0], S * F, down_rows)
        return jnp.concatenate(
            [lax.dynamic_index_in_dim(blocks, unit_block(s, g), 1, False) for g in range(F)], axis=1
        )

    def kernel_b(
        q_ref, kv_ref, qa_ref, ka_ref, wd_ref, wg_ref, wu_ref,
        att_ref, lse_ref, heads_ref, downs_ref, gates_ref, ups_ref,
        o_ref, gate_own, up_own, o_sent, h_sent, h_got, w_sem, here_sem, *cube_refs,
    ):
        s, f = lax.axis_index("seq"), lax.axis_index("fsdp")
        column, part = f // splits, lax.rem(f, splits)
        down_own = wd_ref.at[lax.rem(f // per_plane + s, S)]
        loads = []
        for n, (src, dst) in enumerate(((wg_ref, gate_own), (wu_ref, up_own))):
            if down_rows % 128:
                loads.append(pltpu.make_async_copy(src, dst, w_sem.at[n, 0]))
                continue
            for g in range(F):
                cols = pl.ds(pl.multiple_of(unit_block(s, g) * down_rows, 128), down_rows)
                place = pl.ds(g * down_rows, down_rows)
                loads.append(pltpu.make_async_copy(src.at[:, cols], dst.at[:, place], w_sem.at[n, g]))
        for load in loads:
            load.start()
        greet(along_both(s, f))
        for load in loads:
            load.wait()
        mine = pl.ds(f * local_rows, local_rows)
        here = [
            pltpu.make_async_copy(gate_own, gates_ref.at[mine], here_sem.at[0]),
            pltpu.make_async_copy(up_own, ups_ref.at[mine], here_sem.at[1]),
            pltpu.make_async_copy(
                down_own, downs_ref.at[pl.ds(unit_place(s, f) * down_rows, down_rows)], here_sem.at[2]
            ),
        ]
        for copy in here:
            copy.start()

        def rows_of(ref, size, place=lambda g: g):
            return lambda g, half: ref.at[pl.ds(place(g) * size + half * (size // 2), size // 2)]

        def half_of(ref, size):
            return lambda half: ref.at[pl.ds(half * (size // 2), size // 2)]

        blocks = (
            (rows_of(gates_ref, local_rows), half_of(gate_own, local_rows)),
            (rows_of(ups_ref, local_rows), half_of(up_own, local_rows)),
            (rows_of(downs_ref, down_rows, lambda g: unit_place(s, g)), half_of(down_own, down_rows)),
        )
        gathers = [
            CubeGather(block, mine, cube_refs[3 * n : 3 * n + 3], s, f, F)
            for n, (block, mine) in enumerate(blocks)
        ]
        for gather in gathers:
            gather.start()

        own = s * own_heads + column

        def to_column(turn):
            j = lax.rem(column + turn, groups)
            return pltpu.make_async_remote_copy(
                src_ref=o_ref.at[j], dst_ref=heads_ref.at[own], send_sem=o_sent.at[turn], recv_sem=h_got.at[turn, 0],
                device_id=(s, j * splits + part), device_id_type=MESH,
            )

        def along(turn, d):
            ref = heads_ref.at[s * own_heads + lax.rem(column - turn + groups, groups)]
            return pltpu.make_async_remote_copy(
                src_ref=ref, dst_ref=ref, send_sem=h_sent.at[turn, d], recv_sem=h_got.at[turn, d],
                device_id=(lax.rem(s + d, S), f), device_id_type=MESH,
            )

        for turn in range(groups + 1):
            if turn < groups:
                j = lax.rem(column + turn, groups)
                forward_group(j, q_ref, kv_ref, qa_ref, ka_ref, att_ref, lse_ref, o_ref)
                if turn:
                    to_column(turn).start()
                else:
                    heads_ref[own] = o_ref[j]
            if turn != 1:
                came = max(turn - 1, 0)
                if came:
                    to_column(came).wait_recv()
                for d in range(1, S):
                    along(came, d).start()
        for number in range(1, gathers[0].rounds + 1):
            for gather in gathers:
                gather.step(number)
        for turn in range(groups):
            if turn:
                to_column(turn).wait_send()
            for d in range(1, S):
                along(turn, d).wait()
        for copy in here:
            copy.wait()
        for gather in gathers:
            gather.finish()
            gather.drain()

    attended, log_sum, heads_t, down_full, gate_full, up_full = pl.pallas_call(
        kernel_b,
        in_specs=[VMEM] * 4 + [ANY] * 3,
        out_specs=[VMEM] * 3 + [ANY] * 3,
        out_shape=[
            shape((groups, dim, group), F32),
            shape((groups, 1, group), F32),
            shape((heads, dim, group)),
            shape((hidden, width)),
            shape((width, hidden)),
            shape((width, hidden)),
        ],
        scratch_shapes=[
            pltpu.VMEM((groups, dim, group), BF16),
            pltpu.VMEM((local_rows, hidden), BF16),
            pltpu.VMEM((local_rows, hidden), BF16),
            pltpu.SemaphoreType.DMA((groups,)),
            *[pltpu.SemaphoreType.DMA((groups, S))] * 2,
            pltpu.SemaphoreType.DMA((2, F)),
            pltpu.SemaphoreType.DMA((3,)),
            *cube_sems(F),
            *cube_sems(F),
            *cube_sems(F),
        ],
        compiler_params=pltpu.CompilerParams(
            collective_id=1, has_side_effects=True, vmem_limit_bytes=VMEM_BYTES
        ),
        cost_estimate=pl.CostEstimate(flops=2 * 10**10, bytes_accessed=10**8, transcendentals=10**7),
    )(
        q_all, kv_all, query_marks, key_marks, w_down.reshape(S, down_rows, width), units(w_gate), units(w_up)
    )
    heads_t = heads_t.reshape(heads * dim, group)

    def pair(s, f):
        return (s, flipped(f, 0))

    def same_parity(s, f):
        return [(s, lax.rem(f + 2 * d, F)) for d in range(1, half)]

    def peers_c(s, f):
        return like_parts(s, f) + [(s, lax.rem(f + d, F)) for d in range(1, F) if d % splits]

    block = 256 if width % 256 == 0 and hidden % 256 == 0 else 128

    def kernel_c(
        heads_ref, wo_ref, xs_ref, wg_ref, wu_ref, cots_ref, wd_ref, gain_ref,
        grads_ref, middle_ref, mid_grad_ref, feed_ref, out_ref, gate_got, up_got, down_half, output_half,
        h_v, wo_v, x_v, wg_v, wu_v, cot_v, wd_v, mid_v, n_v, n_t, hid_v, hid_t, gl_v, ul_v, u_ref, from_left, from_right,
        gate_part, up_part, down_part, output_part, gate_other, up_other, down_other, output_other, gate_half, up_half,
        hg_ref, load_sem, u_sent, u_got, pair_sent, pair_got, spread_sent, spread_got, own_sem, f_sent, f_got,
    ):
        s, f = lax.axis_index("seq"), lax.axis_index("fsdp")
        loads = [
            pltpu.make_async_copy(src, dst, load_sem.at[n])
            for n, (src, dst) in enumerate(
                (
                    (heads_ref, h_v), (wo_ref, wo_v), (xs_ref, x_v), (wg_ref, wg_v), (wu_ref, wu_v), (cots_ref, cot_v),
                    (wd_ref, wd_v),
                )
            )
        ]
        for load in loads:
            load.start()
        greet(peers_c(s, f))

        def copy(src, dst, sent, got, to):
            return pltpu.make_async_remote_copy(
                src_ref=src, dst_ref=dst, send_sem=sent, recv_sem=got, device_id=to, device_id_type=MESH
            )

        for load in loads[:3]:
            load.wait()
        heads_rows = h_v[...].T
        for c in range(0, width, block):
            cs = slice(c, c + block)
            mid_v[:, cs] = x_v[:, cs].astype(F32) + nn(heads_rows, wo_v[:, cs])
        normed = rms_scale(mid_v[...], gain_ref[...]).astype(BF16)
        n_v[...] = normed
        n_t[...] = normed.T
        for load in loads[3:]:
            load.wait()
        for c in range(0, hidden, block):
            cs = slice(c, c + block)
            gate_act, up_act = nn(n_v[...], wg_v[:, cs]), nn(n_v[...], wu_v[:, cs])
            hidden_grad = nt(cot_v[...], wd_v[cs, :])
            sigmoid = jax.nn.sigmoid(gate_act)
            silu = gate_act * sigmoid
            hidden_low = (silu * up_act).astype(BF16)
            hid_v[:, cs] = hidden_low
            hid_t[cs, :] = hidden_low.T
            gl_v[:, cs] = (hidden_grad * up_act * sigmoid * (1.0 + gate_act * (1.0 - sigmoid))).astype(BF16)
            ul_v[:, cs] = (hidden_grad * silu).astype(BF16)
        for c in range(0, width, block):
            cs = slice(c, c + block)
            grad = nt(gl_v[...], wg_v[cs, :]) + nt(ul_v[...], wu_v[cs, :])
            u_ref[:, :, cs] = grad.astype(BF16).reshape(S, rows, block)
        mid_sum = LineSum(u_ref, from_left, from_right, (u_sent, u_got), s, f, S)
        mid_sum.step(0)

        parity = lax.rem(f, 2)
        by_owner = (S, half, 2, cut, block)

        def exchange_halves(n, part, other):
            away = part.at[:, 1 - parity] if len(part.shape) == 4 else part.at[:, :, 1 - parity]
            send = copy(away, other, pair_sent.at[n], pair_got.at[n], pair(s, f))
            send.start()
            return send

        for c in range(0, hidden, block):
            cs = slice(c, c + block)
            gate_part[..., cs] = nn(n_t[...], gl_v[:, cs]).astype(BF16).reshape(by_owner)
        swaps = [exchange_halves(0, gate_part, gate_other)]
        for c in range(0, hidden, block):
            cs = slice(c, c + block)
            up_part[..., cs] = nn(n_t[...], ul_v[:, cs]).astype(BF16).reshape(by_owner)
        swaps.append(exchange_halves(1, up_part, up_other))
        for c in range(0, width, block):
            cs = slice(c, c + block)
            down_part[..., cs] = nn(hid_t[...], cot_v[:, cs]).astype(BF16).reshape(half, 2, down_rows, block)
        swaps.append(exchange_halves(2, down_part, down_other))
        for c in range(0, width, block):
            cs = slice(c, c + block)
            out_ref[:, :, cs] = nn(hid_v[...], wd_v[:, cs]).astype(BF16).reshape(S, rows, block)

        def spread(n, halves, got):
            here = pltpu.make_async_copy(halves.at[:, f // 2], got.at[f // 2], own_sem.at[n])
            here.start()
            sends = []
            for d, to in enumerate(same_parity(s, f)):
                send = copy(halves.at[:, to[1] // 2], got.at[f // 2], spread_sent.at[n, d], spread_got.at[n, d], to)
                send.start()
                sends.append(send)
            return here, sends

        def add(a, b):
            return (a.astype(F32) + b.astype(F32)).astype(BF16)

        swaps[0].wait_recv()
        gate_half[...] = add(gate_part[:, :, parity], gate_other[...])
        spreads = [spread(0, gate_half, gate_got)]
        mid_sum.step(1)
        swaps[1].wait_recv()
        up_half[...] = add(up_part[:, :, parity], up_other[...])
        spreads.append(spread(1, up_half, up_got))
        swaps[2].wait_recv()
        down_half[...] = add(down_part[:, parity], down_other[...])
        for time in range(2, S):
            mid_sum.step(time)

        middle = mid_v[pl.ds(pl.multiple_of(s * rows, rows), rows), :]
        grad = u_ref[s].astype(F32)
        inverse = lax.rsqrt(jnp.mean(middle * middle, axis=1, keepdims=True) + EPSILON)
        scaled = grad * gain_ref[...]
        mean = jnp.mean(scaled * middle, axis=1, keepdims=True)
        own_cot = cot_v[pl.ds(pl.multiple_of(s * rows, rows), rows), :].astype(F32)
        middle_grad = own_cot + inverse * scaled - middle * (inverse**3 * mean)
        middle_low = middle_grad.astype(BF16)
        hg_ref[...] = nt(wo_v[...], middle_low).astype(BF16).reshape(heads, dim, rows)

        place = grads_ref.at[f // splits, s]
        grads_here = pltpu.make_async_copy(hg_ref.at[s * own_heads + f // splits], place, own_sem.at[2])
        grads_here.start()
        sends = []
        for n, to in enumerate(like_parts(s, f)):
            send = copy(hg_ref.at[to[0] * own_heads + to[1] // splits], place, f_sent.at[n], f_got.at[n], to)
            send.start()
            sends.append(send)

        middle_ref[...] = middle
        mid_grad_ref[...] = middle_grad
        feed_ref[...] = jnp.sum(grad * middle * inverse, axis=0, keepdims=True)
        own_heads_t = h_v[:, pl.ds(pl.multiple_of(s * rows, rows), rows)]
        for c in range(0, width, block):
            cs = slice(c, c + block)
            output_part[..., cs] = nn(own_heads_t, middle_low[:, cs]).astype(BF16).reshape(by_owner)
        swaps.append(exchange_halves(3, output_part, output_other))
        swaps[3].wait_recv()
        output_half[...] = add(output_part[:, :, parity], output_other[...])
        grads_here.wait()
        for send in sends:
            send.wait()
        for here, others in spreads:
            here.wait()
            for send in others:
                send.wait()
        for swap in swaps:
            swap.wait_send()
        mid_sum.drain()

    dma = pltpu.SemaphoreType.DMA
    wide = (S, half, 2, cut, hidden)
    wide_half = (S, half, cut, hidden)
    grad_heads, own_middle, middle_grad, feed_gain, out_part, gate_got, up_got, down_half, output_half = pl.pallas_call(
        kernel_c,
        in_specs=[ANY] * 7 + [VMEM],
        out_specs=[ANY] + [VMEM] * 4 + [ANY] * 2 + [VMEM] * 2,
        out_shape=[
            shape((groups, S, dim, rows)),
            shape((rows, width), F32),
            shape((rows, width), F32),
            shape((1, width), F32),
            shape((S, rows, width)),
            shape((half, S, cut, hidden)),
            shape((half, S, cut, hidden)),
            shape((half, down_rows, width)),
            shape((S, half, cut, width)),
        ],
        scratch_shapes=[
            pltpu.VMEM((heads * dim, group), BF16),
            pltpu.VMEM((heads * dim, width), BF16),
            pltpu.VMEM((group, width), BF16),
            pltpu.VMEM((width, hidden), BF16),
            pltpu.VMEM((width, hidden), BF16),
            pltpu.VMEM((group, width), BF16),
            pltpu.VMEM((hidden, width), BF16),
            pltpu.VMEM((group, width), F32),
            pltpu.VMEM((group, width), BF16),
            pltpu.VMEM((width, group), BF16),
            pltpu.VMEM((group, hidden), BF16),
            pltpu.VMEM((hidden, group), BF16),
            pltpu.VMEM((group, hidden), BF16),
            pltpu.VMEM((group, hidden), BF16),
            *[pltpu.VMEM((S, rows, width), BF16)] * 3,
            *[pltpu.VMEM(wide, BF16)] * 2,
            pltpu.VMEM((half, 2, down_rows, width), BF16),
            pltpu.VMEM((S, half, 2, cut, width), BF16),
            *[pltpu.VMEM(wide_half, BF16)] * 2,
            pltpu.VMEM((half, down_rows, width), BF16),
            pltpu.VMEM((S, half, cut, width), BF16),
            *[pltpu.VMEM(wide_half, BF16)] * 2,
            pltpu.VMEM((heads, dim, rows), BF16),
            dma((7,)),
            *[dma((2, S))] * 2,
            *[dma((4,))] * 2,
            *[dma((2, half))] * 2,
            dma((3,)),
            *[dma((S * groups,))] * 2,
        ],
        compiler_params=pltpu.CompilerParams(
            collective_id=2, has_side_effects=True, vmem_limit_bytes=VMEM_BYTES
        ),
        cost_estimate=pl.CostEstimate(flops=10**10, bytes_accessed=10**8, transcendentals=10**6),
    )(
        heads_t,
        output_full,
        x_parts.reshape(group, width),
        gate_full,
        up_full,
        cot_parts.reshape(group, width),
        down_full,
        gain_feed[None, :],
    )

    def kernel_g(*refs):
        ins, sends, outs, gots = refs[:7], refs[7:10], refs[10:13], refs[13:16]
        sum_ref, send_sems, recv_sems, local_sems = refs[16:]
        s, f = lax.axis_index("seq"), lax.axis_index("fsdp")
        greet(along_seq(s, f) + same_parity(s, f))
        remote, local = seq_swap(s, f, sends[2], gots[2])
        for t in same_parity(s, f):
            remote.append((sends[0].at[:, t[1] // 2], gots[0].at[f // 2], t, None, None))
            remote.append((sends[1].at[t[1] // 2], gots[1].at[f // 2], t, None, None))
        local.append((sends[0].at[:, f // 2], gots[0].at[f // 2], None))
        local.append((sends[1].at[f // 2], gots[1].at[f // 2], None))
        finish = send_all((remote, local), send_sems, recv_sems, local_sems)
        backward_body(*ins, *outs, sum_ref)
        finish()

    copies = S - 1 + 2 * (half - 1)
    query_grad, kv_grad, bias_terms, output_got, down_got, out_terms = pl.pallas_call(
        kernel_g,
        in_specs=[VMEM] * 7 + [ANY] * 3,
        out_specs=[VMEM] * 3 + [ANY] * 3,
        out_shape=[
            shape((groups, dim, group)),
            shape((F, 2 * dim, group)),
            shape((2, VARIATES, QUERY_BLOCK), F32),
            shape((half, S, cut, width)),
            shape((half, down_rows, width)),
            shape((S, rows, width)),
        ],
        scratch_shapes=[
            pltpu.VMEM((F, 2 * dim, group), F32),
            dma((copies,)),
            dma((copies,)),
            dma((3,)),
        ],
        compiler_params=pltpu.CompilerParams(
            collective_id=3, has_side_effects=True, vmem_limit_bytes=VMEM_BYTES
        ),
    )(
        q_all,
        kv_all,
        query_marks,
        key_marks,
        grad_heads,
        attended,
        log_sum,
        output_half,
        down_half,
        out_part,
    )

    bias_sums = jnp.sum(bias_terms, axis=(1, 2))
    bias_pair = jnp.stack([bias_sums[0], bias_sums[1] - bias_sums[0]])
    bias_row = lax.dynamic_update_slice_in_dim(jnp.zeros((heads, 2), F32), bias_pair[None], head, 0)
    bias_row = jnp.pad(bias_row.reshape(1, 2 * heads), ((0, 0), (0, 128 - 2 * heads)))
    count = S * F
    chunks = width // 128

    def kernel_h(
        dq_ref, dkv_ref, gate_got, up_got, out_got, down_got, out_terms, middle_ref, mid_grad_ref, raw_ref, cos_ref,
        sin_ref, gain_q_ref, gain_k_ref, gain_ref, ws_ref, xs_ref, feed_ref, bias_ref,
        layer_ref, tokens_ref, attn_ref, output_ref, gate_ref, up_ref, down_ref, sums_ref,
        dqs, dkvs, gate_sum, up_sum, out_sum, gate_rows, up_rows, out_rows, down_sum, down_rows_ref, down_sent, down_arrived, pg_ref, u_ref, from_left, from_right,
        w_part, w_got, w_sum, w_rows, vec, vec_got,
        dq_sent, dq_got, dkv_sent, dkv_got, own_sem, swap_sent, swap_got, u_sent, u_got,
        w_sent, w_arrived, rows_sent, rows_got, vec_sent, vec_arrived,
    ):
        s, f = lax.axis_index("seq"), lax.axis_index("fsdp")
        own = f // splits

        def copy(src, dst, sent, got, to):
            return pltpu.make_async_remote_copy(
                src_ref=src, dst_ref=dst, send_sem=sent, recv_sem=got, device_id=to, device_id_type=MESH
            )

        greet(everyone(s, f))
        pending = []
        here = [
            pltpu.make_async_copy(dkv_ref.at[f], dkvs.at[f], own_sem.at[0]),
            pltpu.make_async_copy(dq_ref.at[own], dqs.at[own], own_sem.at[1]),
        ]
        for load in here:
            load.start()
        for d in range(1, F):
            to, source = lax.rem(f + d, F), lax.rem(f + F - d, F)
            if d % splits == 0:
                send = copy(dq_ref.at[to // splits], dqs.at[own], dq_sent.at[d // splits], dq_got.at[d // splits], (s, to))
                send.start()
                pending.append(send)
            send = copy(dkv_ref.at[to], dkvs.at[f], dkv_sent.at[d], dkv_got.at[d], (s, to))
            send.start()
            pending.append(send)

        swaps = []
        for n, (got, total, rows_ref) in enumerate(
            ((gate_got, gate_sum, gate_rows), (up_got, up_sum, up_rows), (out_got, out_sum, out_rows))
        ):
            total[...] = jnp.sum(got[...].astype(F32), axis=0).astype(BF16)
            rows_ref[s] = total[s]
            for d in range(1, S):
                to = lax.rem(s + d, S)
                send = copy(total.at[to], rows_ref.at[s], swap_sent.at[n, d], swap_got.at[n, d], (to, f))
                send.start()
                swaps.append(send)
        layer_ref[...] = (middle_ref[...] + jnp.sum(out_terms[...].astype(F32), axis=0)).astype(BF16)
        to_plane = lax.rem(lax.rem(f, S) - s + S, S)
        down_sum[...] = jnp.sum(down_got[...].astype(F32), axis=0).astype(BF16)
        down_move = copy(down_sum, down_rows_ref, down_sent, down_arrived, (to_plane, f))
        pl.when(to_plane != s)(down_move.start)

        for load in here:
            load.wait()
        for send in pending:
            send.wait_recv()

        cosine, sine = cos_ref[...], sin_ref[...]

        def prepare_back(grad, raw, gain):
            front, back = grad[: dim // 2], grad[dim // 2 :]
            grad = join(front * cosine + back * sine, back * cosine - front * sine)
            inverse = lax.rsqrt(jnp.mean(raw * raw, axis=0, keepdims=True) + EPSILON)
            scaled = grad * gain
            mean = jnp.mean(scaled * raw, axis=0, keepdims=True)
            return inverse * scaled - raw * (inverse**3 * mean), grad * raw * inverse

        def gain_row(terms):
            folded = terms[:, :128]
            for n in range(1, group // 128):
                folded = folded + terms[:, n * 128 : (n + 1) * 128]
            return jnp.sum(folded.T, axis=0, keepdims=True)

        gain_terms = [jnp.zeros((dim, group), F32), jnp.zeros((dim, group), F32)]
        for h in range(own_heads):
            kv_sum = dkvs[h * splits].astype(F32)
            for n in range(1, splits):
                kv_sum = kv_sum + dkvs[h * splits + n].astype(F32)
            kv_sum = kv_sum.astype(BF16).astype(F32)
            for n, (grad, gain) in enumerate(
                ((dqs[h].astype(F32), gain_q_ref[...]), (kv_sum[:dim], gain_k_ref[...]))
            ):
                back, terms = prepare_back(grad, raw_ref[n, h], gain)
                gain_terms[n] += terms
                pg_ref[:, pl.ds(n * lanes + h * dim, dim)] = back.T.astype(BF16)
            pg_ref[:, pl.ds(2 * lanes + h * dim, dim)] = kv_sum[dim:].T.astype(BF16)

        attn_gain = jnp.zeros((1, width), F32)
        for b in range(S):
            grad = nt(pg_ref[pl.ds(b * rows, rows), :], ws_ref[...])
            x = xs_ref[b].astype(F32)
            inverse = lax.rsqrt(jnp.mean(x * x, axis=1, keepdims=True) + EPSILON)
            attn_gain += jnp.sum(grad * x * inverse, axis=0, keepdims=True)
            u_ref[b] = grad.astype(BF16)

        normed_sum = LineSum(u_ref, from_left, from_right, (u_sent, u_got), s, f, S)
        normed_sum.step(0)

        gains = jnp.concatenate([gain_row(gain_terms[0]), gain_row(gain_terms[1])], axis=1)
        gains = jnp.concatenate([gains, jnp.zeros((1, 256 - 2 * dim), F32)], axis=1)[:, :128]
        for n in range(chunks):
            part = slice(n * 128, (n + 1) * 128)
            vec[n] = jnp.concatenate(
                [attn_gain[:, part], feed_ref[:, part], gains, bias_ref[...], jnp.zeros((4, 128), F32)]
            )
        me = s * F + f
        vec_got[me] = vec[me * cut // 128]
        small = []
        for a in range(S):
            for b in range(F):
                if a or b:
                    to = (lax.rem(s + a, S), lax.rem(f + b, F))
                    chunk = (to[0] * F + to[1]) * cut // 128
                    small.append(
                        copy(vec.at[chunk], vec_got.at[me], vec_sent.at[a * F + b], vec_arrived.at[a * F + b], to)
                    )
                    small[-1].start()

        for b in range(S):
            normed = rms_scale(xs_ref[b].astype(F32), gain_ref[...]).astype(BF16)
            u_terms = tn(normed, pg_ref[pl.ds(b * rows, rows), :])
            if b == 0:
                total = u_terms
            else:
                total = total + u_terms
        w_part[...] = total.astype(BF16).reshape(S, F, cut, 3 * lanes)
        w_got[f] = w_part[:, f]
        for d in range(1, F):
            to = lax.rem(f + d, F)
            send = copy(w_part.at[:, to], w_got.at[f], w_sent.at[d], w_arrived.at[d], (s, to))
            send.start()
            swaps.append(send)
        attn_sends = swaps[-(F - 1) :]
        for n in range(1, S - 1):
            normed_sum.step(n)
        for send in attn_sends:
            send.wait_recv()
        w_sum[...] = jnp.sum(w_got[...].astype(F32), axis=0).astype(BF16)
        w_rows[s] = w_sum[s]
        last = []
        for d in range(1, S):
            to = lax.rem(s + d, S)
            last.append(copy(w_sum.at[to], w_rows.at[s], rows_sent.at[d], rows_got.at[d], (to, f)))
            last[-1].start()

        for send in swaps[: 3 * (S - 1)]:
            send.wait_recv()
        for n in range(S):
            for g in range(F):
                holder = (g % S - n) % S * per_plane + g // S
                place = (holder * S + g % S) * down_rows
                part = slice(g * down_rows, (g + 1) * down_rows)
                gate_ref[:, place : place + down_rows] = gate_rows[n, :, part].astype(F32)
                up_ref[:, place : place + down_rows] = up_rows[n, :, part].astype(F32)
        output_ref[...] = jnp.sum(out_rows[...].astype(F32), axis=0)
        pl.when(to_plane != s)(down_move.wait)

        @pl.when(to_plane != s)
        def _():
            down_ref[...] = down_rows_ref[...].astype(F32)

        @pl.when(to_plane == s)
        def _():
            down_ref[...] = down_sum[...].astype(F32)

        for send in small:
            send.wait_recv()
        sums_ref[...] = jnp.sum(vec_got[...], axis=0)

        normed_sum.step(S - 1)
        grad = u_ref[s].astype(F32)
        x = xs_ref[s].astype(F32)
        inverse = lax.rsqrt(jnp.mean(x * x, axis=1, keepdims=True) + EPSILON)
        scaled = grad * gain_ref[...]
        mean = jnp.mean(scaled * x, axis=1, keepdims=True)
        tokens_ref[...] = mid_grad_ref[...] + inverse * scaled - x * (inverse**3 * mean)

        for send in last:
            send.wait_recv()
        for n in range(S):
            for part in range(3):
                place = part * S * lanes + n * lanes
                attn_ref[:, place : place + lanes] = w_rows[n][:, part * lanes : (part + 1) * lanes].astype(F32)
        normed_sum.drain()
        for send in pending + swaps + small + last:
            send.wait_send()

    layer_out, tokens_grad, attn_grad, output_grad, gate_grad, up_grad, down_grad, sums = pl.pallas_call(
        kernel_h,
        in_specs=[ANY] * 2 + [VMEM] * 17,
        out_specs=[VMEM] * 8,
        out_shape=[
            shape((rows, width)),
            shape((rows, width), F32),
            shape((cut, 3 * S * lanes), F32),
            shape((cut, width), F32),
            shape((cut, S * hidden), F32),
            shape((cut, S * hidden), F32),
            shape((down_rows, width), F32),
            shape((8, 128), F32),
        ],
        scratch_shapes=[
            pltpu.VMEM((own_heads, dim, group), BF16),
            pltpu.VMEM((F, 2 * dim, group), BF16),
            pltpu.VMEM((S, cut, hidden), BF16),
            pltpu.VMEM((S, cut, hidden), BF16),
            pltpu.VMEM((S, cut, width), BF16),
            pltpu.VMEM((S, cut, hidden), BF16),
            pltpu.VMEM((S, cut, hidden), BF16),
            pltpu.VMEM((S, cut, width), BF16),
            pltpu.VMEM((down_rows, width), BF16),
            pltpu.VMEM((down_rows, width), BF16),
            dma,
            dma,
            pltpu.VMEM((group, 3 * lanes), BF16),
            pltpu.VMEM((S, rows, width), BF16),
            pltpu.VMEM((S, rows, width), BF16),
            pltpu.VMEM((S, rows, width), BF16),
            pltpu.VMEM((S, F, cut, 3 * lanes), BF16),
            pltpu.VMEM((F, S, cut, 3 * lanes), BF16),
            pltpu.VMEM((S, cut, 3 * lanes), BF16),
            pltpu.VMEM((S, cut, 3 * lanes), BF16),
            pltpu.VMEM((chunks, 8, 128), F32),
            pltpu.VMEM((count, 8, 128), F32),
            *[dma((groups,))] * 2,
            *[dma((F,))] * 2,
            dma((2,)),
            *[dma((3, S))] * 2,
            *[dma((2, S))] * 2,
            *[dma((F,))] * 2,
            *[dma((S,))] * 2,
            *[dma((count,))] * 2,
        ],
        compiler_params=pltpu.CompilerParams(
            collective_id=4, has_side_effects=True, vmem_limit_bytes=VMEM_BYTES
        ),
    )(
        query_grad, kv_grad, gate_got, up_got, output_got, down_got, out_terms, own_middle, middle_grad, raw, cosine, sine,
        gain_query[:, None], gain_key[:, None], gain_attn[None, :], w_qkv, x_parts, feed_gain, bias_row,
    )
    place = lax.rem((s * F + f) * cut, 128)
    return (
        layer_out,
        tokens_grad,
        attn_grad,
        output_grad,
        gate_grad,
        up_grad,
        down_grad,
        lax.dynamic_slice_in_dim(sums[0], place, cut),
        lax.dynamic_slice_in_dim(sums[1], place, cut),
        sums[2, :dim],
        sums[2, dim : 2 * dim],
        sums[3, : 2 * heads].reshape(heads, 2),
    )


def solution(mesh):
    by_token, by_fsdp, by_owner = P(("fsdp", "seq"), None), P("fsdp", None), P(("seq", "fsdp"), None)
    in_specs = (
        by_token,
        by_token,
        P(),
        P(),
        P(),
        P(),
        by_fsdp,
        P(),
        P(),
        P(),
        by_fsdp,
        P(),
        by_fsdp,
        by_fsdp,
        by_fsdp,
    )
    out_specs = (
        (by_token, by_token) + (by_owner,) * 5 + (P(("seq", "fsdp")),) * 2 + (P(),) * 3
    )
    return jax.shard_map(
        per_device, mesh=mesh, in_specs=in_specs, out_specs=out_specs, check_vma=False
    )
```

```python
import functools

import jax
import jax.numpy as jnp
from jax import lax
from jax.experimental import pallas as pl
from jax.experimental.pallas import tpu as pltpu
from jax.sharding import PartitionSpec as P

EPSILON = 1e-06
F32, BF16 = jnp.float32, jnp.bfloat16
VARIATES = 8
AWAY = 1024.0
QUERY_BLOCK = 256
LSE_ROW, VAR_ROW = 32, 40
MESH = pl.DeviceIdType.MESH
ANY = pl.BlockSpec(memory_space=pl.ANY)
VMEM = pl.BlockSpec(memory_space=pltpu.VMEM)
VMEM_BYTES = 60 * 2**20


def nn(a, b):
    return jnp.dot(a, b, preferred_element_type=F32)


def nt(a, b):
    return lax.dot_general(a, b, (((1,), (1,)), ((), ())), preferred_element_type=F32)


def tn(a, b):
    return lax.dot_general(a, b, (((0,), (0,)), ((), ())), preferred_element_type=F32)


def pieces(values):
    high = values.astype(BF16).astype(F32)
    middle = (values - high).astype(BF16).astype(F32)
    return high, middle, (values - high - middle).astype(BF16).astype(F32)


def send_all(plan, send_sems, recv_sems, local_sems):
    remote, local = plan
    copies = []
    for n, (src, dst, device, may_send, may_receive) in enumerate(remote):
        copy = pltpu.make_async_remote_copy(
            src_ref=src,
            dst_ref=dst,
            send_sem=send_sems.at[n],
            recv_sem=recv_sems.at[n],
            device_id=device,
            device_id_type=MESH,
        )
        when(may_send, copy.start)
        copies.append((copy, may_send, may_receive))
    locals_ = []
    for n, (src, dst, may) in enumerate(local):
        copy = pltpu.make_async_copy(src, dst, local_sems.at[n])
        when(may, copy.start)
        locals_.append((copy, may))

    def finish():
        for copy, may in locals_:
            when(may, copy.wait)
        for copy, may_send, may_receive in copies:
            when(may_send, copy.wait_send)
            when(may_receive, copy.wait_recv)

    return finish


def when(condition, action):
    if condition is None:
        action()
    else:
        pl.when(condition)(action)


def greet(devices):
    barrier = pltpu.get_barrier_semaphore()
    for device in devices:
        pl.semaphore_signal(barrier, inc=1, device_id=device, device_id_type=MESH)
    pl.semaphore_wait(barrier, len(devices))


class Line:
    def __init__(self, block, sems, s, f, S):
        self.block, (self.sent, self.got) = block, sems
        self.s, self.f, self.S = s, f, S

    def hop(self, plane, slot, step):
        ref = self.block(plane, slot)
        return pltpu.make_async_remote_copy(
            src_ref=ref,
            dst_ref=ref,
            send_sem=self.sent.at[plane, slot, int(step > 0)],
            recv_sem=self.got.at[plane, slot],
            device_id=(self.s + step, self.f),
            device_id_type=MESH,
        )

    def each_hop(self, slot, distance, action):
        s, S = self.s, self.S
        pl.when((s - distance + 1) * (S - 1 - s) > 0)(
            lambda: action(self.hop(s - distance, slot, 1))
        )
        pl.when((S - s - distance) * s > 0)(lambda: action(self.hop(s + distance, slot, -1)))

    def send(self, slot):
        self.each_hop(slot, 0, lambda hop: hop.start())

    def arrive(self, slot, distance):
        s, S = self.s, self.S
        pl.when(s - distance >= 0)(lambda: self.hop(s - distance, slot, 1).wait_recv())
        pl.when(s + distance < S)(lambda: self.hop(s + distance, slot, -1).wait_recv())
        self.each_hop(slot, distance, lambda hop: hop.start())

    def drain(self, slot):
        for distance in range(self.S):
            self.each_hop(slot, distance, lambda hop: hop.wait_send())


def line_sems(S, slots):
    return [pltpu.SemaphoreType.DMA((S, slots, 2)), pltpu.SemaphoreType.DMA((S, slots))]


class LineSum:
    def __init__(self, terms, from_left, from_right, sems, s, f, S):
        self.terms, self.from_left, self.from_right = terms, from_left, from_right
        self.sent, self.got = sems
        self.s, self.f, self.S = s, f, S

    def hop(self, t, to_right):
        return pltpu.make_async_remote_copy(
            src_ref=self.terms.at[t],
            dst_ref=(self.from_left if to_right else self.from_right).at[t],
            send_sem=self.sent.at[int(to_right), t],
            recv_sem=self.got.at[int(to_right), t],
            device_id=(self.s + (1 if to_right else -1), self.f),
            device_id_type=MESH,
        )

    def take(self, t, to_right):
        self.hop(t, to_right).wait_recv()
        came = (self.from_left if to_right else self.from_right)[t]
        self.terms[t] = (self.terms[t].astype(F32) + came.astype(F32)).astype(BF16)

    def step(self, time, now=True):
        s, S = self.s, self.S
        n = time - s
        here = (n >= 0) & (S - 1 - n >= s) & now
        pl.when(here & (s >= 1))(lambda: self.take(S - 1 - n, True))
        pl.when(here & (S - 1 - n > s))(lambda: self.hop(S - 1 - n, True).start())
        m = time - (S - 1 - s)
        here = (m >= 0) & (m <= s) & now
        pl.when(here & (s < S - 1))(lambda: self.take(m, False))
        pl.when(here & (m < s))(lambda: self.hop(m, False).start())

    def drain(self):
        for t in range(self.S):
            pl.when(self.s < t)(lambda t=t: self.hop(t, True).wait_send())
            pl.when(self.s > t)(lambda t=t: self.hop(t, False).wait_send())


def flipped(f, bit):
    step = 2**bit
    return f + step - 2 * step * lax.rem(f // step, 2)


class CubeGather:
    def __init__(self, block, own, sems, s, f, F):
        self.block, self.own, (self.sent, self.shared, self.got) = block, own, sems
        self.s, self.f, self.F = s, f, F
        bits = list(range(1, F.bit_length() - 1))
        self.orders = (bits, bits[::-1])

    def copy(self, g, half, sem, to, own=False):
        ref = self.block(g, half)
        return pltpu.make_async_remote_copy(
            src_ref=self.own(half) if own else ref,
            dst_ref=ref,
            send_sem=sem,
            recv_sem=self.got.at[g, half],
            device_id=(self.s, to),
            device_id_type=MESH,
        )

    def held(self, half, rounds):
        masks = [((), 0)]
        for n, bit in enumerate(self.orders[half][:rounds]):
            masks += [(mask + (bit,), n + 1) for mask, _ in list(masks)]
        return masks

    def device(self, mask):
        g = self.f
        for bit in mask:
            g = flipped(g, bit)
        return g

    def sends(self, half, since):
        rounds = len(self.orders[half])
        out = []
        for place, (mask, came) in enumerate(self.held(half, rounds)):
            for n in range(came, rounds):
                if came == since:
                    out.append((n, place, mask))
        return out

    def send(self, half, n, place, mask):
        bit = self.orders[half][n]
        sem = self.sent.at[half, n, place]
        return self.copy(self.device(mask), half, sem, flipped(self.f, bit), not mask)

    def shares(self, half, since):
        return [
            self.copy(
                self.device(mask), half, self.shared.at[half, place], flipped(self.f, 0), not mask
            )
            for place, (mask, came) in enumerate(self.held(half, len(self.orders[half])))
            if came == since
        ]

    @property
    def rounds(self):
        return len(self.orders[0])

    def start(self):
        for half in range(2):
            self.send(half, 0, 0, ()).start()
        for half in range(2):
            self.shares(half, 0)[0].start()

    def step(self, number):
        for half in range(2):
            shares = self.shares(half, number)
            for share in shares:
                share.wait_recv()
            if number < self.rounds:
                for which in self.sends(half, number) + self.sends(half, 0)[number : number + 1]:
                    if which[0] == number or which[1]:
                        self.send(half, *which).start()
            for share in shares:
                share.start()

    def finish(self):
        for half in range(2):
            for place, (mask, _) in enumerate(self.held(half, self.rounds)):
                g = flipped(self.device(mask), 0)
                self.copy(g, half, self.shared.at[half, place], self.f).wait_recv()

    def drain(self):
        for half in range(2):
            for number in range(self.rounds + 1):
                for which in self.sends(half, number):
                    self.send(half, *which).wait_send()
                for share in self.shares(half, number):
                    share.wait_send()


def cube_sems(F):
    rounds = F.bit_length() - 2
    return [
        pltpu.SemaphoreType.DMA((2, rounds, F // 4)),
        pltpu.SemaphoreType.DMA((2, F // 2)),
        pltpu.SemaphoreType.DMA((F, 2)),
    ]


def shape(dims, dtype=BF16):
    return jax.ShapeDtypeStruct(tuple(dims), dtype)


def join(a, b):
    return jnp.concatenate([a, b], axis=0)


def side_by_side(ref, *index):
    return jnp.concatenate([ref[(*index, n)] for n in range(ref.shape[len(index)])], axis=1)


def forward_group(j, q_ref, kv_ref, qa_ref, ka_ref, att_ref, lse_ref, o_ref):
    width, rows = att_ref.shape[1:]
    span = q_ref.shape[-1]
    sub = QUERY_BLOCK // span

    def block(i, _):
        cols = pl.ds(pl.multiple_of(i * QUERY_BLOCK, QUERY_BLOCK), QUERY_BLOCK)
        q_t = jnp.concatenate([q_ref[j, i * sub + n] for n in range(sub)], axis=1)
        queries = join(q_t, qa_ref[j, :, cols]).T
        total = jnp.zeros((QUERY_BLOCK, 2 * width), F32)
        for g in range(kv_ref.shape[0]):
            kv = side_by_side(kv_ref, g)
            keys = join(kv[:width], ka_ref[g])
            values = join(kv[width:], jnp.ones((width, rows), BF16))
            weights = jnp.exp(nn(queries, keys)).astype(BF16)
            total += nt(weights, values)
        total = total.T
        weight_sum = total[width : width + 1]
        attended = total[:width] / weight_sum
        att_ref[j, :, cols] = attended
        o_ref[j, :, cols] = attended.astype(BF16)
        lse_ref[j, :, cols] = jnp.log(weight_sum)
        return 0

    lax.fori_loop(0, rows // QUERY_BLOCK, block, 0)


def with_rows(base, first, rows):
    index = lax.broadcasted_iota(jnp.int32, base.shape, 0)
    for n, row in enumerate(rows):
        base = jnp.where(index == first + n, row, base)
    return base


def rms_scale(vector, gain, axis=-1):
    return vector * lax.rsqrt(jnp.mean(vector * vector, axis=axis, keepdims=True) + EPSILON) * gain


def per_device(
    tokens,
    cotangent,
    doc_starts,
    variate_ids,
    time_ids,
    gain_attn,
    w_attn,
    gain_query,
    gain_key,
    variate_bias,
    w_output,
    gain_feed,
    w_gate,
    w_up,
    w_down,
):
    S, F = lax.axis_size("seq"), lax.axis_size("fsdp")
    s, f = lax.axis_index("seq"), lax.axis_index("fsdp")
    rows, width = tokens.shape
    heads = variate_bias.shape[0]
    dim = gain_query.shape[0]
    own_heads = heads // S
    splits = F // own_heads
    group = rows * S
    groups = F // splits
    hidden = w_down.shape[0] * F // S
    half = F // 2
    cut = width // (S * F)
    lanes = own_heads * dim

    def along_seq(s, f):
        return [(lax.rem(s + d, S), f) for d in range(1, S)]

    def along_fsdp(s, f):
        return [(s, lax.rem(f + d, F)) for d in range(1, F)]

    def along_both(s, f):
        return along_seq(s, f) + along_fsdp(s, f)

    def like_parts(s, f):
        return [
            (lax.rem(s + a, S), lax.rem(f + b * splits, F))
            for a in range(S)
            for b in range(groups)
            if a or b
        ]

    def everyone(s, f):
        return [(lax.rem(s + a, S), lax.rem(f + b, F)) for a in range(S) for b in range(F) if a or b]

    def seq_swap(s, f, src, dst):
        remote = [(src.at[t[0]], dst.at[s], t, None, None) for t in along_seq(s, f)]
        return remote, [(src.at[s], dst.at[s], None)]

    per_plane = F // S
    down_rows = w_down.shape[0] // S
    local_rows = w_attn.shape[0]
    whole_tiles = down_rows % 128 == 0

    def unit_place(s, f):
        return lax.rem(f, per_plane) * S + lax.rem(f // per_plane + s, S)

    def unit_block(s, g):
        holder = lax.rem(lax.rem(g, S) - s + S, S) * per_plane + g // S
        return holder * S + lax.rem(g, S)

    def units(w):
        if whole_tiles:
            return w
        blocks = w.reshape(w.shape[0], S * F, down_rows)
        return jnp.concatenate(
            [lax.dynamic_index_in_dim(blocks, unit_block(s, g), 1, False) for g in range(F)], axis=1
        )

    def pair(s, f):
        return (s, flipped(f, 0))

    def same_parity(s, f):
        return [(s, lax.rem(f + 2 * d, F)) for d in range(1, half)]

    def peers_a(s, f):
        return like_parts(s, f) + [(s, lax.rem(f + d, F)) for d in range(1, F) if d % splits]

    block = 256 if width % 256 == 0 and hidden % 256 == 0 else 128

    frequency = (10000.0 ** (-2.0 * jnp.arange(dim // 2, dtype=F32) / dim))[:, None]
    total = F * group

    def kernel_a(
        x_ref, cot_ref, w_ref, wo_ref, wd_ref, wg_ref, wu_ref, times_ref, ids_ref, freq_ref, gain_ref, gain_q_ref, gain_k_ref,
        gain_feed_ref, bias_ref, starts_ref,
        xs_out, ws_out, raw_out, cos_ref, sin_ref, ka_out, qa_out, qs_out, kvs_out, att_out, lse_ref,
        grads_ref, middle_ref, mid_grad_ref, feed_ref, out_ref, gate_got, up_got, down_half, output_half,
        xs_ref, ws_ref, raw_ref, cots_ref, ka_ref, qa_ref, q_ref, kv_ref, att_ref, heads_ref, wos_ref, gates_ref, ups_ref,
        downs_ref, mid_v, n_v, n_t, hid_v, hid_t, gl_v, ul_v, u_ref, from_left, from_right,
        gate_part, up_part, down_part, output_part, gate_other, up_other, down_other, output_other, gate_half, up_half,
        hg_ref, u_sent, u_got, pair_sent, pair_got, spread_sent, spread_got, own_sem, f_sent, f_got, out_sem,
        q_out, kv_out, o_ref, gate_own, up_own,
        w_sem, unit_sem, here_sem, x_sent, x_got, c_sent, c_got, kv_sent, kv_shared, kv_got, q_sent, q_got,
        o_sent, h_sent, h_got, *cube_refs,
    ):
        s, f = lax.axis_index("seq"), lax.axis_index("fsdp")
        column, part = f // splits, lax.rem(f, splits)
        loads = []
        for n in range(3):
            src = w_ref.at[:, pl.ds(pl.multiple_of(n * S * lanes + s * lanes, 128), lanes)]
            dst = ws_ref.at[pl.ds(f * local_rows, local_rows), pl.ds(n * lanes, lanes)]
            loads.append(pltpu.make_async_copy(src, dst, w_sem.at[n]))
        unit_loads = []
        for n, (src, dst) in enumerate(((wg_ref, gate_own), (wu_ref, up_own))):
            for g in range(F if whole_tiles else 1):
                if whole_tiles:
                    cols = pl.ds(pl.multiple_of(unit_block(s, g) * down_rows, 128), down_rows)
                    src_, dst_ = src.at[:, cols], dst.at[:, pl.ds(g * down_rows, down_rows)]
                else:
                    src_, dst_ = src, dst
                unit_loads.append(pltpu.make_async_copy(src_, dst_, unit_sem.at[n, g]))
        for load in loads + unit_loads:
            load.start()
        xs_ref[s] = x_ref[...]
        cots_ref[s] = cot_ref[...]
        greet(peers_a(s, f))
        xs = Line(lambda plane, slot: xs_ref.at[plane], (x_sent, x_got), s, f, S)
        cots = Line(lambda plane, slot: cots_ref.at[plane], (c_sent, c_got), s, f, S)
        xs.send(0)

        def rows_of(ref, size, place=lambda g: g):
            return lambda g, half: ref.at[pl.ds(place(g) * size + half * (size // 2), size // 2)]

        def half_of(ref, size):
            return lambda half: ref.at[pl.ds(half * (size // 2), size // 2)]

        down_own = wd_ref.at[lax.rem(f // per_plane + s, S)]
        down_place = unit_place(s, f)
        blocks = (
            (rows_of(ws_ref, local_rows), lambda half: rows_of(ws_ref, local_rows)(f, half)),
            (rows_of(wos_ref, local_rows), half_of(wo_ref, local_rows)),
            (rows_of(gates_ref, local_rows), half_of(gate_own, local_rows)),
            (rows_of(ups_ref, local_rows), half_of(up_own, local_rows)),
            (rows_of(downs_ref, down_rows, lambda g: unit_place(s, g)), half_of(down_own, down_rows)),
        )
        ws, wos, gates, ups, downs = [
            CubeGather(block, own, cube_refs[3 * n : 3 * n + 3], s, f, F) for n, (block, own) in enumerate(blocks)
        ]
        for load in loads:
            load.wait()
        ws.start()
        for load in unit_loads:
            load.wait()
        mine = pl.ds(f * local_rows, local_rows)
        here = [
            pltpu.make_async_copy(wo_ref, wos_ref.at[mine], here_sem.at[0]),
            pltpu.make_async_copy(gate_own, gates_ref.at[mine], here_sem.at[1]),
            pltpu.make_async_copy(up_own, ups_ref.at[mine], here_sem.at[2]),
            pltpu.make_async_copy(down_own, downs_ref.at[pl.ds(down_place * down_rows, down_rows)], here_sem.at[3]),
        ]
        for copy in here:
            copy.start()

        own_cols = pl.ds(pl.multiple_of(f * group, 128), group)
        angles = freq_ref[...] * times_ref[:, own_cols].astype(F32)
        cos_ref[...] = jnp.cos(angles)
        sin_ref[...] = jnp.sin(angles)
        mine_only = lax.broadcasted_iota(jnp.int32, (2, heads), 1) == s * own_heads + column
        biases = jnp.sum(jnp.where(mine_only, bias_ref[...], 0.0), axis=1, keepdims=True)
        difference = pieces(jnp.broadcast_to(biases[0:1] - biases[1:2], (VARIATES, group)))
        index = lax.broadcasted_iota(jnp.int32, (VARIATES, group), 0)

        def marks(g):
            ids = ids_ref[:, pl.ds(pl.multiple_of(g * group, 128), group)]
            positions = g * group + lax.broadcasted_iota(jnp.int32, (VARIATES, group), 1)
            docs = jnp.zeros((VARIATES, group), jnp.int32) - 1
            for n in range(doc_starts.shape[0]):
                docs = docs + (starts_ref[n] <= positions).astype(jnp.int32)
            return (docs == index).astype(F32), (ids == index).astype(F32)

        for g in range(F):
            doc, var = marks(g)
            tail = (index < 3).astype(F32)
            none = jnp.zeros((dim - LSE_ROW - VARIATES, group), F32)
            ka_ref[g] = jnp.concatenate([var, var, var, 1.0 - doc, tail, none]).astype(BF16)
        for j in range(groups):
            doc, var = marks(j * splits + part)
            none = jnp.zeros((VARIATES, group), F32)
            rest = jnp.zeros((dim - VAR_ROW - VARIATES, group), F32)
            scaled = [var * piece for piece in difference]
            qa_ref[j] = jnp.concatenate([*scaled, doc * -AWAY, none, var, rest]).astype(BF16)
        gain_q, gain_k = [
            jnp.broadcast_to(ref[...], (128, dim)).T[:, :rows] for ref in (gain_q_ref, gain_k_ref)
        ]

        def kv_copy(g, b, src, sem, to):
            return pltpu.make_async_remote_copy(
                src_ref=src, dst_ref=kv_ref.at[g, b], send_sem=sem, recv_sem=kv_got.at[g, b],
                device_id=(s, to), device_id_type=MESH,
            )

        def to_heads(b, d):
            to = lax.rem(f + 2 * d, F)
            return kv_copy(f, b, kv_out.at[b, to // splits], kv_sent.at[b, d], to)

        def to_neighbour(b, d):
            g = lax.rem(f + 2 * d, F)
            src = kv_ref.at[g, b] if d else kv_out.at[b, column]
            return kv_copy(g, b, src, kv_shared.at[b, d], flipped(f, 0))

        def queries_to_heads(b, d):
            to = lax.rem(f + d * splits, F)
            return pltpu.make_async_remote_copy(
                src_ref=q_out.at[b, to // splits], dst_ref=q_ref.at[column, b], send_sem=q_sent.at[b, d],
                recv_sem=q_got.at[column, b], device_id=(s, to), device_id_type=MESH,
            )

        def project(b):
            normed = rms_scale(xs_ref[b].astype(F32), gain_ref[...]).astype(BF16)
            projected = nn(normed, ws_ref[...]).T.reshape(3, own_heads, dim, rows)
            cols = pl.ds(pl.multiple_of(b * rows, rows), rows)
            cosine, sine = cos_ref[:, cols], sin_ref[:, cols]

            def turned(raw, gain):
                raw = rms_scale(raw, gain, axis=1)
                front, back = raw[:, : dim // 2], raw[:, dim // 2 :]
                return jnp.concatenate(
                    [front * cosine - back * sine, front * sine + back * cosine], axis=1
                )

            raw_ref[0, :, :, cols] = projected[0]
            raw_ref[1, :, :, cols] = projected[1]
            q_out[b] = (turned(projected[0], gain_q).astype(BF16).astype(F32) * dim**-0.5).astype(BF16)
            kv_out[b, :, :dim] = turned(projected[1], gain_k).astype(BF16)
            kv_out[b, :, dim:] = projected[2].astype(BF16)
            for d in range(1, half):
                to_heads(b, d).start()
            for d in range(1, groups):
                queries_to_heads(b, d).start()
            to_neighbour(b, 0).start()
            kv_ref[f, b] = kv_out[b, column]
            q_ref[column, b] = q_out[b, column]

        def share(b):
            for d in range(1, half):
                to_neighbour(b, d).wait_recv()
                to_neighbour(b, d).start()

        for number in range(1, ws.rounds + 1):
            ws.step(number)
        wos.start()
        ws.finish()
        project(s)
        for distance in range(1, S):
            xs.arrive(0, distance)
            if distance == S - 1:
                cots.send(0)
            pl.when(s - distance >= 0)(lambda distance=distance: project(s - distance))
            pl.when(s + distance < S)(lambda distance=distance: project(s + distance))
            if distance == S - 2:
                wos.step(1)

        def share_all(b, _):
            share(b)
            return 0

        lax.fori_loop(0, S, share_all, 0)
        gates.start()

        def last(b, _):
            for d in range(half):
                g = lax.rem(flipped(f, 0) + 2 * d, F)
                kv_copy(g, b, kv_ref.at[g, b], kv_shared.at[b, d], f).wait_recv()
            for d in range(1, groups):
                g = lax.rem(f + d * splits, F)
                pltpu.make_async_remote_copy(
                    src_ref=q_out.at[b, 0], dst_ref=q_ref.at[g // splits, b], send_sem=q_sent.at[b, d],
                    recv_sem=q_got.at[g // splits, b], device_id=(s, g), device_id_type=MESH,
                ).wait_recv()
            return 0

        lax.fori_loop(0, S, last, 0)
        ups.start()
        downs.start()

        own = s * own_heads + column

        def to_column(turn):
            j = lax.rem(column + turn, groups)
            return pltpu.make_async_remote_copy(
                src_ref=o_ref.at[j], dst_ref=heads_ref.at[own], send_sem=o_sent.at[turn], recv_sem=h_got.at[turn, 0],
                device_id=(s, j * splits + part), device_id_type=MESH,
            )

        def along(turn, d):
            ref = heads_ref.at[s * own_heads + lax.rem(column - turn + groups, groups)]
            return pltpu.make_async_remote_copy(
                src_ref=ref, dst_ref=ref, send_sem=h_sent.at[turn, d], recv_sem=h_got.at[turn, d],
                device_id=(lax.rem(s + d, S), f), device_id_type=MESH,
            )

        for turn in range(groups + 1):
            if turn < groups:
                j = lax.rem(column + turn, groups)
                forward_group(j, q_ref, kv_ref, qa_ref, ka_ref, att_ref, lse_ref, o_ref)
                if turn:
                    to_column(turn).start()
                else:
                    heads_ref[own] = o_ref[j]
            if turn != 1:
                came = max(turn - 1, 0)
                if came:
                    to_column(came).wait_recv()
                for d in range(1, S):
                    along(came, d).start()
            if turn + 1 < S:
                cots.arrive(0, turn + 1)
            if turn == 0:
                gates.step(1)
            if turn == 2:
                for number in range(2, wos.rounds + 1):
                    wos.step(number)
                    gates.step(number)
            if turn == 3:
                ups.step(1)
                downs.step(1)
        for distance in range(groups + 2, S):
            cots.arrive(0, distance)
        for number in range(2, ups.rounds + 1):
            ups.step(number)
            downs.step(number)

        flushes = [
            pltpu.make_async_copy(src, dst, out_sem.at[n])
            for n, (src, dst) in enumerate(
                (
                    (xs_ref, xs_out), (ws_ref, ws_out), (raw_ref, raw_out), (ka_ref, ka_out), (qa_ref, qa_out),
                    (q_ref, qs_out), (kv_ref, kvs_out), (att_ref, att_out),
                )
            )
        ]
        for flush in flushes:
            flush.start()
        for turn in range(groups):
            for d in range(1, S):
                along(turn, d).wait_recv()
        for copy_ in here:
            copy_.wait()
        wos.finish()

        def copy(src, dst, sent, got, to):
            return pltpu.make_async_remote_copy(
                src_ref=src, dst_ref=dst, send_sem=sent, recv_sem=got, device_id=to, device_id_type=MESH
            )

        heads_rows = heads_ref[...].reshape(heads * dim, group).T
        for c in range(0, width, block):
            cs = slice(c, c + block)
            mid_v[:, cs] = xs_ref[:, :, cs].astype(F32).reshape(group, block) + nn(heads_rows, wos_ref[:, cs])
        normed = rms_scale(mid_v[...], gain_feed_ref[...]).astype(BF16)
        n_v[...] = normed
        n_t[...] = normed.T
        for gather in (gates, ups, downs):
            gather.finish()
        cot_rows = cots_ref[...].reshape(group, width)
        for c in range(0, hidden, block):
            cs = slice(c, c + block)
            gate_act, up_act = nn(n_v[...], gates_ref[:, cs]), nn(n_v[...], ups_ref[:, cs])
            hidden_grad = nt(cot_rows, downs_ref[cs, :])
            sigmoid = jax.nn.sigmoid(gate_act)
            silu = gate_act * sigmoid
            hidden_low = (silu * up_act).astype(BF16)
            hid_v[:, cs] = hidden_low
            hid_t[cs, :] = hidden_low.T
            gl_v[:, cs] = (hidden_grad * up_act * sigmoid * (1.0 + gate_act * (1.0 - sigmoid))).astype(BF16)
            ul_v[:, cs] = (hidden_grad * silu).astype(BF16)
        for c in range(0, width, block):
            cs = slice(c, c + block)
            grad = nt(gl_v[...], gates_ref[cs, :]) + nt(ul_v[...], ups_ref[cs, :])
            u_ref[:, :, cs] = grad.astype(BF16).reshape(S, rows, block)
        mid_sum = LineSum(u_ref, from_left, from_right, (u_sent, u_got), s, f, S)
        mid_sum.step(0)

        parity = lax.rem(f, 2)
        by_owner = (S, half, 2, cut, block)

        def exchange_halves(n, part, other):
            away = part.at[:, 1 - parity] if len(part.shape) == 4 else part.at[:, :, 1 - parity]
            send = copy(away, other, pair_sent.at[n], pair_got.at[n], pair(s, f))
            send.start()
            return send

        for c in range(0, hidden, block):
            cs = slice(c, c + block)
            gate_part[..., cs] = nn(n_t[...], gl_v[:, cs]).astype(BF16).reshape(by_owner)
        swaps = [exchange_halves(0, gate_part, gate_other)]
        for c in range(0, hidden, block):
            cs = slice(c, c + block)
            up_part[..., cs] = nn(n_t[...], ul_v[:, cs]).astype(BF16).reshape(by_owner)
        swaps.append(exchange_halves(1, up_part, up_other))
        for c in range(0, width, block):
            cs = slice(c, c + block)
            down_part[..., cs] = nn(hid_t[...], cots_ref[:, :, cs].reshape(group, block)).astype(BF16).reshape(half, 2, down_rows, block)
        swaps.append(exchange_halves(2, down_part, down_other))
        for c in range(0, width, block):
            cs = slice(c, c + block)
            out_ref[:, :, cs] = nn(hid_v[...], downs_ref[:, cs]).astype(BF16).reshape(S, rows, block)

        def spread(n, halves, got):
            here = pltpu.make_async_copy(halves.at[:, f // 2], got.at[f // 2], own_sem.at[n])
            here.start()
            sends = []
            for d, to in enumerate(same_parity(s, f)):
                send = copy(halves.at[:, to[1] // 2], got.at[f // 2], spread_sent.at[n, d], spread_got.at[n, d], to)
                send.start()
                sends.append(send)
            return here, sends

        def add(a, b):
            return (a.astype(F32) + b.astype(F32)).astype(BF16)

        swaps[0].wait_recv()
        gate_half[...] = add(gate_part[:, :, parity], gate_other[...])
        spreads = [spread(0, gate_half, gate_got)]
        mid_sum.step(1)
        swaps[1].wait_recv()
        up_half[...] = add(up_part[:, :, parity], up_other[...])
        spreads.append(spread(1, up_half, up_got))
        swaps[2].wait_recv()
        down_half[...] = add(down_part[:, parity], down_other[...])
        for time in range(2, S):
            mid_sum.step(time)

        middle = mid_v[pl.ds(pl.multiple_of(s * rows, rows), rows), :]
        grad = u_ref[s].astype(F32)
        inverse = lax.rsqrt(jnp.mean(middle * middle, axis=1, keepdims=True) + EPSILON)
        scaled = grad * gain_feed_ref[...]
        mean = jnp.mean(scaled * middle, axis=1, keepdims=True)
        own_cot = cots_ref[s].astype(F32)
        middle_grad = own_cot + inverse * scaled - middle * (inverse**3 * mean)
        middle_low = middle_grad.astype(BF16)
        hg_ref[...] = nt(wos_ref[...], middle_low).astype(BF16).reshape(heads, dim, rows)

        place = grads_ref.at[f // splits, s]
        grads_here = pltpu.make_async_copy(hg_ref.at[s * own_heads + f // splits], place, own_sem.at[2])
        grads_here.start()
        sends = []
        for n, to in enumerate(like_parts(s, f)):
            send = copy(hg_ref.at[to[0] * own_heads + to[1] // splits], place, f_sent.at[n], f_got.at[n], to)
            send.start()
            sends.append(send)

        middle_ref[...] = middle
        mid_grad_ref[...] = middle_grad
        feed_ref[...] = jnp.sum(grad * middle * inverse, axis=0, keepdims=True)
        own_heads_t = heads_ref[:, :, pl.ds(pl.multiple_of(s * rows, rows), rows)].reshape(heads * dim, rows)
        for c in range(0, width, block):
            cs = slice(c, c + block)
            output_part[..., cs] = nn(own_heads_t, middle_low[:, cs]).astype(BF16).reshape(by_owner)
        swaps.append(exchange_halves(3, output_part, output_other))
        swaps[3].wait_recv()
        output_half[...] = add(output_part[:, :, parity], output_other[...])
        grads_here.wait()
        for send in sends:
            send.wait()
        for here, others in spreads:
            here.wait()
            for send in others:
                send.wait()
        for swap in swaps:
            swap.wait_send()
        mid_sum.drain()

        for flush in flushes:
            flush.wait()
        def sent(b, _):
            for d in range(half):
                if d:
                    to_heads(b, d).wait_send()
                to_neighbour(b, d).wait_send()
            for d in range(1, groups):
                queries_to_heads(b, d).wait_send()
            return 0

        lax.fori_loop(0, S, sent, 0)
        xs.drain(0)
        cots.drain(0)
        ws.drain()
        for turn in range(groups):
            if turn:
                to_column(turn).wait_send()
            for d in range(1, S):
                along(turn, d).wait_send()
        for gather in (wos, gates, ups, downs):
            gather.drain()

    dma = pltpu.SemaphoreType.DMA
    wide = (S, half, 2, cut, hidden)
    wide_half = (S, half, cut, hidden)
    kept = [
        shape((S, rows, width)),
        shape((width, 3 * lanes)),
        shape((2, own_heads, dim, group), F32),
        shape((F, dim, group)),
        shape((groups, dim, group)),
        shape((groups, S, dim, rows)),
        shape((F, S, 2 * dim, rows)),
        shape((groups, dim, group), F32),
    ]
    (
        x_parts, w_qkv, raw, cosine, sine, key_marks, query_marks, q_all, kv_all, attended, log_sum,
        grad_heads, own_middle, middle_grad, feed_gain, out_part, gate_got, up_got, down_half, output_half,
    ) = pl.pallas_call(
        kernel_a,
        in_specs=[VMEM] * 2 + [ANY] * 5 + [VMEM] * 8 + [pl.BlockSpec(memory_space=pltpu.SMEM)],
        out_specs=[ANY] * 3 + [VMEM] * 2 + [ANY] * 5 + [VMEM] + [ANY] + [VMEM] * 4 + [ANY] * 2 + [VMEM] * 2,
        out_shape=[
            *kept[:3],
            shape((dim // 2, group), F32),
            shape((dim // 2, group), F32),
            *kept[3:],
            shape((groups, 1, group), F32),
            shape((groups, S, dim, rows)),
            shape((rows, width), F32),
            shape((rows, width), F32),
            shape((1, width), F32),
            shape((S, rows, width)),
            shape((half, S, cut, hidden)),
            shape((half, S, cut, hidden)),
            shape((half, down_rows, width)),
            shape((S, half, cut, width)),
        ],
        scratch_shapes=[
            *[pltpu.VMEM(kept[n].shape, kept[n].dtype) for n in range(3)],
            pltpu.VMEM((S, rows, width), BF16),
            *[pltpu.VMEM(one.shape, one.dtype) for one in kept[3:]],
            pltpu.VMEM((heads, dim, group), BF16),
            pltpu.VMEM((heads * dim, width), BF16),
            pltpu.VMEM((width, hidden), BF16),
            pltpu.VMEM((width, hidden), BF16),
            pltpu.VMEM((hidden, width), BF16),
            pltpu.VMEM((group, width), F32),
            pltpu.VMEM((group, width), BF16),
            pltpu.VMEM((width, group), BF16),
            pltpu.VMEM((group, hidden), BF16),
            pltpu.VMEM((hidden, group), BF16),
            pltpu.VMEM((group, hidden), BF16),
            pltpu.VMEM((group, hidden), BF16),
            *[pltpu.VMEM((S, rows, width), BF16)] * 3,
            *[pltpu.VMEM(wide, BF16)] * 2,
            pltpu.VMEM((half, 2, down_rows, width), BF16),
            pltpu.VMEM((S, half, 2, cut, width), BF16),
            *[pltpu.VMEM(wide_half, BF16)] * 2,
            pltpu.VMEM((half, down_rows, width), BF16),
            pltpu.VMEM((S, half, cut, width), BF16),
            *[pltpu.VMEM(wide_half, BF16)] * 2,
            pltpu.VMEM((heads, dim, rows), BF16),
            *[dma((2, S))] * 2,
            *[dma((4,))] * 2,
            *[dma((2, half))] * 2,
            dma((3,)),
            *[dma((S * groups,))] * 2,
            dma((len(kept),)),
            pltpu.VMEM((S, own_heads, dim, rows), BF16),
            pltpu.VMEM((S, own_heads, 2 * dim, rows), BF16),
            pltpu.VMEM((groups, dim, group), BF16),
            pltpu.VMEM((local_rows, hidden), BF16),
            pltpu.VMEM((local_rows, hidden), BF16),
            dma((3,)),
            dma((2, F)),
            dma((4,)),
            *line_sems(S, 1),
            *line_sems(S, 1),
            dma((S, half)),
            dma((S, half)),
            dma((F, S)),
            dma((S, groups)),
            dma((groups, S)),
            dma((groups,)),
            dma((groups, S)),
            dma((groups, S)),
            *[sem for _ in range(5) for sem in cube_sems(F)],
        ],
        compiler_params=pltpu.CompilerParams(
            collective_id=0, has_side_effects=True, vmem_limit_bytes=VMEM_BYTES
        ),
        cost_estimate=pl.CostEstimate(flops=2 * 10**10, bytes_accessed=10**8, transcendentals=10**7),
    )(
        tokens,
        cotangent,
        w_attn,
        w_output,
        w_down.reshape(S, down_rows, width),
        units(w_gate),
        units(w_up),
        time_ids[None, :],
        variate_ids[None, :],
        frequency,
        gain_attn[None, :],
        gain_query[None, :],
        gain_key[None, :],
        gain_feed[None, :],
        variate_bias.T,
        doc_starts,
    )

    count = S * F
    chunks = width // 128
    blocks = group // QUERY_BLOCK
    span = QUERY_BLOCK // rows
    small_rows = 8

    def kernel_g(
        q_ref, kv_ref, qa_ref, ka_ref, do_ref, att_ref, lse_ref, cos_ref, sin_ref, gain_q_ref, gain_k_ref, feed_ref,
        gain_ref, out_half, down_half, out_hbm, gate_hbm, up_hbm, raw_hbm, ws_hbm, xs_hbm,
        u_own, w_rows, gate_rows, up_rows, out_rows, down_moved, layer_own, vec_got,
        out_got, down_got, gate_got, up_got,
        qq_ref, dd_ref, dq_sum, kv_sum, kv_send, kv_other, dq_send, dqs, dkvs, gate_sum, up_sum, out_sum, down_sum,
        layer_ref, layer_left, layer_right, raw_ref, ws_ref, xs_ref, pg_ref, u_ref, from_left, from_right, w_part, w_got,
        w_sum, vec, bias_ref,
        load_sem, own_sem, spread_sent, spread_got, layer_sent, layer_got, swap_sent, swap_got, pair_sent, pair_got,
        dkv_sent, dkv_got, dq_sent, dq_got, u_sent, u_got, w_sent, w_arrived, rows_sent, rows_got, vec_sent, vec_arrived,
        down_sent, down_arrived,
    ):
        s, f = lax.axis_index("seq"), lax.axis_index("fsdp")
        column, part, parity = f // splits, lax.rem(f, splits), lax.rem(f, 2)

        def copy(src, dst, sent, got, to):
            return pltpu.make_async_remote_copy(
                src_ref=src, dst_ref=dst, send_sem=sent, recv_sem=got, device_id=to, device_id_type=MESH
            )

        loads = [
            pltpu.make_async_copy(src, dst, load_sem.at[n])
            for n, (src, dst) in enumerate(
                (
                    (out_hbm, layer_ref), (gate_hbm, gate_got), (up_hbm, up_got), (raw_hbm, raw_ref), (ws_hbm, ws_ref),
                    (xs_hbm, xs_ref),
                )
            )
        ]
        for load in loads:
            load.start()
        greet(everyone(s, f))

        spreads = []
        for n, (src, got) in enumerate(((out_half, out_got), (down_half, down_got))):
            pick = (lambda ref, g: ref.at[:, g]) if n == 0 else (lambda ref, g: ref.at[g])
            here = pltpu.make_async_copy(pick(src, f // 2), got.at[f // 2], own_sem.at[n])
            here.start()
            sends = []
            for d, to in enumerate(same_parity(s, f)):
                sends.append(copy(pick(src, to[1] // 2), got.at[f // 2], spread_sent.at[n, d], spread_got.at[n, d], to))
                sends[-1].start()
            spreads.append((here, sends))
        layer = LineSum(layer_ref, layer_left, layer_right, (layer_sent, layer_got), s, f, S)
        loads[0].wait()
        layer.step(0)
        swaps = []

        def swap_rows(n, got, total, rows_ref):
            total[...] = jnp.sum(got[...].astype(F32), axis=0).astype(BF16)
            rows_ref[s] = total[s]
            for d in range(1, S):
                to = lax.rem(s + d, S)
                swaps.append(copy(total.at[to], rows_ref.at[s], swap_sent.at[n, d], swap_got.at[n, d], (to, f)))
                swaps[-1].start()

        def rows_at(i):
            return pl.ds(pl.multiple_of(i * QUERY_BLOCK, QUERY_BLOCK), QUERY_BLOCK)

        def tokens_of(ref, i):
            j, first = i // blocks, (i % blocks) * span
            return jnp.concatenate([ref[j, first + n] for n in range(span)], axis=1)

        def ready(i, _):
            j, cols = i // blocks, rows_at(i % blocks)
            marks = qa_ref[j, :, cols].astype(F32)
            extra = with_rows(marks, LSE_ROW, pieces(-lse_ref[j, :, cols])).astype(BF16)
            qq_ref[rows_at(i), :] = join(tokens_of(q_ref, i), extra).T
            grad_t = tokens_of(do_ref, i)
            delta = jnp.sum(grad_t.astype(F32) * att_ref[j, :, cols], axis=0, keepdims=True)
            extra = with_rows(jnp.zeros((dim, QUERY_BLOCK), F32), 0, pieces(-delta)).astype(BF16)
            dd_ref[rows_at(i), :] = join(grad_t, extra).T
            return 0

        lax.fori_loop(0, groups * blocks, ready, 0)
        for load in loads[1:3]:
            load.wait()
        swap_rows(0, gate_got, gate_sum, gate_rows)
        swap_rows(1, up_got, up_sum, up_rows)
        dq_sum[...] = jnp.zeros_like(dq_sum)

        def key_group(g):
            kv = side_by_side(kv_ref, g)
            keys = join(kv[:dim], ka_ref[g])
            values = join(kv[dim:], jnp.ones((dim, group), BF16))
            kv_sum[...] = jnp.zeros_like(kv_sum)
            for i in range(groups * blocks):
                q_rows = slice(i * QUERY_BLOCK, (i + 1) * QUERY_BLOCK)
                probs = jnp.exp(nn(qq_ref[q_rows, :], keys))
                score_grad = (probs * nn(dd_ref[q_rows, :], values)).astype(BF16)
                kv_sum[dim:, :] += nn(tokens_of(do_ref, i), probs.astype(BF16))
                kv_sum[:dim, :] += nn(tokens_of(q_ref, i), score_grad)
                dq_sum[q_rows, :] += nt(score_grad, keys)

        def to_pair(i):
            return copy(kv_send.at[0, i], kv_other.at[i], pair_sent.at[i], pair_got.at[i], (s, flipped(f, 0)))

        def to_owner(i):
            to = lax.rem(f + 2 * (i + 1), F)
            return copy(kv_send.at[1, i], dkvs.at[f // 2], dkv_sent.at[i], dkv_got.at[i], (s, to))

        def others(i, _):
            key_group(lax.rem(flipped(f, 0) + 2 * (i + 1), F))
            kv_send[0, i] = kv_sum[...].astype(BF16)
            to_pair(i).start()
            return 0

        lax.fori_loop(0, half, others, 0)
        layer.step(1)
        here, sends = spreads[0]
        here.wait()
        for send in sends:
            send.wait_recv()
        swap_rows(2, out_got, out_sum, out_rows)

        def owns(i, _):
            key_group(lax.rem(f + 2 * (i + 1), F))
            to_pair(i).wait_recv()
            kv_send[1, i] = (kv_sum[...] + kv_other[i].astype(F32)).astype(BF16)
            pl.when(i < half - 1)(lambda: to_owner(i).start())
            layer.step(2 + i // 2, lax.rem(i, 2) == 1)
            return 0

        lax.fori_loop(0, half, owns, 0)
        dkvs[f // 2] = kv_send[1, half - 1]
        for time in range(2 + half // 2, S):
            layer.step(time)

        bias_ref[...] = jnp.zeros_like(bias_ref)

        def dq_copy(d):
            to = lax.rem(f + d * splits, F)
            return copy(dq_send.at[to // splits], dqs.at[column], dq_sent.at[d], dq_got.at[d], (s, to))

        def queries_done(i, _):
            j, cols = i // blocks, rows_at(i % blocks)
            dq_t = dq_sum[rows_at(i), :].T
            dq_send[j, :, cols] = (dq_t[:dim] * dim**-0.5).astype(BF16)
            by_variate = dq_t[dim : dim + VARIATES]
            bias_ref[0] += by_variate * qa_ref[j, VAR_ROW : VAR_ROW + VARIATES, cols].astype(F32)
            bias_ref[1] += by_variate
            return 0

        lax.fori_loop(0, groups * blocks, queries_done, 0)
        for d in range(1, groups):
            dq_copy(d).start()
        dqs[column] = dq_send[column]
        here, sends = spreads[1]
        here.wait()
        for send in sends:
            send.wait_recv()
        to_plane = lax.rem(lax.rem(f, S) - s + S, S)
        down_sum[...] = jnp.sum(down_got[...].astype(F32), axis=0).astype(BF16)
        down_move = copy(down_sum, down_moved, down_sent, down_arrived, (to_plane, f))
        pl.when(to_plane != s)(down_move.start)

        @pl.when(to_plane == s)
        def _():
            down_moved[...] = down_sum[...]

        same = jnp.sum(bias_ref[0], keepdims=True)
        other = jnp.sum(bias_ref[1], keepdims=True) - same
        mine = lax.broadcasted_iota(jnp.int32, (1, 128), 1) == s * own_heads + column
        bias_tile = jnp.concatenate([jnp.where(mine, same, 0.0), jnp.where(mine, other, 0.0)])
        layer_own[...] = layer_ref[s]

        for load in loads[3:]:
            load.wait()
        for d in range(1, groups):
            dq_copy(d).wait_recv()
        for i in range(half - 1):
            to_owner(i).wait_recv()

        cosine, sine = cos_ref[...], sin_ref[...]
        gain_q, gain_k = [
            jnp.broadcast_to(ref[...], (128, dim)).T[:, :1] for ref in (gain_q_ref, gain_k_ref)
        ]

        def prepare_back(grad, raw, gain):
            front, back = grad[: dim // 2], grad[dim // 2 :]
            grad = join(front * cosine + back * sine, back * cosine - front * sine)
            inverse = lax.rsqrt(jnp.mean(raw * raw, axis=0, keepdims=True) + EPSILON)
            scaled = grad * gain
            mean = jnp.mean(scaled * raw, axis=0, keepdims=True)
            return inverse * scaled - raw * (inverse**3 * mean), grad * raw * inverse

        def gain_row(terms):
            folded = terms[:, :128]
            for n in range(1, group // 128):
                folded = folded + terms[:, n * 128 : (n + 1) * 128]
            return jnp.sum(folded.T, axis=0, keepdims=True)

        gain_terms = [jnp.zeros((dim, group), F32), jnp.zeros((dim, group), F32)]
        for h in range(own_heads):
            kv_grad = dkvs[h * (splits // 2)].astype(F32)
            for n in range(1, splits // 2):
                kv_grad = kv_grad + dkvs[h * (splits // 2) + n].astype(F32)
            kv_grad = kv_grad.astype(BF16).astype(F32)
            for n, (grad, gain) in enumerate(((dqs[h].astype(F32), gain_q), (kv_grad[:dim], gain_k))):
                back, terms = prepare_back(grad, raw_ref[n, h], gain)
                gain_terms[n] += terms
                pg_ref[:, pl.ds(n * lanes + h * dim, dim)] = back.T.astype(BF16)
            pg_ref[:, pl.ds(2 * lanes + h * dim, dim)] = kv_grad[dim:].T.astype(BF16)

        attn_gain = jnp.zeros((1, width), F32)
        for b in range(S):
            grad = nt(pg_ref[pl.ds(b * rows, rows), :], ws_ref[...])
            x = xs_ref[b].astype(F32)
            inverse = lax.rsqrt(jnp.mean(x * x, axis=1, keepdims=True) + EPSILON)
            attn_gain += jnp.sum(grad * x * inverse, axis=0, keepdims=True)
            u_ref[b] = grad.astype(BF16)
        normed_sum = LineSum(u_ref, from_left, from_right, (u_sent, u_got), s, f, S)
        normed_sum.step(0)

        for b in range(S):
            normed = rms_scale(xs_ref[b].astype(F32), gain_ref[...]).astype(BF16)
            terms = tn(normed, pg_ref[pl.ds(b * rows, rows), :])
            w_terms = terms if b == 0 else w_terms + terms
        w_part[...] = w_terms.astype(BF16).reshape(S, F, cut, 3 * lanes)
        w_got[f] = w_part[:, f]
        w_sends = []
        for d in range(1, F):
            to = lax.rem(f + d, F)
            w_sends.append(copy(w_part.at[:, to], w_got.at[f], w_sent.at[d], w_arrived.at[d], (s, to)))
            w_sends[-1].start()

        gains = jnp.concatenate([gain_row(gain_terms[0]), gain_row(gain_terms[1])], axis=1)
        gains = jnp.concatenate([gains, jnp.zeros((1, 256 - 2 * dim), F32)], axis=1)[:, :128]
        for n in range(chunks):
            lanes_ = slice(n * 128, (n + 1) * 128)
            vec[n] = jnp.concatenate(
                [attn_gain[:, lanes_], feed_ref[:, lanes_], gains, bias_tile, jnp.zeros((3, 128), F32)]
            )
        me = s * F + f
        vec_got[me] = vec[me * cut // 128]
        small = []
        for a in range(S):
            for b in range(F):
                if a or b:
                    to = (lax.rem(s + a, S), lax.rem(f + b, F))
                    chunk = (to[0] * F + to[1]) * cut // 128
                    n = a * F + b
                    small.append(copy(vec.at[chunk], vec_got.at[me], vec_sent.at[n], vec_arrived.at[n], to))
                    small[-1].start()

        for time in range(1, S - 1):
            normed_sum.step(time)
        for send in w_sends:
            send.wait_recv()
        w_sum[...] = jnp.sum(w_got[...].astype(F32), axis=0).astype(BF16)
        w_rows[s] = w_sum[s]
        last = []
        for d in range(1, S):
            to = lax.rem(s + d, S)
            last.append(copy(w_sum.at[to], w_rows.at[s], rows_sent.at[d], rows_got.at[d], (to, f)))
            last[-1].start()
        normed_sum.step(S - 1)
        u_own[...] = u_ref[s]

        for send in swaps + small + last:
            send.wait()
        for send in w_sends:
            send.wait_send()
        pl.when(to_plane != s)(down_move.wait)
        for _, sends in spreads:
            for send in sends:
                send.wait_send()
        for i in range(half):
            to_pair(i).wait_send()
            if i < half - 1:
                to_owner(i).wait_send()
        for d in range(1, groups):
            dq_copy(d).wait_send()
        layer.drain()
        normed_sum.drain()

    u_own, w_rows, gate_rows, up_rows, out_rows, down_moved, layer_own, vec_got = pl.pallas_call(
        kernel_g,
        in_specs=[VMEM] * 13 + [ANY] * 8,
        out_specs=[VMEM] * 8,
        out_shape=[
            shape((rows, width)),
            shape((S, cut, 3 * lanes)),
            shape((S, cut, hidden)),
            shape((S, cut, hidden)),
            shape((S, cut, width)),
            shape((down_rows, width)),
            shape((rows, width)),
            shape((count, small_rows, 128), F32),
        ],
        scratch_shapes=[
            pltpu.VMEM((half, S, cut, width), BF16),
            pltpu.VMEM((half, down_rows, width), BF16),
            pltpu.VMEM((half, S, cut, hidden), BF16),
            pltpu.VMEM((half, S, cut, hidden), BF16),
            *[pltpu.VMEM((groups * group, 2 * dim), BF16)] * 2,
            pltpu.VMEM((groups * group, 2 * dim), F32),
            pltpu.VMEM((2 * dim, group), F32),
            pltpu.VMEM((2, half, 2 * dim, group), BF16),
            pltpu.VMEM((half, 2 * dim, group), BF16),
            pltpu.VMEM((groups, dim, group), BF16),
            pltpu.VMEM((own_heads, dim, group), BF16),
            pltpu.VMEM((half, 2 * dim, group), BF16),
            pltpu.VMEM((S, cut, hidden), BF16),
            pltpu.VMEM((S, cut, hidden), BF16),
            pltpu.VMEM((S, cut, width), BF16),
            pltpu.VMEM((down_rows, width), BF16),
            *[pltpu.VMEM((S, rows, width), BF16)] * 3,
            pltpu.VMEM((2, own_heads, dim, group), F32),
            pltpu.VMEM((width, 3 * lanes), BF16),
            pltpu.VMEM((S, rows, width), BF16),
            pltpu.VMEM((group, 3 * lanes), BF16),
            *[pltpu.VMEM((S, rows, width), BF16)] * 3,
            pltpu.VMEM((S, F, cut, 3 * lanes), BF16),
            pltpu.VMEM((F, S, cut, 3 * lanes), BF16),
            pltpu.VMEM((S, cut, 3 * lanes), BF16),
            pltpu.VMEM((chunks, small_rows, 128), F32),
            pltpu.VMEM((2, VARIATES, QUERY_BLOCK), F32),
            dma((6,)),
            dma((2,)),
            *[dma((2, half))] * 2,
            *[dma((2, S))] * 2,
            *[dma((3, S))] * 2,
            *[dma((half,))] * 2,
            *[dma((half,))] * 2,
            *[dma((groups,))] * 2,
            *[dma((2, S))] * 2,
            *[dma((F,))] * 2,
            *[dma((S,))] * 2,
            *[dma((count,))] * 2,
            dma,
            dma,
        ],
        compiler_params=pltpu.CompilerParams(
            collective_id=1, has_side_effects=True, vmem_limit_bytes=VMEM_BYTES
        ),
    )(
        q_all, kv_all, query_marks, key_marks, grad_heads, attended, log_sum, cosine, sine, gain_query[None, :],
        gain_key[None, :], feed_gain, gain_attn[None, :], output_half, down_half, out_part, gate_got, up_got, raw, w_qkv,
        x_parts,
    )

    def kernel_z(
        x_ref, middle_ref, mid_grad_ref, u_ref, w_ref, gate_rows, up_rows, out_rows, down_ref, layer_ref, vec_ref, gain_ref,
        layer_out, tokens_out, attn_out, output_out, gate_out, up_out, down_out, attn_gain, feed_gain, gain_q, gain_k, bias,
    ):
        s, f = lax.axis_index("seq"), lax.axis_index("fsdp")
        layer_out[...] = (middle_ref[...] + layer_ref[...].astype(F32)).astype(BF16)
        x, grad = x_ref[...].astype(F32), u_ref[...].astype(F32)
        inverse = lax.rsqrt(jnp.mean(x * x, axis=1, keepdims=True) + EPSILON)
        scaled = grad * gain_ref[...]
        mean = jnp.mean(scaled * x, axis=1, keepdims=True)
        tokens_out[...] = mid_grad_ref[...] + inverse * scaled - x * (inverse**3 * mean)
        for n in range(S):
            for part in range(3):
                place = part * S * lanes + n * lanes
                attn_out[:, place : place + lanes] = w_ref[n, :, part * lanes : (part + 1) * lanes].astype(F32)
            for g in range(F):
                holder = (g % S - n) % S * per_plane + g // S
                place = (holder * S + g % S) * down_rows
                cols = slice(g * down_rows, (g + 1) * down_rows)
                gate_out[:, place : place + down_rows] = gate_rows[n, :, cols].astype(F32)
                up_out[:, place : place + down_rows] = up_rows[n, :, cols].astype(F32)
        output_out[...] = jnp.sum(out_rows[...].astype(F32), axis=0)
        down_out[...] = down_ref[...].astype(F32)
        sums = jnp.sum(vec_ref[...], axis=0)
        place = lax.rem((s * F + f) * cut, 128)
        for row, ref in ((0, attn_gain), (1, feed_gain)):
            picked = jnp.zeros((1, cut), F32)
            for n in range(0, 128, cut):
                picked = picked + jnp.where(place == n, sums[row : row + 1, n : n + cut], 0.0)
            ref[...] = picked
        gain_q[...] = sums[2:3, :dim]
        gain_k[...] = sums[2:3, dim : 2 * dim]
        bias[...] = sums[3:5, :heads]

    out = pl.pallas_call(
        kernel_z,
        in_specs=[VMEM] * 12,
        out_specs=[VMEM] * 12,
        out_shape=[
            shape((rows, width)),
            shape((rows, width), F32),
            shape((cut, 3 * S * lanes), F32),
            shape((cut, width), F32),
            shape((cut, S * hidden), F32),
            shape((cut, S * hidden), F32),
            shape((down_rows, width), F32),
            shape((1, cut), F32),
            shape((1, cut), F32),
            shape((1, dim), F32),
            shape((1, dim), F32),
            shape((2, heads), F32),
        ],
        compiler_params=pltpu.CompilerParams(vmem_limit_bytes=VMEM_BYTES),
    )(
        tokens, own_middle, middle_grad, u_own, w_rows, gate_rows, up_rows, out_rows, down_moved, layer_own, vec_got,
        gain_attn[None, :],
    )
    return (*out[:7], *[row[0] for row in out[7:11]], out[11].T)


def solution(mesh):
    by_token, by_fsdp, by_owner = P(("fsdp", "seq"), None), P("fsdp", None), P(("seq", "fsdp"), None)
    in_specs = (
        by_token,
        by_token,
        P(),
        P(),
        P(),
        P(),
        by_fsdp,
        P(),
        P(),
        P(),
        by_fsdp,
        P(),
        by_fsdp,
        by_fsdp,
        by_fsdp,
    )
    out_specs = (
        (by_token, by_token) + (by_owner,) * 5 + (P(("seq", "fsdp")),) * 2 + (P(),) * 3
    )
    return jax.shard_map(
        per_device, mesh=mesh, in_specs=in_specs, out_specs=out_specs, check_vma=False
    )
```

```python
import functools

import jax
import jax.numpy as jnp
from jax import lax
from jax.experimental import pallas as pl
from jax.experimental.pallas import tpu as pltpu
from jax.sharding import PartitionSpec as P

EPSILON = 1e-06
F32, BF16 = jnp.float32, jnp.bfloat16
VARIATES = 8
AWAY = 1024.0
QUERY_BLOCK = 256
LSE_ROW, VAR_ROW = 32, 40
MESH = pl.DeviceIdType.MESH
ANY = pl.BlockSpec(memory_space=pl.ANY)
VMEM = pl.BlockSpec(memory_space=pltpu.VMEM)
VMEM_BYTES = 60 * 2**20


def nn(a, b):
    return jnp.dot(a, b, preferred_element_type=F32)


def nt(a, b):
    return lax.dot_general(a, b, (((1,), (1,)), ((), ())), preferred_element_type=F32)


def tn(a, b):
    return lax.dot_general(a, b, (((0,), (0,)), ((), ())), preferred_element_type=F32)


def pieces(values):
    high = values.astype(BF16).astype(F32)
    middle = (values - high).astype(BF16).astype(F32)
    return high, middle, (values - high - middle).astype(BF16).astype(F32)


def send_all(plan, send_sems, recv_sems, local_sems):
    remote, local = plan
    copies = []
    for n, (src, dst, device, may_send, may_receive) in enumerate(remote):
        copy = pltpu.make_async_remote_copy(
            src_ref=src,
            dst_ref=dst,
            send_sem=send_sems.at[n],
            recv_sem=recv_sems.at[n],
            device_id=device,
            device_id_type=MESH,
        )
        when(may_send, copy.start)
        copies.append((copy, may_send, may_receive))
    locals_ = []
    for n, (src, dst, may) in enumerate(local):
        copy = pltpu.make_async_copy(src, dst, local_sems.at[n])
        when(may, copy.start)
        locals_.append((copy, may))

    def finish():
        for copy, may in locals_:
            when(may, copy.wait)
        for copy, may_send, may_receive in copies:
            when(may_send, copy.wait_send)
            when(may_receive, copy.wait_recv)

    return finish


def when(condition, action):
    if condition is None:
        action()
    else:
        pl.when(condition)(action)


def greet(devices):
    barrier = pltpu.get_barrier_semaphore()
    for device in devices:
        pl.semaphore_signal(barrier, inc=1, device_id=device, device_id_type=MESH)
    pl.semaphore_wait(barrier, len(devices))


class Line:
    def __init__(self, block, sems, s, f, S):
        self.block, (self.sent, self.got) = block, sems
        self.s, self.f, self.S = s, f, S

    def hop(self, plane, slot, step):
        ref = self.block(plane, slot)
        return pltpu.make_async_remote_copy(
            src_ref=ref,
            dst_ref=ref,
            send_sem=self.sent.at[plane, slot, int(step > 0)],
            recv_sem=self.got.at[plane, slot],
            device_id=(self.s + step, self.f),
            device_id_type=MESH,
        )

    def each_hop(self, slot, distance, action):
        s, S = self.s, self.S
        pl.when((s - distance + 1) * (S - 1 - s) > 0)(
            lambda: action(self.hop(s - distance, slot, 1))
        )
        pl.when((S - s - distance) * s > 0)(lambda: action(self.hop(s + distance, slot, -1)))

    def send(self, slot):
        self.each_hop(slot, 0, lambda hop: hop.start())

    def arrive(self, slot, distance):
        s, S = self.s, self.S
        pl.when(s - distance >= 0)(lambda: self.hop(s - distance, slot, 1).wait_recv())
        pl.when(s + distance < S)(lambda: self.hop(s + distance, slot, -1).wait_recv())
        self.each_hop(slot, distance, lambda hop: hop.start())

    def follow(self, slot, time):
        s, S = self.s, self.S
        p = 2 * s + 1 - time
        now = (p >= 0) & (p <= s) & (s + 1 < S)
        pl.when(now & (p < s))(lambda: self.hop(p, slot, 1).wait_recv())
        pl.when(now)(lambda: self.hop(p, slot, 1).start())
        m = S - 1 - s
        q = 2 * m + 1 - time
        now = (q >= 0) & (q <= m) & (s >= 1)
        pl.when(now & (q < m))(lambda: self.hop(S - 1 - q, slot, -1).wait_recv())
        pl.when(now)(lambda: self.hop(S - 1 - q, slot, -1).start())

    def follow_end(self, slot):
        for distance in range(1, self.S):
            pl.when(self.s == self.S - 1)(
                lambda distance=distance: self.hop(self.s - distance, slot, 1).wait_recv()
            )
            pl.when(self.s == 0)(
                lambda distance=distance: self.hop(self.s + distance, slot, -1).wait_recv()
            )

    def drain(self, slot):
        for distance in range(self.S):
            self.each_hop(slot, distance, lambda hop: hop.wait_send())


def line_sems(S, slots):
    return [pltpu.SemaphoreType.DMA((S, slots, 2)), pltpu.SemaphoreType.DMA((S, slots))]


class LineSum:
    def __init__(self, terms, from_left, from_right, sems, s, f, S):
        self.terms, self.from_left, self.from_right = terms, from_left, from_right
        self.sent, self.got = sems
        self.s, self.f, self.S = s, f, S

    def hop(self, t, to_right):
        return pltpu.make_async_remote_copy(
            src_ref=self.terms.at[t],
            dst_ref=(self.from_left if to_right else self.from_right).at[t],
            send_sem=self.sent.at[int(to_right), t],
            recv_sem=self.got.at[int(to_right), t],
            device_id=(self.s + (1 if to_right else -1), self.f),
            device_id_type=MESH,
        )

    def take(self, t, to_right):
        self.hop(t, to_right).wait_recv()
        came = (self.from_left if to_right else self.from_right)[t]
        self.terms[t] = (self.terms[t].astype(F32) + came.astype(F32)).astype(BF16)

    def step(self, time, now=True):
        s, S = self.s, self.S
        n = time - s
        here = (n >= 0) & (S - 1 - n >= s) & now
        pl.when(here & (s >= 1))(lambda: self.take(S - 1 - n, True))
        pl.when(here & (S - 1 - n > s))(lambda: self.hop(S - 1 - n, True).start())
        m = time - (S - 1 - s)
        here = (m >= 0) & (m <= s) & now
        pl.when(here & (s < S - 1))(lambda: self.take(m, False))
        pl.when(here & (m < s))(lambda: self.hop(m, False).start())

    def drain(self):
        for t in range(self.S):
            pl.when(self.s < t)(lambda t=t: self.hop(t, True).wait_send())
            pl.when(self.s > t)(lambda t=t: self.hop(t, False).wait_send())


class LineSums:
    def __init__(self, terms, from_left, from_right, sems, s, f, S):
        size = terms.shape[1] // 2
        self.parts = []
        for n in range(2):
            refs = [ref.at[:, pl.ds(n * size, size)] for ref in (terms, from_left, from_right)]
            self.parts.append(LineSum(*refs, sems[2 * n : 2 * n + 2], s, f, S))

    def step(self, time, now=True):
        for part in self.parts:
            part.step(time, now)

    def drain(self):
        for part in self.parts:
            part.drain()


def flipped(f, bit):
    step = 2**bit
    return f + step - 2 * step * lax.rem(f // step, 2)


class CubeGather:
    def __init__(self, block, own, sems, s, f, F):
        self.block, self.own, (self.sent, self.shared, self.got) = block, own, sems
        self.s, self.f, self.F = s, f, F
        bits = list(range(1, F.bit_length() - 1))
        self.orders = (bits, bits[::-1])

    def copy(self, g, half, sem, to, own=False):
        ref = self.block(g, half)
        return pltpu.make_async_remote_copy(
            src_ref=self.own(half) if own else ref,
            dst_ref=ref,
            send_sem=sem,
            recv_sem=self.got.at[g, half],
            device_id=(self.s, to),
            device_id_type=MESH,
        )

    def held(self, half, rounds):
        masks = [((), 0)]
        for n, bit in enumerate(self.orders[half][:rounds]):
            masks += [(mask + (bit,), n + 1) for mask, _ in list(masks)]
        return masks

    def device(self, mask):
        g = self.f
        for bit in mask:
            g = flipped(g, bit)
        return g

    def sends(self, half, since):
        rounds = len(self.orders[half])
        out = []
        for place, (mask, came) in enumerate(self.held(half, rounds)):
            for n in range(came, rounds):
                if came == since:
                    out.append((n, place, mask))
        return out

    def send(self, half, n, place, mask):
        bit = self.orders[half][n]
        sem = self.sent.at[half, n, place]
        return self.copy(self.device(mask), half, sem, flipped(self.f, bit), not mask)

    def shares(self, half, since):
        return [
            self.copy(
                self.device(mask), half, self.shared.at[half, place], flipped(self.f, 0), not mask
            )
            for place, (mask, came) in enumerate(self.held(half, len(self.orders[half])))
            if came == since
        ]

    @property
    def rounds(self):
        return len(self.orders[0])

    def start(self):
        for half in range(2):
            self.send(half, 0, 0, ()).start()
        for half in range(2):
            self.shares(half, 0)[0].start()

    def step(self, number):
        for half in range(2):
            shares = self.shares(half, number)
            for share in shares:
                share.wait_recv()
            if number < self.rounds:
                for which in self.sends(half, number) + self.sends(half, 0)[number : number + 1]:
                    if which[0] == number or which[1]:
                        self.send(half, *which).start()
            for share in shares:
                share.start()

    def finish(self):
        for half in range(2):
            for place, (mask, _) in enumerate(self.held(half, self.rounds)):
                g = flipped(self.device(mask), 0)
                self.copy(g, half, self.shared.at[half, place], self.f).wait_recv()

    def drain(self):
        for half in range(2):
            for number in range(self.rounds + 1):
                for which in self.sends(half, number):
                    self.send(half, *which).wait_send()
                for share in self.shares(half, number):
                    share.wait_send()


def cube_sems(F):
    rounds = F.bit_length() - 2
    return [
        pltpu.SemaphoreType.DMA((2, rounds, F // 4)),
        pltpu.SemaphoreType.DMA((2, F // 2)),
        pltpu.SemaphoreType.DMA((F, 2)),
    ]


def shape(dims, dtype=BF16):
    return jax.ShapeDtypeStruct(tuple(dims), dtype)


def join(a, b):
    return jnp.concatenate([a, b], axis=0)


def side_by_side(ref, *index):
    return jnp.concatenate([ref[(*index, n)] for n in range(ref.shape[len(index)])], axis=1)


def forward_group(j, q_ref, kv_ref, qa_ref, ka_ref, att_ref, lse_ref, o_ref):
    width, rows = att_ref.shape[1:]
    span = q_ref.shape[-1]
    sub = QUERY_BLOCK // span

    def block(i, _):
        cols = pl.ds(pl.multiple_of(i * QUERY_BLOCK, QUERY_BLOCK), QUERY_BLOCK)
        q_t = jnp.concatenate([q_ref[j, i * sub + n] for n in range(sub)], axis=1)
        queries = join(q_t, qa_ref[j, :, cols]).T
        total = jnp.zeros((QUERY_BLOCK, 2 * width), F32)
        for g in range(kv_ref.shape[0]):
            kv = side_by_side(kv_ref, g)
            keys = join(kv[:width], ka_ref[g])
            values = join(kv[width:], jnp.ones((width, rows), BF16))
            weights = jnp.exp(nn(queries, keys)).astype(BF16)
            total += nt(weights, values)
        total = total.T
        weight_sum = total[width : width + 1]
        attended = total[:width] / weight_sum
        att_ref[j, :, cols] = attended
        o_ref[j, :, cols] = attended.astype(BF16)
        lse_ref[j, :, cols] = jnp.log(weight_sum)
        return 0

    lax.fori_loop(0, rows // QUERY_BLOCK, block, 0)


def with_rows(base, first, rows):
    index = lax.broadcasted_iota(jnp.int32, base.shape, 0)
    for n, row in enumerate(rows):
        base = jnp.where(index == first + n, row, base)
    return base


def rms_scale(vector, gain, axis=-1):
    return vector * lax.rsqrt(jnp.mean(vector * vector, axis=axis, keepdims=True) + EPSILON) * gain


def per_device(
    tokens,
    cotangent,
    doc_starts,
    variate_ids,
    time_ids,
    gain_attn,
    w_attn,
    gain_query,
    gain_key,
    variate_bias,
    w_output,
    gain_feed,
    w_gate,
    w_up,
    w_down,
):
    S, F = lax.axis_size("seq"), lax.axis_size("fsdp")
    s, f = lax.axis_index("seq"), lax.axis_index("fsdp")
    rows, width = tokens.shape
    heads = variate_bias.shape[0]
    dim = gain_query.shape[0]
    own_heads = heads // S
    splits = F // own_heads
    group = rows * S
    groups = F // splits
    hidden = w_down.shape[0] * F // S
    half = F // 2
    cut = width // (S * F)
    lanes = own_heads * dim

    def along_seq(s, f):
        return [(lax.rem(s + d, S), f) for d in range(1, S)]

    def along_fsdp(s, f):
        return [(s, lax.rem(f + d, F)) for d in range(1, F)]

    def along_both(s, f):
        return along_seq(s, f) + along_fsdp(s, f)

    def like_parts(s, f):
        return [
            (lax.rem(s + a, S), lax.rem(f + b * splits, F))
            for a in range(S)
            for b in range(groups)
            if a or b
        ]

    def everyone(s, f):
        return [(lax.rem(s + a, S), lax.rem(f + b, F)) for a in range(S) for b in range(F) if a or b]

    def seq_swap(s, f, src, dst):
        remote = [(src.at[t[0]], dst.at[s], t, None, None) for t in along_seq(s, f)]
        return remote, [(src.at[s], dst.at[s], None)]

    per_plane = F // S
    down_rows = w_down.shape[0] // S
    local_rows = w_attn.shape[0]
    whole_tiles = down_rows % 128 == 0

    def unit_place(s, f):
        return lax.rem(f, per_plane) * S + lax.rem(f // per_plane + s, S)

    def unit_block(s, g):
        holder = lax.rem(lax.rem(g, S) - s + S, S) * per_plane + g // S
        return holder * S + lax.rem(g, S)

    def units(w):
        if whole_tiles:
            return w
        blocks = w.reshape(w.shape[0], S * F, down_rows)
        return jnp.concatenate(
            [lax.dynamic_index_in_dim(blocks, unit_block(s, g), 1, False) for g in range(F)], axis=1
        )

    def pair(s, f):
        return (s, flipped(f, 0))

    def same_parity(s, f):
        return [(s, lax.rem(f + 2 * d, F)) for d in range(1, half)]

    def peers_a(s, f):
        return like_parts(s, f) + [(s, lax.rem(f + d, F)) for d in range(1, F) if d % splits]

    block = 256 if width % 256 == 0 and hidden % 256 == 0 else 128

    frequency = (10000.0 ** (-2.0 * jnp.arange(dim // 2, dtype=F32) / dim))[:, None]
    total = F * group

    def kernel_a(
        x_ref, cot_ref, w_ref, wo_ref, wd_ref, wg_ref, wu_ref, times_ref, ids_ref, freq_ref, gain_ref, gain_q_ref, gain_k_ref,
        gain_feed_ref, bias_ref, starts_ref,
        xs_out, ws_out, raw_out, cos_ref, sin_ref, ka_out, qa_out, qs_out, kvs_out, att_out, lse_ref,
        grads_ref, middle_ref, mid_grad_ref, feed_ref, out_ref, gate_got, up_got, down_half, output_half,
        xs_ref, ws_ref, raw_ref, cots_ref, ka_ref, qa_ref, q_ref, kv_ref, att_ref, heads_ref, wos_ref, gates_ref, ups_ref,
        downs_ref, mid_v, n_v, n_t, hid_v, hid_t, gl_v, ul_v, u_ref, from_left, from_right,
        gate_part, up_part, down_part, output_part, gate_other, up_other, down_other, output_other, gate_half, up_half,
        hg_ref, u_sent, u_got, u_sent_, u_got_, pair_sent, pair_got, spread_sent, spread_got, own_sem, f_sent, f_got, out_sem,
        q_out, kv_out, o_ref, gate_own, up_own,
        w_sem, unit_sem, here_sem, x_sent, x_got, c_sent, c_got, kv_sent, kv_shared, kv_got, q_sent, q_got,
        o_sent, h_sent, h_got, *cube_refs,
    ):
        s, f = lax.axis_index("seq"), lax.axis_index("fsdp")
        column, part = f // splits, lax.rem(f, splits)
        loads = []
        for n in range(3):
            src = w_ref.at[:, pl.ds(pl.multiple_of(n * S * lanes + s * lanes, 128), lanes)]
            dst = ws_ref.at[pl.ds(f * local_rows, local_rows), pl.ds(n * lanes, lanes)]
            loads.append(pltpu.make_async_copy(src, dst, w_sem.at[n]))
        unit_loads = []
        for n, (src, dst) in enumerate(((wg_ref, gate_own), (wu_ref, up_own))):
            for g in range(F if whole_tiles else 1):
                if whole_tiles:
                    cols = pl.ds(pl.multiple_of(unit_block(s, g) * down_rows, 128), down_rows)
                    src_, dst_ = src.at[:, cols], dst.at[:, pl.ds(g * down_rows, down_rows)]
                else:
                    src_, dst_ = src, dst
                unit_loads.append(pltpu.make_async_copy(src_, dst_, unit_sem.at[n, g]))
        for load in loads + unit_loads:
            load.start()
        xs_ref[s] = x_ref[...]
        cots_ref[s] = cot_ref[...]
        greet(peers_a(s, f))
        xs = Line(lambda plane, slot: xs_ref.at[plane], (x_sent, x_got), s, f, S)
        cots = Line(lambda plane, slot: cots_ref.at[plane], (c_sent, c_got), s, f, S)
        xs.send(0)

        def rows_of(ref, size, place=lambda g: g):
            return lambda g, half: ref.at[pl.ds(place(g) * size + half * (size // 2), size // 2)]

        def half_of(ref, size):
            return lambda half: ref.at[pl.ds(half * (size // 2), size // 2)]

        down_own = wd_ref.at[lax.rem(f // per_plane + s, S)]
        down_place = unit_place(s, f)
        blocks = (
            (rows_of(ws_ref, local_rows), lambda half: rows_of(ws_ref, local_rows)(f, half)),
            (rows_of(wos_ref, local_rows), half_of(wo_ref, local_rows)),
            (rows_of(gates_ref, local_rows), half_of(gate_own, local_rows)),
            (rows_of(ups_ref, local_rows), half_of(up_own, local_rows)),
            (rows_of(downs_ref, down_rows, lambda g: unit_place(s, g)), half_of(down_own, down_rows)),
        )
        ws, wos, gates, ups, downs = [
            CubeGather(block, own, cube_refs[3 * n : 3 * n + 3], s, f, F) for n, (block, own) in enumerate(blocks)
        ]
        for load in loads:
            load.wait()
        ws.start()
        for load in unit_loads:
            load.wait()
        mine = pl.ds(f * local_rows, local_rows)
        here = [
            pltpu.make_async_copy(wo_ref, wos_ref.at[mine], here_sem.at[0]),
            pltpu.make_async_copy(gate_own, gates_ref.at[mine], here_sem.at[1]),
            pltpu.make_async_copy(up_own, ups_ref.at[mine], here_sem.at[2]),
            pltpu.make_async_copy(down_own, downs_ref.at[pl.ds(down_place * down_rows, down_rows)], here_sem.at[3]),
        ]
        for copy in here:
            copy.start()

        own_cols = pl.ds(pl.multiple_of(f * group, 128), group)
        angles = freq_ref[...] * times_ref[:, own_cols].astype(F32)
        cos_ref[...] = jnp.cos(angles)
        sin_ref[...] = jnp.sin(angles)
        mine_only = lax.broadcasted_iota(jnp.int32, (2, heads), 1) == s * own_heads + column
        biases = jnp.sum(jnp.where(mine_only, bias_ref[...], 0.0), axis=1, keepdims=True)
        difference = pieces(jnp.broadcast_to(biases[0:1] - biases[1:2], (VARIATES, group)))
        index = lax.broadcasted_iota(jnp.int32, (VARIATES, group), 0)

        def marks(g):
            ids = ids_ref[:, pl.ds(pl.multiple_of(g * group, 128), group)]
            positions = g * group + lax.broadcasted_iota(jnp.int32, (VARIATES, group), 1)
            docs = jnp.zeros((VARIATES, group), jnp.int32) - 1
            for n in range(doc_starts.shape[0]):
                docs = docs + (starts_ref[n] <= positions).astype(jnp.int32)
            return (docs == index).astype(F32), (ids == index).astype(F32)

        for g in range(F):
            doc, var = marks(g)
            tail = (index < 3).astype(F32)
            none = jnp.zeros((dim - LSE_ROW - VARIATES, group), F32)
            ka_ref[g] = jnp.concatenate([var, var, var, 1.0 - doc, tail, none]).astype(BF16)
        for j in range(groups):
            doc, var = marks(j * splits + part)
            none = jnp.zeros((VARIATES, group), F32)
            rest = jnp.zeros((dim - VAR_ROW - VARIATES, group), F32)
            scaled = [var * piece for piece in difference]
            qa_ref[j] = jnp.concatenate([*scaled, doc * -AWAY, none, var, rest]).astype(BF16)
        gain_q, gain_k = [
            jnp.broadcast_to(ref[...], (128, dim)).T[:, :rows] for ref in (gain_q_ref, gain_k_ref)
        ]

        def kv_copy(g, b, src, sem, to):
            return pltpu.make_async_remote_copy(
                src_ref=src, dst_ref=kv_ref.at[g, b], send_sem=sem, recv_sem=kv_got.at[g, b],
                device_id=(s, to), device_id_type=MESH,
            )

        def to_heads(b, d):
            to = lax.rem(f + 2 * d, F)
            return kv_copy(f, b, kv_out.at[b, to // splits], kv_sent.at[b, d], to)

        def to_neighbour(b, d):
            g = lax.rem(f + 2 * d, F)
            src = kv_ref.at[g, b] if d else kv_out.at[b, column]
            return kv_copy(g, b, src, kv_shared.at[b, d], flipped(f, 0))

        def queries_to_heads(b, d):
            to = lax.rem(f + d * splits, F)
            return pltpu.make_async_remote_copy(
                src_ref=q_out.at[b, to // splits], dst_ref=q_ref.at[column, b], send_sem=q_sent.at[b, d],
                recv_sem=q_got.at[column, b], device_id=(s, to), device_id_type=MESH,
            )

        def project(b):
            normed = rms_scale(xs_ref[b].astype(F32), gain_ref[...]).astype(BF16)
            projected = nn(normed, ws_ref[...]).T.reshape(3, own_heads, dim, rows)
            cols = pl.ds(pl.multiple_of(b * rows, rows), rows)
            cosine, sine = cos_ref[:, cols], sin_ref[:, cols]

            def turned(raw, gain):
                raw = rms_scale(raw, gain, axis=1)
                front, back = raw[:, : dim // 2], raw[:, dim // 2 :]
                return jnp.concatenate(
                    [front * cosine - back * sine, front * sine + back * cosine], axis=1
                )

            raw_ref[0, :, :, cols] = projected[0]
            raw_ref[1, :, :, cols] = projected[1]
            q_out[b] = (turned(projected[0], gain_q).astype(BF16).astype(F32) * dim**-0.5).astype(BF16)
            kv_out[b, :, :dim] = turned(projected[1], gain_k).astype(BF16)
            kv_out[b, :, dim:] = projected[2].astype(BF16)
            for d in range(1, half):
                to_heads(b, d).start()
            for d in range(1, groups):
                queries_to_heads(b, d).start()
            to_neighbour(b, 0).start()
            kv_ref[f, b] = kv_out[b, column]
            q_ref[column, b] = q_out[b, column]

        def share(b):
            for d in range(1, half):
                to_neighbour(b, d).wait_recv()
                to_neighbour(b, d).start()

        wos.start()
        gates.start()
        ws.step(1)
        wos.step(1)
        gates.step(1)
        for number in range(2, ws.rounds + 1):
            ws.step(number)
        ws.finish()
        project(s)
        for distance in range(1, S):
            xs.arrive(0, distance)
            cots.follow(0, distance)
            pl.when(s - distance >= 0)(lambda distance=distance: project(s - distance))
            pl.when(s + distance < S)(lambda distance=distance: project(s + distance))

        def share_all(b, _):
            share(b)
            return 0

        for time in range(S, 2 * S - 2):
            if time == (3 * S - 2) // 2:
                lax.fori_loop(0, S, share_all, 0)
            cots.follow(0, time)

        def last(b, _):
            for d in range(half):
                g = lax.rem(flipped(f, 0) + 2 * d, F)
                kv_copy(g, b, kv_ref.at[g, b], kv_shared.at[b, d], f).wait_recv()
            for d in range(1, groups):
                g = lax.rem(f + d * splits, F)
                pltpu.make_async_remote_copy(
                    src_ref=q_out.at[b, 0], dst_ref=q_ref.at[g // splits, b], send_sem=q_sent.at[b, d],
                    recv_sem=q_got.at[g // splits, b], device_id=(s, g), device_id_type=MESH,
                ).wait_recv()
            return 0

        lax.fori_loop(0, S, last, 0)
        ups.start()
        downs.start()

        own = s * own_heads + column

        def to_column(turn):
            j = lax.rem(column + turn, groups)
            return pltpu.make_async_remote_copy(
                src_ref=o_ref.at[j], dst_ref=heads_ref.at[own], send_sem=o_sent.at[turn], recv_sem=h_got.at[turn, 0],
                device_id=(s, j * splits + part), device_id_type=MESH,
            )

        def along(turn, d):
            ref = heads_ref.at[s * own_heads + lax.rem(column - turn + groups, groups)]
            return pltpu.make_async_remote_copy(
                src_ref=ref, dst_ref=ref, send_sem=h_sent.at[turn, d], recv_sem=h_got.at[turn, d],
                device_id=(lax.rem(s + d, S), f), device_id_type=MESH,
            )

        for turn in range(groups + 1):
            if turn < groups:
                j = lax.rem(column + turn, groups)
                forward_group(j, q_ref, kv_ref, qa_ref, ka_ref, att_ref, lse_ref, o_ref)
                if turn:
                    to_column(turn).start()
                else:
                    heads_ref[own] = o_ref[j]
            if turn != 1:
                came = max(turn - 1, 0)
                if came:
                    to_column(came).wait_recv()
                for d in range(1, S):
                    along(came, d).start()
            if turn == 0:
                for number in range(2, wos.rounds + 1):
                    wos.step(number)
                    gates.step(number)
            if turn == 3:
                ups.step(1)
                downs.step(1)
        for number in range(2, ups.rounds + 1):
            ups.step(number)
            downs.step(number)

        flushes = [
            pltpu.make_async_copy(src, dst, out_sem.at[n])
            for n, (src, dst) in enumerate(
                (
                    (xs_ref, xs_out), (ws_ref, ws_out), (raw_ref, raw_out), (ka_ref, ka_out), (qa_ref, qa_out),
                    (q_ref, qs_out), (kv_ref, kvs_out), (att_ref, att_out),
                )
            )
        ]
        for flush in flushes:
            flush.start()
        for turn in range(groups):
            for d in range(1, S):
                along(turn, d).wait_recv()
        for copy_ in here:
            copy_.wait()
        cots.follow_end(0)
        wos.finish()

        def copy(src, dst, sent, got, to):
            return pltpu.make_async_remote_copy(
                src_ref=src, dst_ref=dst, send_sem=sent, recv_sem=got, device_id=to, device_id_type=MESH
            )

        heads_rows = heads_ref[...].reshape(heads * dim, group).T
        for c in range(0, width, block):
            cs = slice(c, c + block)
            mid_v[:, cs] = xs_ref[:, :, cs].astype(F32).reshape(group, block) + nn(heads_rows, wos_ref[:, cs])
        normed = rms_scale(mid_v[...], gain_feed_ref[...]).astype(BF16)
        n_v[...] = normed
        n_t[...] = normed.T
        for gather in (gates, ups, downs):
            gather.finish()
        cot_rows = cots_ref[...].reshape(group, width)
        for c in range(0, hidden, block):
            cs = slice(c, c + block)
            gate_act, up_act = nn(n_v[...], gates_ref[:, cs]), nn(n_v[...], ups_ref[:, cs])
            hidden_grad = nt(cot_rows, downs_ref[cs, :])
            sigmoid = jax.nn.sigmoid(gate_act)
            silu = gate_act * sigmoid
            hidden_low = (silu * up_act).astype(BF16)
            hid_v[:, cs] = hidden_low
            hid_t[cs, :] = hidden_low.T
            gl_v[:, cs] = (hidden_grad * up_act * sigmoid * (1.0 + gate_act * (1.0 - sigmoid))).astype(BF16)
            ul_v[:, cs] = (hidden_grad * silu).astype(BF16)
        for c in range(0, width, block):
            cs = slice(c, c + block)
            grad = nt(gl_v[...], gates_ref[cs, :]) + nt(ul_v[...], ups_ref[cs, :])
            u_ref[:, :, cs] = grad.astype(BF16).reshape(S, rows, block)
        u_sems = (u_sent, u_got, u_sent_, u_got_)
        mid_sum = LineSums(u_ref, from_left, from_right, u_sems, s, f, S)
        mid_sum.step(0)

        parity = lax.rem(f, 2)
        by_owner = (S, half, 2, cut, block)

        def exchange_halves(n, part, other):
            away = part.at[:, 1 - parity] if len(part.shape) == 4 else part.at[:, :, 1 - parity]
            send = copy(away, other, pair_sent.at[n], pair_got.at[n], pair(s, f))
            send.start()
            return send

        for c in range(0, hidden, block):
            cs = slice(c, c + block)
            gate_part[..., cs] = nn(n_t[...], gl_v[:, cs]).astype(BF16).reshape(by_owner)
        swaps = [exchange_halves(0, gate_part, gate_other)]
        for c in range(0, hidden, block):
            cs = slice(c, c + block)
            up_part[..., cs] = nn(n_t[...], ul_v[:, cs]).astype(BF16).reshape(by_owner)
        swaps.append(exchange_halves(1, up_part, up_other))
        for c in range(0, width, block):
            cs = slice(c, c + block)
            down_part[..., cs] = nn(hid_t[...], cots_ref[:, :, cs].reshape(group, block)).astype(BF16).reshape(half, 2, down_rows, block)
        swaps.append(exchange_halves(2, down_part, down_other))
        for c in range(0, width, block):
            cs = slice(c, c + block)
            out_ref[:, :, cs] = nn(hid_v[...], downs_ref[:, cs]).astype(BF16).reshape(S, rows, block)

        def spread(n, halves, got):
            here = pltpu.make_async_copy(halves.at[:, f // 2], got.at[f // 2], own_sem.at[n])
            here.start()
            sends = []
            for d, to in enumerate(same_parity(s, f)):
                send = copy(halves.at[:, to[1] // 2], got.at[f // 2], spread_sent.at[n, d], spread_got.at[n, d], to)
                send.start()
                sends.append(send)
            return here, sends

        def add(a, b):
            return (a.astype(F32) + b.astype(F32)).astype(BF16)

        swaps[0].wait_recv()
        gate_half[...] = add(gate_part[:, :, parity], gate_other[...])
        spreads = [spread(0, gate_half, gate_got)]
        mid_sum.step(1)
        swaps[1].wait_recv()
        up_half[...] = add(up_part[:, :, parity], up_other[...])
        spreads.append(spread(1, up_half, up_got))
        swaps[2].wait_recv()
        down_half[...] = add(down_part[:, parity], down_other[...])
        for time in range(2, S):
            mid_sum.step(time)

        middle = mid_v[pl.ds(pl.multiple_of(s * rows, rows), rows), :]
        grad = u_ref[s].astype(F32)
        inverse = lax.rsqrt(jnp.mean(middle * middle, axis=1, keepdims=True) + EPSILON)
        scaled = grad * gain_feed_ref[...]
        mean = jnp.mean(scaled * middle, axis=1, keepdims=True)
        own_cot = cots_ref[s].astype(F32)
        middle_grad = own_cot + inverse * scaled - middle * (inverse**3 * mean)
        middle_low = middle_grad.astype(BF16)
        hg_ref[...] = nt(wos_ref[...], middle_low).astype(BF16).reshape(heads, dim, rows)

        place = grads_ref.at[f // splits, s]
        grads_here = pltpu.make_async_copy(hg_ref.at[s * own_heads + f // splits], place, own_sem.at[2])
        grads_here.start()
        sends = []
        for n, to in enumerate(like_parts(s, f)):
            send = copy(hg_ref.at[to[0] * own_heads + to[1] // splits], place, f_sent.at[n], f_got.at[n], to)
            send.start()
            sends.append(send)

        middle_ref[...] = middle
        mid_grad_ref[...] = middle_grad
        feed_ref[...] = jnp.sum(grad * middle * inverse, axis=0, keepdims=True)
        own_heads_t = heads_ref[:, :, pl.ds(pl.multiple_of(s * rows, rows), rows)].reshape(heads * dim, rows)
        for c in range(0, width, block):
            cs = slice(c, c + block)
            output_part[..., cs] = nn(own_heads_t, middle_low[:, cs]).astype(BF16).reshape(by_owner)
        swaps.append(exchange_halves(3, output_part, output_other))
        swaps[3].wait_recv()
        output_half[...] = add(output_part[:, :, parity], output_other[...])
        grads_here.wait()
        for send in sends:
            send.wait()
        for here, others in spreads:
            here.wait()
            for send in others:
                send.wait()
        for swap in swaps:
            swap.wait_send()
        mid_sum.drain()

        for flush in flushes:
            flush.wait()
        def sent(b, _):
            for d in range(half):
                if d:
                    to_heads(b, d).wait_send()
                to_neighbour(b, d).wait_send()
            for d in range(1, groups):
                queries_to_heads(b, d).wait_send()
            return 0

        lax.fori_loop(0, S, sent, 0)
        xs.drain(0)
        cots.drain(0)
        ws.drain()
        for turn in range(groups):
            if turn:
                to_column(turn).wait_send()
            for d in range(1, S):
                along(turn, d).wait_send()
        for gather in (wos, gates, ups, downs):
            gather.drain()

    dma = pltpu.SemaphoreType.DMA
    wide = (S, half, 2, cut, hidden)
    wide_half = (S, half, cut, hidden)
    kept = [
        shape((S, rows, width)),
        shape((width, 3 * lanes)),
        shape((2, own_heads, dim, group), F32),
        shape((F, dim, group)),
        shape((groups, dim, group)),
        shape((groups, S, dim, rows)),
        shape((F, S, 2 * dim, rows)),
        shape((groups, dim, group), F32),
    ]
    (
        x_parts, w_qkv, raw, cosine, sine, key_marks, query_marks, q_all, kv_all, attended, log_sum,
        grad_heads, own_middle, middle_grad, feed_gain, out_part, gate_got, up_got, down_half, output_half,
    ) = pl.pallas_call(
        kernel_a,
        in_specs=[VMEM] * 2 + [ANY] * 5 + [VMEM] * 8 + [pl.BlockSpec(memory_space=pltpu.SMEM)],
        out_specs=[ANY] * 3 + [VMEM] * 2 + [ANY] * 5 + [VMEM] + [ANY] + [VMEM] * 4 + [ANY] * 2 + [VMEM] * 2,
        out_shape=[
            *kept[:3],
            shape((dim // 2, group), F32),
            shape((dim // 2, group), F32),
            *kept[3:],
            shape((groups, 1, group), F32),
            shape((groups, S, dim, rows)),
            shape((rows, width), F32),
            shape((rows, width), F32),
            shape((1, width), F32),
            shape((S, rows, width)),
            shape((half, S, cut, hidden)),
            shape((half, S, cut, hidden)),
            shape((half, down_rows, width)),
            shape((S, half, cut, width)),
        ],
        scratch_shapes=[
            *[pltpu.VMEM(kept[n].shape, kept[n].dtype) for n in range(3)],
            pltpu.VMEM((S, rows, width), BF16),
            *[pltpu.VMEM(one.shape, one.dtype) for one in kept[3:]],
            pltpu.VMEM((heads, dim, group), BF16),
            pltpu.VMEM((heads * dim, width), BF16),
            pltpu.VMEM((width, hidden), BF16),
            pltpu.VMEM((width, hidden), BF16),
            pltpu.VMEM((hidden, width), BF16),
            pltpu.VMEM((group, width), F32),
            pltpu.VMEM((group, width), BF16),
            pltpu.VMEM((width, group), BF16),
            pltpu.VMEM((group, hidden), BF16),
            pltpu.VMEM((hidden, group), BF16),
            pltpu.VMEM((group, hidden), BF16),
            pltpu.VMEM((group, hidden), BF16),
            *[pltpu.VMEM((S, rows, width), BF16)] * 3,
            *[pltpu.VMEM(wide, BF16)] * 2,
            pltpu.VMEM((half, 2, down_rows, width), BF16),
            pltpu.VMEM((S, half, 2, cut, width), BF16),
            *[pltpu.VMEM(wide_half, BF16)] * 2,
            pltpu.VMEM((half, down_rows, width), BF16),
            pltpu.VMEM((S, half, cut, width), BF16),
            *[pltpu.VMEM(wide_half, BF16)] * 2,
            pltpu.VMEM((heads, dim, rows), BF16),
            *[dma((2, S))] * 4,
            *[dma((4,))] * 2,
            *[dma((2, half))] * 2,
            dma((3,)),
            *[dma((S * groups,))] * 2,
            dma((len(kept),)),
            pltpu.VMEM((S, own_heads, dim, rows), BF16),
            pltpu.VMEM((S, own_heads, 2 * dim, rows), BF16),
            pltpu.VMEM((groups, dim, group), BF16),
            pltpu.VMEM((local_rows, hidden), BF16),
            pltpu.VMEM((local_rows, hidden), BF16),
            dma((3,)),
            dma((2, F)),
            dma((4,)),
            *line_sems(S, 1),
            *line_sems(S, 1),
            dma((S, half)),
            dma((S, half)),
            dma((F, S)),
            dma((S, groups)),
            dma((groups, S)),
            dma((groups,)),
            dma((groups, S)),
            dma((groups, S)),
            *[sem for _ in range(5) for sem in cube_sems(F)],
        ],
        compiler_params=pltpu.CompilerParams(
            collective_id=0, has_side_effects=True, vmem_limit_bytes=VMEM_BYTES
        ),
        cost_estimate=pl.CostEstimate(flops=2 * 10**10, bytes_accessed=10**8, transcendentals=10**7),
    )(
        tokens,
        cotangent,
        w_attn,
        w_output,
        w_down.reshape(S, down_rows, width),
        units(w_gate),
        units(w_up),
        time_ids[None, :],
        variate_ids[None, :],
        frequency,
        gain_attn[None, :],
        gain_query[None, :],
        gain_key[None, :],
        gain_feed[None, :],
        variate_bias.T,
        doc_starts,
    )

    chunks = width // 128
    blocks = group // QUERY_BLOCK
    span = QUERY_BLOCK // rows
    small_rows = 8

    def kernel_g(
        q_ref, kv_ref, qa_ref, ka_ref, do_ref, att_ref, lse_ref, cos_ref, sin_ref, gain_q_ref, gain_k_ref, feed_ref,
        gain_ref, out_half, down_half, out_hbm, gate_hbm, up_hbm, raw_hbm, ws_hbm, xs_hbm,
        u_own, w_rows, gate_rows, up_rows, out_rows, down_moved, layer_own, vec_got,
        out_got, down_got, gate_got, up_got,
        qq_ref, dd_ref, dq_sum, kv_sum, kv_send, kv_other, dq_send, dqs, dkvs, gate_sum, up_sum, out_sum, down_sum,
        layer_ref, layer_left, layer_right, raw_ref, ws_ref, xs_ref, pg_ref, u_ref, from_left, from_right, w_part, w_other,
        w_half, w_got, w_sum, vec, normed_t, bias_ref,
        load_sem, own_sem, spread_sent, spread_got, layer_sent, layer_got, swap_sent, swap_got, pair_sent, pair_got,
        dkv_sent, dkv_got, dq_sent, dq_got, u_sent, u_got, u_sent_, u_got_, half_sent, half_got, w_sent, w_arrived, rows_sent, rows_got, vec_sent, vec_arrived,
        down_sent, down_arrived,
    ):
        s, f = lax.axis_index("seq"), lax.axis_index("fsdp")
        column, part, parity = f // splits, lax.rem(f, splits), lax.rem(f, 2)

        def copy(src, dst, sent, got, to):
            return pltpu.make_async_remote_copy(
                src_ref=src, dst_ref=dst, send_sem=sent, recv_sem=got, device_id=to, device_id_type=MESH
            )

        loads = [
            pltpu.make_async_copy(src, dst, load_sem.at[n])
            for n, (src, dst) in enumerate(
                (
                    (out_hbm, layer_ref), (gate_hbm, gate_got), (up_hbm, up_got), (raw_hbm, raw_ref), (ws_hbm, ws_ref),
                    (xs_hbm, xs_ref),
                )
            )
        ]
        for load in loads:
            load.start()
        greet(everyone(s, f))

        spreads = []
        for n, (src, got) in enumerate(((out_half, out_got), (down_half, down_got))):
            pick = (lambda ref, g: ref.at[:, g]) if n == 0 else (lambda ref, g: ref.at[g])
            here = pltpu.make_async_copy(pick(src, f // 2), got.at[f // 2], own_sem.at[n])
            here.start()
            sends = []
            for d, to in enumerate(same_parity(s, f)):
                sends.append(copy(pick(src, to[1] // 2), got.at[f // 2], spread_sent.at[n, d], spread_got.at[n, d], to))
                sends[-1].start()
            spreads.append((here, sends))
        layer = LineSum(layer_ref, layer_left, layer_right, (layer_sent, layer_got), s, f, S)
        loads[0].wait()
        layer.step(0)
        swaps = []

        def swap_rows(n, got, total, rows_ref):
            total[...] = jnp.sum(got[...].astype(F32), axis=0).astype(BF16)
            rows_ref[s] = total[s]
            for d in range(1, S):
                to = lax.rem(s + d, S)
                swaps.append(copy(total.at[to], rows_ref.at[s], swap_sent.at[n, d], swap_got.at[n, d], (to, f)))
                swaps[-1].start()

        for load in loads[1:3]:
            load.wait()
        swap_rows(0, gate_got, gate_sum, gate_rows)
        swap_rows(1, up_got, up_sum, up_rows)

        def rows_at(i):
            return pl.ds(pl.multiple_of(i * QUERY_BLOCK, QUERY_BLOCK), QUERY_BLOCK)

        def tokens_of(ref, i):
            j, first = i // blocks, (i % blocks) * span
            return jnp.concatenate([ref[j, first + n] for n in range(span)], axis=1)

        def ready(i, _):
            j, cols = i // blocks, rows_at(i % blocks)
            marks = qa_ref[j, :, cols].astype(F32)
            extra = with_rows(marks, LSE_ROW, pieces(-lse_ref[j, :, cols])).astype(BF16)
            qq_ref[rows_at(i), :] = join(tokens_of(q_ref, i), extra).T
            grad_t = tokens_of(do_ref, i)
            delta = jnp.sum(grad_t.astype(F32) * att_ref[j, :, cols], axis=0, keepdims=True)
            extra = with_rows(jnp.zeros((dim, QUERY_BLOCK), F32), 0, pieces(-delta)).astype(BF16)
            dd_ref[rows_at(i), :] = join(grad_t, extra).T
            return 0

        lax.fori_loop(0, groups * blocks, ready, 0)
        dq_sum[...] = jnp.zeros_like(dq_sum)

        def key_group(g):
            kv = side_by_side(kv_ref, g)
            keys = join(kv[:dim], ka_ref[g])
            values = join(kv[dim:], jnp.ones((dim, group), BF16))
            kv_sum[...] = jnp.zeros_like(kv_sum)
            for i in range(groups * blocks):
                q_rows = slice(i * QUERY_BLOCK, (i + 1) * QUERY_BLOCK)
                probs = jnp.exp(nn(qq_ref[q_rows, :], keys))
                score_grad = (probs * nn(dd_ref[q_rows, :], values)).astype(BF16)
                kv_sum[dim:, :] += nn(tokens_of(do_ref, i), probs.astype(BF16))
                kv_sum[:dim, :] += nn(tokens_of(q_ref, i), score_grad)
                dq_sum[q_rows, :] += nt(score_grad, keys)

        def to_pair(i):
            return copy(kv_send.at[0, i], kv_other.at[i], pair_sent.at[i], pair_got.at[i], (s, flipped(f, 0)))

        def to_owner(i):
            to = lax.rem(f + 2 * (i + 1), F)
            return copy(kv_send.at[1, i], dkvs.at[f // 2], dkv_sent.at[i], dkv_got.at[i], (s, to))

        def others(i, _):
            key_group(lax.rem(flipped(f, 0) + 2 * (i + 1), F))
            kv_send[0, i] = kv_sum[...].astype(BF16)
            to_pair(i).start()
            return 0

        lax.fori_loop(0, half, others, 0)
        layer.step(1)
        here, sends = spreads[0]
        here.wait()
        for send in sends:
            send.wait_recv()
        swap_rows(2, out_got, out_sum, out_rows)

        def owns(i, _):
            key_group(lax.rem(f + 2 * (i + 1), F))
            to_pair(i).wait_recv()
            kv_send[1, i] = (kv_sum[...] + kv_other[i].astype(F32)).astype(BF16)
            pl.when(i < half - 1)(lambda: to_owner(i).start())
            return 0

        lax.fori_loop(0, half, owns, 0)
        dkvs[f // 2] = kv_send[1, half - 1]
        layer.step(2)

        bias_ref[...] = jnp.zeros_like(bias_ref)

        def dq_copy(d):
            to = lax.rem(f + d * splits, F)
            return copy(dq_send.at[to // splits], dqs.at[column], dq_sent.at[d], dq_got.at[d], (s, to))

        def queries_done(i, _):
            j, cols = i // blocks, rows_at(i % blocks)
            dq_t = dq_sum[rows_at(i), :].T
            dq_send[j, :, cols] = (dq_t[:dim] * dim**-0.5).astype(BF16)
            by_variate = dq_t[dim : dim + VARIATES]
            bias_ref[0] += by_variate * qa_ref[j, VAR_ROW : VAR_ROW + VARIATES, cols].astype(F32)
            bias_ref[1] += by_variate
            return 0

        lax.fori_loop(0, groups * blocks, queries_done, 0)
        for d in range(1, groups):
            dq_copy(d).start()
        dqs[column] = dq_send[column]
        here, sends = spreads[1]
        here.wait()
        for send in sends:
            send.wait_recv()
        to_plane = lax.rem(lax.rem(f, S) - s + S, S)
        down_sum[...] = jnp.sum(down_got[...].astype(F32), axis=0).astype(BF16)
        down_move = copy(down_sum, down_moved, down_sent, down_arrived, (to_plane, f))
        pl.when(to_plane != s)(down_move.start)

        @pl.when(to_plane == s)
        def _():
            down_moved[...] = down_sum[...]

        same = jnp.sum(bias_ref[0], keepdims=True)
        other = jnp.sum(bias_ref[1], keepdims=True) - same
        mine = lax.broadcasted_iota(jnp.int32, (1, 128), 1) == s * own_heads + column
        bias_tile = jnp.concatenate([jnp.where(mine, same, 0.0), jnp.where(mine, other, 0.0)])

        for load in loads[3:]:
            load.wait()
        for time in range(3, S):
            layer.step(time)
        layer_own[...] = layer_ref[s]
        x = xs_ref[...].astype(F32).reshape(group, width)
        inverse = lax.rsqrt(jnp.mean(x * x, axis=1, keepdims=True) + EPSILON)
        normed_t[...] = (x * inverse * gain_ref[...]).astype(BF16).T
        for i in range(half - 1):
            to_owner(i).wait_recv()

        cosine, sine = cos_ref[...], sin_ref[...]
        gain_q, gain_k = [
            jnp.broadcast_to(ref[...], (128, dim)).T[:, :1] for ref in (gain_q_ref, gain_k_ref)
        ]

        def prepare_back(grad, raw, gain):
            front, back = grad[: dim // 2], grad[dim // 2 :]
            grad = join(front * cosine + back * sine, back * cosine - front * sine)
            inverse = lax.rsqrt(jnp.mean(raw * raw, axis=0, keepdims=True) + EPSILON)
            scaled = grad * gain
            mean = jnp.mean(scaled * raw, axis=0, keepdims=True)
            return inverse * scaled - raw * (inverse**3 * mean), grad * raw * inverse

        def gain_row(terms):
            folded = terms[:, :128]
            for n in range(1, group // 128):
                folded = folded + terms[:, n * 128 : (n + 1) * 128]
            return jnp.sum(folded.T, axis=0, keepdims=True)

        key_terms = jnp.zeros((dim, group), F32)
        for h in range(own_heads):
            kv_grad = dkvs[h * (splits // 2)].astype(F32)
            for n in range(1, splits // 2):
                kv_grad = kv_grad + dkvs[h * (splits // 2) + n].astype(F32)
            kv_grad = kv_grad.astype(BF16).astype(F32)
            back, terms = prepare_back(kv_grad[:dim], raw_ref[1, h], gain_k)
            key_terms += terms
            pg_ref[:, pl.ds(lanes + h * dim, dim)] = back.T.astype(BF16)
            pg_ref[:, pl.ds(2 * lanes + h * dim, dim)] = kv_grad[dim:].T.astype(BF16)
        for d in range(1, groups):
            dq_copy(d).wait_recv()
        query_terms = jnp.zeros((dim, group), F32)
        for h in range(own_heads):
            back, terms = prepare_back(dqs[h].astype(F32), raw_ref[0, h], gain_q)
            query_terms += terms
            pg_ref[:, pl.ds(h * dim, dim)] = back.T.astype(BF16)

        attn_gain = []
        for c in range(0, width, block):
            cs = slice(c, c + block)
            grad = nt(pg_ref[...], ws_ref[cs, :])
            scaled = xs_ref[:, :, cs].astype(F32).reshape(group, block) * inverse
            attn_gain.append(jnp.sum(grad * scaled, axis=0, keepdims=True))
            u_ref[:, :, cs] = grad.astype(BF16).reshape(S, rows, block)
        attn_gain = jnp.concatenate(attn_gain, axis=1)
        normed_sum = LineSums(u_ref, from_left, from_right, (u_sent, u_got, u_sent_, u_got_), s, f, S)
        normed_sum.step(0)

        step = 256 if 3 * lanes % 256 == 0 else 128
        for c in range(0, 3 * lanes, step):
            cs = slice(c, c + step)
            terms = nn(normed_t[...], pg_ref[:, cs]).astype(BF16)
            w_part[..., cs] = terms.reshape(S, half, 2, cut, step)
        to_other = copy(w_part.at[:, :, 1 - parity], w_other, half_sent, half_got, (s, flipped(f, 0)))
        to_other.start()
        gains = jnp.concatenate([gain_row(query_terms), gain_row(key_terms)], axis=1)
        gains = jnp.concatenate([gains, jnp.zeros((1, 256 - 2 * dim), F32)], axis=1)[:, :128]
        for n in range(chunks):
            lanes_ = slice(n * 128, (n + 1) * 128)
            vec[n] = jnp.concatenate(
                [attn_gain[:, lanes_], feed_ref[:, lanes_], gains, bias_tile, jnp.zeros((3, 128), F32)]
            )
        me = s * F + f
        vec_got[me] = vec[me * cut // 128]
        small = []
        for n, to in enumerate(everyone(s, f)):
            chunk = (to[0] * F + to[1]) * cut // 128
            small.append(copy(vec.at[chunk], vec_got.at[me], vec_sent.at[n], vec_arrived.at[n], to))
            small[-1].start()

        to_other.wait()
        w_half[...] = (w_part[:, :, parity].astype(F32) + w_other[...].astype(F32)).astype(BF16)
        w_got[f // 2] = w_half[:, f // 2]
        w_sends = []
        for d, to in enumerate(same_parity(s, f)):
            w_sends.append(copy(w_half.at[:, to[1] // 2], w_got.at[f // 2], w_sent.at[d], w_arrived.at[d], to))
            w_sends[-1].start()
        for time in range(1, S - 1):
            normed_sum.step(time)
        for send in w_sends:
            send.wait_recv()
        w_sum[...] = jnp.sum(w_got[...].astype(F32), axis=0).astype(BF16)
        w_rows[s] = w_sum[s]
        last = []
        for d in range(1, S):
            to = lax.rem(s + d, S)
            last.append(copy(w_sum.at[to], w_rows.at[s], rows_sent.at[d], rows_got.at[d], (to, f)))
            last[-1].start()
        normed_sum.step(S - 1)
        u_own[...] = u_ref[s]

        for send in swaps + small + last:
            send.wait()
        for send in w_sends:
            send.wait_send()
        pl.when(to_plane != s)(down_move.wait)
        for _, sends in spreads:
            for send in sends:
                send.wait_send()
        for i in range(half):
            to_pair(i).wait_send()
            if i < half - 1:
                to_owner(i).wait_send()
        for d in range(1, groups):
            dq_copy(d).wait_send()
        layer.drain()
        normed_sum.drain()

    u_own, w_rows, gate_rows, up_rows, out_rows, down_moved, layer_own, vec_got = pl.pallas_call(
        kernel_g,
        in_specs=[VMEM] * 13 + [ANY] * 8,
        out_specs=[VMEM] * 8,
        out_shape=[
            shape((rows, width)),
            shape((S, cut, 3 * lanes)),
            shape((S, cut, hidden)),
            shape((S, cut, hidden)),
            shape((S, cut, width)),
            shape((down_rows, width)),
            shape((rows, width)),
            shape((S * F, small_rows, 128), F32),
        ],
        scratch_shapes=[
            pltpu.VMEM((half, S, cut, width), BF16),
            pltpu.VMEM((half, down_rows, width), BF16),
            pltpu.VMEM((half, S, cut, hidden), BF16),
            pltpu.VMEM((half, S, cut, hidden), BF16),
            *[pltpu.VMEM((groups * group, 2 * dim), BF16)] * 2,
            pltpu.VMEM((groups * group, 2 * dim), F32),
            pltpu.VMEM((2 * dim, group), F32),
            pltpu.VMEM((2, half, 2 * dim, group), BF16),
            pltpu.VMEM((half, 2 * dim, group), BF16),
            pltpu.VMEM((groups, dim, group), BF16),
            pltpu.VMEM((own_heads, dim, group), BF16),
            pltpu.VMEM((half, 2 * dim, group), BF16),
            pltpu.VMEM((S, cut, hidden), BF16),
            pltpu.VMEM((S, cut, hidden), BF16),
            pltpu.VMEM((S, cut, width), BF16),
            pltpu.VMEM((down_rows, width), BF16),
            *[pltpu.VMEM((S, rows, width), BF16)] * 3,
            pltpu.VMEM((2, own_heads, dim, group), F32),
            pltpu.VMEM((width, 3 * lanes), BF16),
            pltpu.VMEM((S, rows, width), BF16),
            pltpu.VMEM((group, 3 * lanes), BF16),
            *[pltpu.VMEM((S, rows, width), BF16)] * 3,
            pltpu.VMEM((S, half, 2, cut, 3 * lanes), BF16),
            pltpu.VMEM((S, half, cut, 3 * lanes), BF16),
            pltpu.VMEM((S, half, cut, 3 * lanes), BF16),
            pltpu.VMEM((half, S, cut, 3 * lanes), BF16),
            pltpu.VMEM((S, cut, 3 * lanes), BF16),
            pltpu.VMEM((chunks, small_rows, 128), F32),
            pltpu.VMEM((width, group), BF16),
            pltpu.VMEM((2, VARIATES, QUERY_BLOCK), F32),
            dma((6,)),
            dma((2,)),
            *[dma((2, half))] * 2,
            *[dma((2, S))] * 2,
            *[dma((3, S))] * 2,
            *[dma((half,))] * 2,
            *[dma((half,))] * 2,
            *[dma((groups,))] * 2,
            *[dma((2, S))] * 4,
            dma,
            dma,
            *[dma((half,))] * 2,
            *[dma((S,))] * 2,
            *[dma((S * F,))] * 2,
            dma,
            dma,
        ],
        compiler_params=pltpu.CompilerParams(
            collective_id=1, has_side_effects=True, vmem_limit_bytes=VMEM_BYTES
        ),
    )(
        q_all, kv_all, query_marks, key_marks, grad_heads, attended, log_sum, cosine, sine, gain_query[None, :],
        gain_key[None, :], feed_gain, gain_attn[None, :], output_half, down_half, out_part, gate_got, up_got, raw, w_qkv,
        x_parts,
    )

    def kernel_z(
        x_ref, middle_ref, mid_grad_ref, u_ref, w_ref, gate_rows, up_rows, out_rows, down_ref, layer_ref, vec_ref, gain_ref,
        layer_out, tokens_out, attn_out, output_out, gate_out, up_out, down_out, attn_gain, feed_gain, gain_q, gain_k, bias,
    ):
        s, f = lax.axis_index("seq"), lax.axis_index("fsdp")
        layer_out[...] = (middle_ref[...] + layer_ref[...].astype(F32)).astype(BF16)
        x, grad = x_ref[...].astype(F32), u_ref[...].astype(F32)
        inverse = lax.rsqrt(jnp.mean(x * x, axis=1, keepdims=True) + EPSILON)
        scaled = grad * gain_ref[...]
        mean = jnp.mean(scaled * x, axis=1, keepdims=True)
        tokens_out[...] = mid_grad_ref[...] + inverse * scaled - x * (inverse**3 * mean)
        for n in range(S):
            for part in range(3):
                place = part * S * lanes + n * lanes
                attn_out[:, place : place + lanes] = w_ref[n, :, part * lanes : (part + 1) * lanes].astype(F32)
            for g in range(F):
                holder = (g % S - n) % S * per_plane + g // S
                place = (holder * S + g % S) * down_rows
                cols = slice(g * down_rows, (g + 1) * down_rows)
                gate_out[:, place : place + down_rows] = gate_rows[n, :, cols].astype(F32)
                up_out[:, place : place + down_rows] = up_rows[n, :, cols].astype(F32)
        output_out[...] = jnp.sum(out_rows[...].astype(F32), axis=0)
        down_out[...] = down_ref[...].astype(F32)
        sums = jnp.sum(vec_ref[...], axis=0)
        place = lax.rem((s * F + f) * cut, 128)
        for row, ref in ((0, attn_gain), (1, feed_gain)):
            picked = jnp.zeros((1, cut), F32)
            for n in range(0, 128, cut):
                picked = picked + jnp.where(place == n, sums[row : row + 1, n : n + cut], 0.0)
            ref[...] = picked
        gain_q[...] = sums[2:3, :dim]
        gain_k[...] = sums[2:3, dim : 2 * dim]
        bias[...] = sums[3:5, :heads]

    out = pl.pallas_call(
        kernel_z,
        in_specs=[VMEM] * 12,
        out_specs=[VMEM] * 12,
        out_shape=[
            shape((rows, width)),
            shape((rows, width), F32),
            shape((cut, 3 * S * lanes), F32),
            shape((cut, width), F32),
            shape((cut, S * hidden), F32),
            shape((cut, S * hidden), F32),
            shape((down_rows, width), F32),
            shape((1, cut), F32),
            shape((1, cut), F32),
            shape((1, dim), F32),
            shape((1, dim), F32),
            shape((2, heads), F32),
        ],
        compiler_params=pltpu.CompilerParams(vmem_limit_bytes=VMEM_BYTES),
    )(
        tokens, own_middle, middle_grad, u_own, w_rows, gate_rows, up_rows, out_rows, down_moved, layer_own, vec_got,
        gain_attn[None, :],
    )
    return (*out[:7], *[row[0] for row in out[7:11]], out[11].T)


def solution(mesh):
    by_token, by_fsdp, by_owner = P(("fsdp", "seq"), None), P("fsdp", None), P(("seq", "fsdp"), None)
    in_specs = (
        by_token,
        by_token,
        P(),
        P(),
        P(),
        P(),
        by_fsdp,
        P(),
        P(),
        P(),
        by_fsdp,
        P(),
        by_fsdp,
        by_fsdp,
        by_fsdp,
    )
    out_specs = (
        (by_token, by_token) + (by_owner,) * 5 + (P(("seq", "fsdp")),) * 2 + (P(),) * 3
    )
    return jax.shard_map(
        per_device, mesh=mesh, in_specs=in_specs, out_specs=out_specs, check_vma=False
    )
```

```python
import functools

import jax
import jax.numpy as jnp
from jax import lax
from jax.experimental import pallas as pl
from jax.experimental.pallas import tpu as pltpu
from jax.sharding import PartitionSpec as P

EPSILON = 1e-06
F32, BF16 = jnp.float32, jnp.bfloat16
VARIATES = 8
AWAY = 1024.0
QUERY_BLOCK = 256
LSE_ROW, VAR_ROW = 32, 40
MESH = pl.DeviceIdType.MESH
ANY = pl.BlockSpec(memory_space=pl.ANY)
VMEM = pl.BlockSpec(memory_space=pltpu.VMEM)
VMEM_BYTES = 60 * 2**20


def nn(a, b):
    return jnp.dot(a, b, preferred_element_type=F32)


def nt(a, b):
    return lax.dot_general(a, b, (((1,), (1,)), ((), ())), preferred_element_type=F32)


def tn(a, b):
    return lax.dot_general(a, b, (((0,), (0,)), ((), ())), preferred_element_type=F32)


def pieces(values):
    high = values.astype(BF16).astype(F32)
    middle = (values - high).astype(BF16).astype(F32)
    return high, middle, (values - high - middle).astype(BF16).astype(F32)


def send_all(plan, send_sems, recv_sems, local_sems):
    remote, local = plan
    copies = []
    for n, (src, dst, device, may_send, may_receive) in enumerate(remote):
        copy = pltpu.make_async_remote_copy(
            src_ref=src,
            dst_ref=dst,
            send_sem=send_sems.at[n],
            recv_sem=recv_sems.at[n],
            device_id=device,
            device_id_type=MESH,
        )
        when(may_send, copy.start)
        copies.append((copy, may_send, may_receive))
    locals_ = []
    for n, (src, dst, may) in enumerate(local):
        copy = pltpu.make_async_copy(src, dst, local_sems.at[n])
        when(may, copy.start)
        locals_.append((copy, may))

    def finish():
        for copy, may in locals_:
            when(may, copy.wait)
        for copy, may_send, may_receive in copies:
            when(may_send, copy.wait_send)
            when(may_receive, copy.wait_recv)

    return finish


def when(condition, action):
    if condition is None:
        action()
    else:
        pl.when(condition)(action)


def greet(devices):
    barrier = pltpu.get_barrier_semaphore()
    for device in devices:
        pl.semaphore_signal(barrier, inc=1, device_id=device, device_id_type=MESH)
    pl.semaphore_wait(barrier, len(devices))


class Line:
    def __init__(self, block, sems, s, f, S):
        self.block, (self.sent, self.got) = block, sems
        self.s, self.f, self.S = s, f, S

    def hop(self, plane, slot, step):
        ref = self.block(plane, slot)
        return pltpu.make_async_remote_copy(
            src_ref=ref,
            dst_ref=ref,
            send_sem=self.sent.at[plane, slot, int(step > 0)],
            recv_sem=self.got.at[plane, slot],
            device_id=(self.s + step, self.f),
            device_id_type=MESH,
        )

    def each_hop(self, slot, distance, action):
        s, S = self.s, self.S
        pl.when((s - distance + 1) * (S - 1 - s) > 0)(
            lambda: action(self.hop(s - distance, slot, 1))
        )
        pl.when((S - s - distance) * s > 0)(lambda: action(self.hop(s + distance, slot, -1)))

    def send(self, slot):
        self.each_hop(slot, 0, lambda hop: hop.start())

    def arrive(self, slot, distance):
        s, S = self.s, self.S
        pl.when(s - distance >= 0)(lambda: self.hop(s - distance, slot, 1).wait_recv())
        pl.when(s + distance < S)(lambda: self.hop(s + distance, slot, -1).wait_recv())
        self.each_hop(slot, distance, lambda hop: hop.start())

    def follow(self, slot, time):
        s, S = self.s, self.S
        p = 2 * s + 1 - time
        now = (p >= 0) & (p <= s) & (s + 1 < S)
        pl.when(now & (p < s))(lambda: self.hop(p, slot, 1).wait_recv())
        pl.when(now)(lambda: self.hop(p, slot, 1).start())
        m = S - 1 - s
        q = 2 * m + 1 - time
        now = (q >= 0) & (q <= m) & (s >= 1)
        pl.when(now & (q < m))(lambda: self.hop(S - 1 - q, slot, -1).wait_recv())
        pl.when(now)(lambda: self.hop(S - 1 - q, slot, -1).start())

    def follow_end(self, slot):
        for distance in range(1, self.S):
            pl.when(self.s == self.S - 1)(
                lambda distance=distance: self.hop(self.s - distance, slot, 1).wait_recv()
            )
            pl.when(self.s == 0)(
                lambda distance=distance: self.hop(self.s + distance, slot, -1).wait_recv()
            )

    def drain(self, slot):
        for distance in range(self.S):
            self.each_hop(slot, distance, lambda hop: hop.wait_send())


def line_sems(S, slots):
    return [pltpu.SemaphoreType.DMA((S, slots, 2)), pltpu.SemaphoreType.DMA((S, slots))]


class LineSum:
    def __init__(self, terms, from_left, from_right, sems, s, f, S):
        self.terms, self.from_left, self.from_right = terms, from_left, from_right
        self.sent, self.got = sems
        self.s, self.f, self.S = s, f, S

    def hop(self, t, to_right):
        return pltpu.make_async_remote_copy(
            src_ref=self.terms.at[t],
            dst_ref=(self.from_left if to_right else self.from_right).at[t],
            send_sem=self.sent.at[int(to_right), t],
            recv_sem=self.got.at[int(to_right), t],
            device_id=(self.s + (1 if to_right else -1), self.f),
            device_id_type=MESH,
        )

    def take(self, t, to_right):
        self.hop(t, to_right).wait_recv()
        came = (self.from_left if to_right else self.from_right)[t]
        self.terms[t] = (self.terms[t].astype(F32) + came.astype(F32)).astype(BF16)

    def step(self, time, now=True):
        s, S = self.s, self.S
        n = time - s
        here = (n >= 0) & (S - 1 - n >= s) & now
        pl.when(here & (s >= 1))(lambda: self.take(S - 1 - n, True))
        pl.when(here & (S - 1 - n > s))(lambda: self.hop(S - 1 - n, True).start())
        m = time - (S - 1 - s)
        here = (m >= 0) & (m <= s) & now
        pl.when(here & (s < S - 1))(lambda: self.take(m, False))
        pl.when(here & (m < s))(lambda: self.hop(m, False).start())

    def drain(self):
        for t in range(self.S):
            pl.when(self.s < t)(lambda t=t: self.hop(t, True).wait_send())
            pl.when(self.s > t)(lambda t=t: self.hop(t, False).wait_send())


class LineSums:
    def __init__(self, terms, from_left, from_right, sems, s, f, S):
        size = terms.shape[1] // 2
        self.parts = []
        for n in range(2):
            refs = [ref.at[:, pl.ds(n * size, size)] for ref in (terms, from_left, from_right)]
            self.parts.append(LineSum(*refs, sems[2 * n : 2 * n + 2], s, f, S))

    def step(self, time, now=True):
        for part in self.parts:
            part.step(time, now)

    def drain(self):
        for part in self.parts:
            part.drain()


def flipped(f, bit):
    step = 2**bit
    return f + step - 2 * step * lax.rem(f // step, 2)


class CubeGather:
    def __init__(self, block, own, sems, s, f, F):
        self.block, self.own, (self.sent, self.shared, self.got) = block, own, sems
        self.s, self.f, self.F = s, f, F
        bits = list(range(1, F.bit_length() - 1))
        self.orders = (bits, bits[::-1])

    def copy(self, g, half, sem, to, own=False):
        ref = self.block(g, half)
        return pltpu.make_async_remote_copy(
            src_ref=self.own(half) if own else ref,
            dst_ref=ref,
            send_sem=sem,
            recv_sem=self.got.at[g, half],
            device_id=(self.s, to),
            device_id_type=MESH,
        )

    def held(self, half, rounds):
        masks = [((), 0)]
        for n, bit in enumerate(self.orders[half][:rounds]):
            masks += [(mask + (bit,), n + 1) for mask, _ in list(masks)]
        return masks

    def device(self, mask):
        g = self.f
        for bit in mask:
            g = flipped(g, bit)
        return g

    def sends(self, half, since):
        rounds = len(self.orders[half])
        out = []
        for place, (mask, came) in enumerate(self.held(half, rounds)):
            for n in range(came, rounds):
                if came == since:
                    out.append((n, place, mask))
        return out

    def send(self, half, n, place, mask):
        bit = self.orders[half][n]
        sem = self.sent.at[half, n, place]
        return self.copy(self.device(mask), half, sem, flipped(self.f, bit), not mask)

    def shares(self, half, since):
        return [
            self.copy(
                self.device(mask), half, self.shared.at[half, place], flipped(self.f, 0), not mask
            )
            for place, (mask, came) in enumerate(self.held(half, len(self.orders[half])))
            if came == since
        ]

    @property
    def rounds(self):
        return len(self.orders[0])

    def start(self):
        for half in range(2):
            self.send(half, 0, 0, ()).start()
        for half in range(2):
            self.shares(half, 0)[0].start()

    def step(self, number):
        for half in range(2):
            shares = self.shares(half, number)
            for share in shares:
                share.wait_recv()
            if number < self.rounds:
                for which in self.sends(half, number) + self.sends(half, 0)[number : number + 1]:
                    if which[0] == number or which[1]:
                        self.send(half, *which).start()
            for share in shares:
                share.start()

    def finish(self):
        for half in range(2):
            for place, (mask, _) in enumerate(self.held(half, self.rounds)):
                g = flipped(self.device(mask), 0)
                self.copy(g, half, self.shared.at[half, place], self.f).wait_recv()

    def drain(self):
        for half in range(2):
            for number in range(self.rounds + 1):
                for which in self.sends(half, number):
                    self.send(half, *which).wait_send()
                for share in self.shares(half, number):
                    share.wait_send()


def cube_sems(F):
    rounds = F.bit_length() - 2
    return [
        pltpu.SemaphoreType.DMA((2, rounds, F // 4)),
        pltpu.SemaphoreType.DMA((2, F // 2)),
        pltpu.SemaphoreType.DMA((F, 2)),
    ]


def shape(dims, dtype=BF16):
    return jax.ShapeDtypeStruct(tuple(dims), dtype)


def join(a, b):
    return jnp.concatenate([a, b], axis=0)


def side_by_side(ref, *index):
    return jnp.concatenate([ref[(*index, n)] for n in range(ref.shape[len(index)])], axis=1)


def forward_group(j, q_ref, kv_ref, qa_ref, ka_ref, att_ref, lse_ref, o_ref):
    width, rows = att_ref.shape[1:]
    span = q_ref.shape[-1]
    sub = QUERY_BLOCK // span

    def block(i, _):
        cols = pl.ds(pl.multiple_of(i * QUERY_BLOCK, QUERY_BLOCK), QUERY_BLOCK)
        q_t = jnp.concatenate([q_ref[j, i * sub + n] for n in range(sub)], axis=1)
        queries = join(q_t, qa_ref[j, :, cols]).T
        total = jnp.zeros((QUERY_BLOCK, 2 * width), F32)
        for g in range(kv_ref.shape[0]):
            kv = side_by_side(kv_ref, g)
            keys = join(kv[:width], ka_ref[g])
            values = join(kv[width:], jnp.ones((width, rows), BF16))
            weights = jnp.exp(nn(queries, keys)).astype(BF16)
            total += nt(weights, values)
        total = total.T
        weight_sum = total[width : width + 1]
        attended = total[:width] / weight_sum
        att_ref[j, :, cols] = attended
        o_ref[j, :, cols] = attended.astype(BF16)
        lse_ref[j, :, cols] = jnp.log(weight_sum)
        return 0

    lax.fori_loop(0, rows // QUERY_BLOCK, block, 0)


def with_rows(base, first, rows):
    index = lax.broadcasted_iota(jnp.int32, base.shape, 0)
    for n, row in enumerate(rows):
        base = jnp.where(index == first + n, row, base)
    return base


def rms_scale(vector, gain, axis=-1):
    return vector * lax.rsqrt(jnp.mean(vector * vector, axis=axis, keepdims=True) + EPSILON) * gain


def per_device(
    tokens,
    cotangent,
    doc_starts,
    variate_ids,
    time_ids,
    gain_attn,
    w_attn,
    gain_query,
    gain_key,
    variate_bias,
    w_output,
    gain_feed,
    w_gate,
    w_up,
    w_down,
):
    S, F = lax.axis_size("seq"), lax.axis_size("fsdp")
    s, f = lax.axis_index("seq"), lax.axis_index("fsdp")
    rows, width = tokens.shape
    heads = variate_bias.shape[0]
    dim = gain_query.shape[0]
    own_heads = heads // S
    splits = F // own_heads
    group = rows * S
    groups = F // splits
    hidden = w_down.shape[0] * F // S
    half = F // 2
    cut = width // (S * F)
    lanes = own_heads * dim

    def along_seq(s, f):
        return [(lax.rem(s + d, S), f) for d in range(1, S)]

    def along_fsdp(s, f):
        return [(s, lax.rem(f + d, F)) for d in range(1, F)]

    def along_both(s, f):
        return along_seq(s, f) + along_fsdp(s, f)

    def like_parts(s, f):
        return [
            (lax.rem(s + a, S), lax.rem(f + b * splits, F))
            for a in range(S)
            for b in range(groups)
            if a or b
        ]

    def everyone(s, f):
        return [(lax.rem(s + a, S), lax.rem(f + b, F)) for a in range(S) for b in range(F) if a or b]

    def seq_swap(s, f, src, dst):
        remote = [(src.at[t[0]], dst.at[s], t, None, None) for t in along_seq(s, f)]
        return remote, [(src.at[s], dst.at[s], None)]

    per_plane = F // S
    down_rows = w_down.shape[0] // S
    local_rows = w_attn.shape[0]
    whole_tiles = down_rows % 128 == 0

    def unit_place(s, f):
        return lax.rem(f, per_plane) * S + lax.rem(f // per_plane + s, S)

    def unit_block(s, g):
        holder = lax.rem(lax.rem(g, S) - s + S, S) * per_plane + g // S
        return holder * S + lax.rem(g, S)

    def units(w):
        if whole_tiles:
            return w
        blocks = w.reshape(w.shape[0], S * F, down_rows)
        return jnp.concatenate(
            [lax.dynamic_index_in_dim(blocks, unit_block(s, g), 1, False) for g in range(F)], axis=1
        )

    def pair(s, f):
        return (s, flipped(f, 0))

    def same_parity(s, f):
        return [(s, lax.rem(f + 2 * d, F)) for d in range(1, half)]

    def peers_a(s, f):
        return like_parts(s, f) + [(s, lax.rem(f + d, F)) for d in range(1, F) if d % splits]

    block = 256 if width % 256 == 0 and hidden % 256 == 0 else 128

    frequency = (10000.0 ** (-2.0 * jnp.arange(dim // 2, dtype=F32) / dim))[:, None]
    total = F * group

    def kernel_a(
        x_ref, cot_ref, w_ref, wo_ref, wd_ref, wg_ref, wu_ref, times_ref, ids_ref, freq_ref, gain_ref, gain_q_ref, gain_k_ref,
        gain_feed_ref, bias_ref, starts_ref,
        xs_out, ws_out, raw_out, cos_ref, sin_ref, ka_out, qa_out, qs_out, kvs_out, att_out, lse_ref,
        grads_ref, middle_ref, mid_grad_ref, feed_ref, out_hbm, gate_got, up_got, down_hbm, output_half,
        xs_ref, ws_ref, raw_ref, cots_ref, ka_ref, qa_ref, q_ref, kv_ref, att_ref, heads_ref, wos_ref, gates_ref, ups_ref,
        downs_ref, mid_v, n_v, n_t, hid_v, hid_t, gl_v, ul_v, u_ref, from_left, from_right,
        gate_part, up_part, down_part, output_part, gate_other, up_other, down_other, output_other, gate_half, up_half,
        hg_ref, out_ref, down_half, u_sent, u_got, u_sent_, u_got_, pair_sent, pair_got, spread_sent, spread_got, own_sem, f_sent, f_got, out_sem,
        q_out, kv_out, o_ref, gate_own, up_own,
        w_sem, unit_sem, here_sem, x_sent, x_got, c_sent, c_got, kv_sent, kv_shared, kv_got, q_sent, q_got,
        o_sent, h_sent, h_got, *cube_refs,
    ):
        s, f = lax.axis_index("seq"), lax.axis_index("fsdp")
        column, part = f // splits, lax.rem(f, splits)
        loads = []
        for n in range(3):
            src = w_ref.at[:, pl.ds(pl.multiple_of(n * S * lanes + s * lanes, 128), lanes)]
            dst = ws_ref.at[pl.ds(f * local_rows, local_rows), pl.ds(n * lanes, lanes)]
            loads.append(pltpu.make_async_copy(src, dst, w_sem.at[n]))
        unit_loads = []
        for n, (src, dst) in enumerate(((wg_ref, gate_own), (wu_ref, up_own))):
            for g in range(F if whole_tiles else 1):
                if whole_tiles:
                    cols = pl.ds(pl.multiple_of(unit_block(s, g) * down_rows, 128), down_rows)
                    src_, dst_ = src.at[:, cols], dst.at[:, pl.ds(g * down_rows, down_rows)]
                else:
                    src_, dst_ = src, dst
                unit_loads.append(pltpu.make_async_copy(src_, dst_, unit_sem.at[n, g]))
        for load in loads + unit_loads:
            load.start()
        xs_ref[s] = x_ref[...]
        cots_ref[s] = cot_ref[...]
        greet(peers_a(s, f))
        xs = Line(lambda plane, slot: xs_ref.at[plane], (x_sent, x_got), s, f, S)
        cots = Line(lambda plane, slot: cots_ref.at[plane], (c_sent, c_got), s, f, S)
        xs.send(0)

        def rows_of(ref, size, place=lambda g: g):
            return lambda g, half: ref.at[pl.ds(place(g) * size + half * (size // 2), size // 2)]

        def half_of(ref, size):
            return lambda half: ref.at[pl.ds(half * (size // 2), size // 2)]

        down_own = wd_ref.at[lax.rem(f // per_plane + s, S)]
        down_place = unit_place(s, f)
        blocks = (
            (rows_of(ws_ref, local_rows), lambda half: rows_of(ws_ref, local_rows)(f, half)),
            (rows_of(wos_ref, local_rows), half_of(wo_ref, local_rows)),
            (rows_of(gates_ref, local_rows), half_of(gate_own, local_rows)),
            (rows_of(ups_ref, local_rows), half_of(up_own, local_rows)),
            (rows_of(downs_ref, down_rows, lambda g: unit_place(s, g)), half_of(down_own, down_rows)),
        )
        ws, wos, gates, ups, downs = [
            CubeGather(block, own, cube_refs[3 * n : 3 * n + 3], s, f, F) for n, (block, own) in enumerate(blocks)
        ]
        for load in loads:
            load.wait()
        ws.start()
        for load in unit_loads:
            load.wait()
        mine = pl.ds(f * local_rows, local_rows)
        here = [
            pltpu.make_async_copy(wo_ref, wos_ref.at[mine], here_sem.at[0]),
            pltpu.make_async_copy(gate_own, gates_ref.at[mine], here_sem.at[1]),
            pltpu.make_async_copy(up_own, ups_ref.at[mine], here_sem.at[2]),
            pltpu.make_async_copy(down_own, downs_ref.at[pl.ds(down_place * down_rows, down_rows)], here_sem.at[3]),
        ]
        for copy in here:
            copy.start()

        own_cols = pl.ds(pl.multiple_of(f * group, 128), group)
        angles = freq_ref[...] * times_ref[:, own_cols].astype(F32)
        cos_ref[...] = jnp.cos(angles)
        sin_ref[...] = jnp.sin(angles)
        mine_only = lax.broadcasted_iota(jnp.int32, (2, heads), 1) == s * own_heads + column
        biases = jnp.sum(jnp.where(mine_only, bias_ref[...], 0.0), axis=1, keepdims=True)
        difference = pieces(jnp.broadcast_to(biases[0:1] - biases[1:2], (VARIATES, group)))
        index = lax.broadcasted_iota(jnp.int32, (VARIATES, group), 0)

        def marks(g):
            ids = ids_ref[:, pl.ds(pl.multiple_of(g * group, 128), group)]
            positions = g * group + lax.broadcasted_iota(jnp.int32, (VARIATES, group), 1)
            docs = jnp.zeros((VARIATES, group), jnp.int32) - 1
            for n in range(doc_starts.shape[0]):
                docs = docs + (starts_ref[n] <= positions).astype(jnp.int32)
            return (docs == index).astype(F32), (ids == index).astype(F32)

        for g in range(F):
            doc, var = marks(g)
            tail = (index < 3).astype(F32)
            none = jnp.zeros((dim - LSE_ROW - VARIATES, group), F32)
            ka_ref[g] = jnp.concatenate([var, var, var, 1.0 - doc, tail, none]).astype(BF16)
        for j in range(groups):
            doc, var = marks(j * splits + part)
            none = jnp.zeros((VARIATES, group), F32)
            rest = jnp.zeros((dim - VAR_ROW - VARIATES, group), F32)
            scaled = [var * piece for piece in difference]
            qa_ref[j] = jnp.concatenate([*scaled, doc * -AWAY, none, var, rest]).astype(BF16)
        gain_q, gain_k = [
            jnp.broadcast_to(ref[...], (128, dim)).T[:, :rows] for ref in (gain_q_ref, gain_k_ref)
        ]

        def kv_copy(g, b, src, sem, to):
            return pltpu.make_async_remote_copy(
                src_ref=src, dst_ref=kv_ref.at[g, b], send_sem=sem, recv_sem=kv_got.at[g, b],
                device_id=(s, to), device_id_type=MESH,
            )

        def to_heads(b, d):
            to = lax.rem(f + 2 * d, F)
            return kv_copy(f, b, kv_out.at[b, to // splits], kv_sent.at[b, d], to)

        def to_neighbour(b, d):
            g = lax.rem(f + 2 * d, F)
            src = kv_ref.at[g, b] if d else kv_out.at[b, column]
            return kv_copy(g, b, src, kv_shared.at[b, d], flipped(f, 0))

        def queries_to_heads(b, d):
            to = lax.rem(f + d * splits, F)
            return pltpu.make_async_remote_copy(
                src_ref=q_out.at[b, to // splits], dst_ref=q_ref.at[column, b], send_sem=q_sent.at[b, d],
                recv_sem=q_got.at[column, b], device_id=(s, to), device_id_type=MESH,
            )

        def project(b):
            normed = rms_scale(xs_ref[b].astype(F32), gain_ref[...]).astype(BF16)
            projected = nn(normed, ws_ref[...]).T.reshape(3, own_heads, dim, rows)
            cols = pl.ds(pl.multiple_of(b * rows, rows), rows)
            cosine, sine = cos_ref[:, cols], sin_ref[:, cols]

            def turned(raw, gain):
                raw = rms_scale(raw, gain, axis=1)
                front, back = raw[:, : dim // 2], raw[:, dim // 2 :]
                return jnp.concatenate(
                    [front * cosine - back * sine, front * sine + back * cosine], axis=1
                )

            raw_ref[0, :, :, cols] = projected[0]
            raw_ref[1, :, :, cols] = projected[1]
            q_out[b] = (turned(projected[0], gain_q).astype(BF16).astype(F32) * dim**-0.5).astype(BF16)
            kv_out[b, :, :dim] = turned(projected[1], gain_k).astype(BF16)
            kv_out[b, :, dim:] = projected[2].astype(BF16)
            for d in range(1, half):
                to_heads(b, d).start()
            for d in range(1, groups):
                queries_to_heads(b, d).start()
            to_neighbour(b, 0).start()
            kv_ref[f, b] = kv_out[b, column]
            q_ref[column, b] = q_out[b, column]

        def share(b):
            for d in range(1, half):
                to_neighbour(b, d).wait_recv()
                to_neighbour(b, d).start()

        wos.start()
        gates.start()
        ws.step(1)
        wos.step(1)
        gates.step(1)
        for number in range(2, ws.rounds + 1):
            ws.step(number)
        ws.finish()
        project(s)
        for distance in range(1, S):
            xs.arrive(0, distance)
            cots.follow(0, distance)
            pl.when(s - distance >= 0)(lambda distance=distance: project(s - distance))
            pl.when(s + distance < S)(lambda distance=distance: project(s + distance))

        def share_all(b, _):
            share(b)
            return 0

        for time in range(S, 2 * S - 2):
            if time == (3 * S - 2) // 2:
                lax.fori_loop(0, S, share_all, 0)
            cots.follow(0, time)

        def last(b, _):
            for d in range(half):
                g = lax.rem(flipped(f, 0) + 2 * d, F)
                kv_copy(g, b, kv_ref.at[g, b], kv_shared.at[b, d], f).wait_recv()
            for d in range(1, groups):
                g = lax.rem(f + d * splits, F)
                pltpu.make_async_remote_copy(
                    src_ref=q_out.at[b, 0], dst_ref=q_ref.at[g // splits, b], send_sem=q_sent.at[b, d],
                    recv_sem=q_got.at[g // splits, b], device_id=(s, g), device_id_type=MESH,
                ).wait_recv()
            return 0

        lax.fori_loop(0, S, last, 0)
        ups.start()
        downs.start()

        own = s * own_heads + column

        def to_column(turn):
            j = lax.rem(column + turn, groups)
            return pltpu.make_async_remote_copy(
                src_ref=o_ref.at[j], dst_ref=heads_ref.at[own], send_sem=o_sent.at[turn], recv_sem=h_got.at[turn, 0],
                device_id=(s, j * splits + part), device_id_type=MESH,
            )

        def along(turn, d):
            ref = heads_ref.at[s * own_heads + lax.rem(column - turn + groups, groups)]
            return pltpu.make_async_remote_copy(
                src_ref=ref, dst_ref=ref, send_sem=h_sent.at[turn, d], recv_sem=h_got.at[turn, d],
                device_id=(lax.rem(s + d, S), f), device_id_type=MESH,
            )

        for turn in range(groups + 1):
            if turn < groups:
                j = lax.rem(column + turn, groups)
                forward_group(j, q_ref, kv_ref, qa_ref, ka_ref, att_ref, lse_ref, o_ref)
                if turn:
                    to_column(turn).start()
                else:
                    heads_ref[own] = o_ref[j]
            if turn != 1:
                came = max(turn - 1, 0)
                if came:
                    to_column(came).wait_recv()
                for d in range(1, S):
                    along(came, d).start()
            if turn == 0:
                for number in range(2, wos.rounds + 1):
                    wos.step(number)
                    gates.step(number)
            if turn == 3:
                ups.step(1)
                downs.step(1)
        for number in range(2, ups.rounds + 1):
            ups.step(number)
            downs.step(number)

        flushes = [
            pltpu.make_async_copy(src, dst, out_sem.at[n])
            for n, (src, dst) in enumerate(
                (
                    (xs_ref, xs_out), (ws_ref, ws_out), (raw_ref, raw_out), (ka_ref, ka_out), (qa_ref, qa_out),
                    (q_ref, qs_out), (kv_ref, kvs_out), (att_ref, att_out),
                )
            )
        ]
        for flush in flushes:
            flush.start()
        for turn in range(groups):
            for d in range(1, S):
                along(turn, d).wait_recv()
        for copy_ in here:
            copy_.wait()
        cots.follow_end(0)
        wos.finish()

        def copy(src, dst, sent, got, to):
            return pltpu.make_async_remote_copy(
                src_ref=src, dst_ref=dst, send_sem=sent, recv_sem=got, device_id=to, device_id_type=MESH
            )

        heads_rows = heads_ref[...].reshape(heads * dim, group).T
        for c in range(0, width, block):
            cs = slice(c, c + block)
            mid_v[:, cs] = xs_ref[:, :, cs].astype(F32).reshape(group, block) + nn(heads_rows, wos_ref[:, cs])
        normed = rms_scale(mid_v[...], gain_feed_ref[...]).astype(BF16)
        n_v[...] = normed
        n_t[...] = normed.T
        for gather in (gates, ups, downs):
            gather.finish()
        cot_rows = cots_ref[...].reshape(group, width)
        for c in range(0, hidden, block):
            cs = slice(c, c + block)
            gate_act, up_act = nn(n_v[...], gates_ref[:, cs]), nn(n_v[...], ups_ref[:, cs])
            hidden_grad = nt(cot_rows, downs_ref[cs, :])
            sigmoid = jax.nn.sigmoid(gate_act)
            silu = gate_act * sigmoid
            hidden_low = (silu * up_act).astype(BF16)
            hid_v[:, cs] = hidden_low
            hid_t[cs, :] = hidden_low.T
            gl_v[:, cs] = (hidden_grad * up_act * sigmoid * (1.0 + gate_act * (1.0 - sigmoid))).astype(BF16)
            ul_v[:, cs] = (hidden_grad * silu).astype(BF16)
        for c in range(0, width, block):
            cs = slice(c, c + block)
            grad = nt(gl_v[...], gates_ref[cs, :]) + nt(ul_v[...], ups_ref[cs, :])
            u_ref[:, :, cs] = grad.astype(BF16).reshape(S, rows, block)
        u_sems = (u_sent, u_got, u_sent_, u_got_)
        mid_sum = LineSums(u_ref, from_left, from_right, u_sems, s, f, S)
        mid_sum.step(0)

        parity = lax.rem(f, 2)
        by_owner = (S, half, 2, cut, block)

        def exchange_halves(n, part, other):
            away = part.at[:, 1 - parity] if len(part.shape) == 4 else part.at[:, :, 1 - parity]
            send = copy(away, other, pair_sent.at[n], pair_got.at[n], pair(s, f))
            send.start()
            return send

        for c in range(0, hidden, block):
            cs = slice(c, c + block)
            gate_part[..., cs] = nn(n_t[...], gl_v[:, cs]).astype(BF16).reshape(by_owner)
        swaps = [exchange_halves(0, gate_part, gate_other)]
        for c in range(0, hidden, block):
            cs = slice(c, c + block)
            up_part[..., cs] = nn(n_t[...], ul_v[:, cs]).astype(BF16).reshape(by_owner)
        swaps.append(exchange_halves(1, up_part, up_other))
        for c in range(0, width, block):
            cs = slice(c, c + block)
            down_part[..., cs] = nn(hid_t[...], cots_ref[:, :, cs].reshape(group, block)).astype(BF16).reshape(half, 2, down_rows, block)
        swaps.append(exchange_halves(2, down_part, down_other))
        for c in range(0, width, block):
            cs = slice(c, c + block)
            out_ref[:, :, cs] = nn(hid_v[...], downs_ref[:, cs]).astype(BF16).reshape(S, rows, block)

        def spread(n, halves, got):
            here = pltpu.make_async_copy(halves.at[:, f // 2], got.at[f // 2], own_sem.at[n])
            here.start()
            sends = []
            for d, to in enumerate(same_parity(s, f)):
                send = copy(halves.at[:, to[1] // 2], got.at[f // 2], spread_sent.at[n, d], spread_got.at[n, d], to)
                send.start()
                sends.append(send)
            return here, sends

        def add(a, b):
            return (a.astype(F32) + b.astype(F32)).astype(BF16)

        swaps[0].wait_recv()
        gate_half[...] = add(gate_part[:, :, parity], gate_other[...])
        spreads = [spread(0, gate_half, gate_got)]
        mid_sum.step(1)
        swaps[1].wait_recv()
        up_half[...] = add(up_part[:, :, parity], up_other[...])
        spreads.append(spread(1, up_half, up_got))
        swaps[2].wait_recv()
        down_half[...] = add(down_part[:, parity], down_other[...])
        for src, dst in ((out_ref, out_hbm), (down_half, down_hbm)):
            flushes.append(pltpu.make_async_copy(src, dst, out_sem.at[len(flushes)]))
            flushes[-1].start()
        for time in range(2, S):
            mid_sum.step(time)

        middle = mid_v[pl.ds(pl.multiple_of(s * rows, rows), rows), :]
        grad = u_ref[s].astype(F32)
        inverse = lax.rsqrt(jnp.mean(middle * middle, axis=1, keepdims=True) + EPSILON)
        scaled = grad * gain_feed_ref[...]
        mean = jnp.mean(scaled * middle, axis=1, keepdims=True)
        own_cot = cots_ref[s].astype(F32)
        middle_grad = own_cot + inverse * scaled - middle * (inverse**3 * mean)
        middle_low = middle_grad.astype(BF16)
        hg_ref[...] = nt(wos_ref[...], middle_low).astype(BF16).reshape(heads, dim, rows)

        place = grads_ref.at[f // splits, s]
        grads_here = pltpu.make_async_copy(hg_ref.at[s * own_heads + f // splits], place, own_sem.at[2])
        grads_here.start()
        sends = []
        for n, to in enumerate(like_parts(s, f)):
            send = copy(hg_ref.at[to[0] * own_heads + to[1] // splits], place, f_sent.at[n], f_got.at[n], to)
            send.start()
            sends.append(send)

        middle_ref[...] = middle
        mid_grad_ref[...] = middle_grad
        feed_ref[...] = jnp.sum(grad * middle * inverse, axis=0, keepdims=True)
        own_heads_t = heads_ref[:, :, pl.ds(pl.multiple_of(s * rows, rows), rows)].reshape(heads * dim, rows)
        for c in range(0, width, block):
            cs = slice(c, c + block)
            output_part[..., cs] = nn(own_heads_t, middle_low[:, cs]).astype(BF16).reshape(by_owner)
        swaps.append(exchange_halves(3, output_part, output_other))
        swaps[3].wait_recv()
        output_half[...] = add(output_part[:, :, parity], output_other[...])
        grads_here.wait()
        for send in sends:
            send.wait()
        for here, others in spreads:
            here.wait()
            for send in others:
                send.wait()
        for swap in swaps:
            swap.wait_send()
        mid_sum.drain()

        for flush in flushes:
            flush.wait()
        def sent(b, _):
            for d in range(half):
                if d:
                    to_heads(b, d).wait_send()
                to_neighbour(b, d).wait_send()
            for d in range(1, groups):
                queries_to_heads(b, d).wait_send()
            return 0

        lax.fori_loop(0, S, sent, 0)
        xs.drain(0)
        cots.drain(0)
        ws.drain()
        for turn in range(groups):
            if turn:
                to_column(turn).wait_send()
            for d in range(1, S):
                along(turn, d).wait_send()
        for gather in (wos, gates, ups, downs):
            gather.drain()

    dma = pltpu.SemaphoreType.DMA
    wide = (S, half, 2, cut, hidden)
    wide_half = (S, half, cut, hidden)
    kept = [
        shape((S, rows, width)),
        shape((width, 3 * lanes)),
        shape((2, own_heads, dim, group), F32),
        shape((F, dim, group)),
        shape((groups, dim, group)),
        shape((groups, S, dim, rows)),
        shape((F, S, 2 * dim, rows)),
        shape((groups, dim, group), F32),
    ]
    (
        x_parts, w_qkv, raw, cosine, sine, key_marks, query_marks, q_all, kv_all, attended, log_sum,
        grad_heads, own_middle, middle_grad, feed_gain, out_part, gate_got, up_got, down_half, output_half,
    ) = pl.pallas_call(
        kernel_a,
        in_specs=[VMEM] * 2 + [ANY] * 5 + [VMEM] * 8 + [pl.BlockSpec(memory_space=pltpu.SMEM)],
        out_specs=[ANY] * 3 + [VMEM] * 2 + [ANY] * 5 + [VMEM] + [ANY] + [VMEM] * 3 + [ANY] * 4 + [VMEM],
        out_shape=[
            *kept[:3],
            shape((dim // 2, group), F32),
            shape((dim // 2, group), F32),
            *kept[3:],
            shape((groups, 1, group), F32),
            shape((groups, S, dim, rows)),
            shape((rows, width), F32),
            shape((rows, width), F32),
            shape((1, width), F32),
            shape((S, rows, width)),
            shape((half, S, cut, hidden)),
            shape((half, S, cut, hidden)),
            shape((half, down_rows, width)),
            shape((S, half, cut, width)),
        ],
        scratch_shapes=[
            *[pltpu.VMEM(kept[n].shape, kept[n].dtype) for n in range(3)],
            pltpu.VMEM((S, rows, width), BF16),
            *[pltpu.VMEM(one.shape, one.dtype) for one in kept[3:]],
            pltpu.VMEM((heads, dim, group), BF16),
            pltpu.VMEM((heads * dim, width), BF16),
            pltpu.VMEM((width, hidden), BF16),
            pltpu.VMEM((width, hidden), BF16),
            pltpu.VMEM((hidden, width), BF16),
            pltpu.VMEM((group, width), F32),
            pltpu.VMEM((group, width), BF16),
            pltpu.VMEM((width, group), BF16),
            pltpu.VMEM((group, hidden), BF16),
            pltpu.VMEM((hidden, group), BF16),
            pltpu.VMEM((group, hidden), BF16),
            pltpu.VMEM((group, hidden), BF16),
            *[pltpu.VMEM((S, rows, width), BF16)] * 3,
            *[pltpu.VMEM(wide, BF16)] * 2,
            pltpu.VMEM((half, 2, down_rows, width), BF16),
            pltpu.VMEM((S, half, 2, cut, width), BF16),
            *[pltpu.VMEM(wide_half, BF16)] * 2,
            pltpu.VMEM((half, down_rows, width), BF16),
            pltpu.VMEM((S, half, cut, width), BF16),
            *[pltpu.VMEM(wide_half, BF16)] * 2,
            pltpu.VMEM((heads, dim, rows), BF16),
            pltpu.VMEM((S, rows, width), BF16),
            pltpu.VMEM((half, down_rows, width), BF16),
            *[dma((2, S))] * 4,
            *[dma((4,))] * 2,
            *[dma((2, half))] * 2,
            dma((3,)),
            *[dma((S * groups,))] * 2,
            dma((len(kept) + 2,)),
            pltpu.VMEM((S, own_heads, dim, rows), BF16),
            pltpu.VMEM((S, own_heads, 2 * dim, rows), BF16),
            pltpu.VMEM((groups, dim, group), BF16),
            pltpu.VMEM((local_rows, hidden), BF16),
            pltpu.VMEM((local_rows, hidden), BF16),
            dma((3,)),
            dma((2, F)),
            dma((4,)),
            *line_sems(S, 1),
            *line_sems(S, 1),
            dma((S, half)),
            dma((S, half)),
            dma((F, S)),
            dma((S, groups)),
            dma((groups, S)),
            dma((groups,)),
            dma((groups, S)),
            dma((groups, S)),
            *[sem for _ in range(5) for sem in cube_sems(F)],
        ],
        compiler_params=pltpu.CompilerParams(
            collective_id=0, has_side_effects=True, vmem_limit_bytes=VMEM_BYTES
        ),
        cost_estimate=pl.CostEstimate(flops=2 * 10**10, bytes_accessed=10**8, transcendentals=10**7),
    )(
        tokens,
        cotangent,
        w_attn,
        w_output,
        w_down.reshape(S, down_rows, width),
        units(w_gate),
        units(w_up),
        time_ids[None, :],
        variate_ids[None, :],
        frequency,
        gain_attn[None, :],
        gain_query[None, :],
        gain_key[None, :],
        gain_feed[None, :],
        variate_bias.T,
        doc_starts,
    )

    chunks = width // 128
    blocks = group // QUERY_BLOCK
    span = QUERY_BLOCK // rows
    small_rows = 8

    def kernel_g(
        q_ref, kv_ref, qa_ref, ka_ref, do_ref, att_ref, lse_ref, cos_ref, sin_ref, gain_q_ref, gain_k_ref, feed_ref,
        gain_ref, out_half, down_half, out_hbm, gate_hbm, up_hbm, raw_hbm, ws_hbm, xs_hbm,
        u_own, w_rows, gate_rows, up_rows, out_rows, down_moved, layer_own, vec_got,
        out_got, down_got, gate_got, up_got,
        qq_ref, dd_ref, dq_sum, kv_sum, kv_send, kv_other, dq_send, dqs, dkvs, gate_sum, up_sum, out_sum, down_sum,
        layer_ref, layer_left, layer_right, raw_ref, ws_ref, xs_ref, pg_ref, u_ref, from_left, from_right, w_part, w_other,
        w_half, w_got, w_sum, vec, normed_t, bias_ref,
        load_sem, own_sem, spread_sent, spread_got, layer_sent, layer_got, swap_sent, swap_got, pair_sent, pair_got,
        dkv_sent, dkv_got, dq_sent, dq_got, u_sent, u_got, u_sent_, u_got_, half_sent, half_got, w_sent, w_arrived, rows_sent, rows_got, vec_sent, vec_arrived,
        down_sent, down_arrived,
    ):
        s, f = lax.axis_index("seq"), lax.axis_index("fsdp")
        column, part, parity = f // splits, lax.rem(f, splits), lax.rem(f, 2)

        def copy(src, dst, sent, got, to):
            return pltpu.make_async_remote_copy(
                src_ref=src, dst_ref=dst, send_sem=sent, recv_sem=got, device_id=to, device_id_type=MESH
            )

        loads = [
            pltpu.make_async_copy(src, dst, load_sem.at[n])
            for n, (src, dst) in enumerate(
                (
                    (out_hbm, layer_ref), (gate_hbm, gate_got), (up_hbm, up_got), (raw_hbm, raw_ref), (ws_hbm, ws_ref),
                    (xs_hbm, xs_ref),
                )
            )
        ]
        for load in loads:
            load.start()
        greet(everyone(s, f))

        spreads = []
        for n, (src, got) in enumerate(((out_half, out_got), (down_half, down_got))):
            pick = (lambda ref, g: ref.at[:, g]) if n == 0 else (lambda ref, g: ref.at[g])
            here = pltpu.make_async_copy(pick(src, f // 2), got.at[f // 2], own_sem.at[n])
            here.start()
            sends = []
            for d, to in enumerate(same_parity(s, f)):
                sends.append(copy(pick(src, to[1] // 2), got.at[f // 2], spread_sent.at[n, d], spread_got.at[n, d], to))
                sends[-1].start()
            spreads.append((here, sends))
        layer = LineSum(layer_ref, layer_left, layer_right, (layer_sent, layer_got), s, f, S)
        loads[0].wait()
        layer.step(0)
        swaps = []

        def swap_rows(n, got, total, rows_ref):
            total[...] = jnp.sum(got[...].astype(F32), axis=0).astype(BF16)
            rows_ref[s] = total[s]
            for d in range(1, S):
                to = lax.rem(s + d, S)
                swaps.append(copy(total.at[to], rows_ref.at[s], swap_sent.at[n, d], swap_got.at[n, d], (to, f)))
                swaps[-1].start()

        for load in loads[1:3]:
            load.wait()
        swap_rows(0, gate_got, gate_sum, gate_rows)
        swap_rows(1, up_got, up_sum, up_rows)

        def rows_at(i):
            return pl.ds(pl.multiple_of(i * QUERY_BLOCK, QUERY_BLOCK), QUERY_BLOCK)

        def tokens_of(ref, i):
            j, first = i // blocks, (i % blocks) * span
            return jnp.concatenate([ref[j, first + n] for n in range(span)], axis=1)

        def ready(i, _):
            j, cols = i // blocks, rows_at(i % blocks)
            marks = qa_ref[j, :, cols].astype(F32)
            extra = with_rows(marks, LSE_ROW, pieces(-lse_ref[j, :, cols])).astype(BF16)
            qq_ref[rows_at(i), :] = join(tokens_of(q_ref, i), extra).T
            grad_t = tokens_of(do_ref, i)
            delta = jnp.sum(grad_t.astype(F32) * att_ref[j, :, cols], axis=0, keepdims=True)
            extra = with_rows(jnp.zeros((dim, QUERY_BLOCK), F32), 0, pieces(-delta)).astype(BF16)
            dd_ref[rows_at(i), :] = join(grad_t, extra).T
            return 0

        lax.fori_loop(0, groups * blocks, ready, 0)
        dq_sum[...] = jnp.zeros_like(dq_sum)

        def key_group(g):
            kv = side_by_side(kv_ref, g)
            keys = join(kv[:dim], ka_ref[g])
            values = join(kv[dim:], jnp.ones((dim, group), BF16))
            kv_sum[...] = jnp.zeros_like(kv_sum)
            for i in range(groups * blocks):
                q_rows = slice(i * QUERY_BLOCK, (i + 1) * QUERY_BLOCK)
                probs = jnp.exp(nn(qq_ref[q_rows, :], keys))
                score_grad = (probs * nn(dd_ref[q_rows, :], values)).astype(BF16)
                kv_sum[dim:, :] += nn(tokens_of(do_ref, i), probs.astype(BF16))
                kv_sum[:dim, :] += nn(tokens_of(q_ref, i), score_grad)
                dq_sum[q_rows, :] += nt(score_grad, keys)

        def to_pair(i):
            return copy(kv_send.at[0, i], kv_other.at[i], pair_sent.at[i], pair_got.at[i], (s, flipped(f, 0)))

        def to_owner(i):
            to = lax.rem(f + 2 * (i + 1), F)
            return copy(kv_send.at[1, i], dkvs.at[f // 2], dkv_sent.at[i], dkv_got.at[i], (s, to))

        def others(i, _):
            key_group(lax.rem(flipped(f, 0) + 2 * (i + 1), F))
            kv_send[0, i] = kv_sum[...].astype(BF16)
            to_pair(i).start()
            return 0

        lax.fori_loop(0, half, others, 0)
        layer.step(1)
        here, sends = spreads[0]
        here.wait()
        for send in sends:
            send.wait_recv()
        swap_rows(2, out_got, out_sum, out_rows)

        def owns(i, _):
            key_group(lax.rem(f + 2 * (i + 1), F))
            to_pair(i).wait_recv()
            kv_send[1, i] = (kv_sum[...] + kv_other[i].astype(F32)).astype(BF16)
            pl.when(i < half - 1)(lambda: to_owner(i).start())
            return 0

        lax.fori_loop(0, half, owns, 0)
        dkvs[f // 2] = kv_send[1, half - 1]
        layer.step(2)

        bias_ref[...] = jnp.zeros_like(bias_ref)

        def dq_copy(d):
            to = lax.rem(f + d * splits, F)
            return copy(dq_send.at[to // splits], dqs.at[column], dq_sent.at[d], dq_got.at[d], (s, to))

        def queries_done(i, _):
            j, cols = i // blocks, rows_at(i % blocks)
            dq_t = dq_sum[rows_at(i), :].T
            dq_send[j, :, cols] = (dq_t[:dim] * dim**-0.5).astype(BF16)
            by_variate = dq_t[dim : dim + VARIATES]
            bias_ref[0] += by_variate * qa_ref[j, VAR_ROW : VAR_ROW + VARIATES, cols].astype(F32)
            bias_ref[1] += by_variate
            return 0

        lax.fori_loop(0, groups * blocks, queries_done, 0)
        for d in range(1, groups):
            dq_copy(d).start()
        dqs[column] = dq_send[column]
        here, sends = spreads[1]
        here.wait()
        for send in sends:
            send.wait_recv()
        to_plane = lax.rem(lax.rem(f, S) - s + S, S)
        down_sum[...] = jnp.sum(down_got[...].astype(F32), axis=0).astype(BF16)
        down_move = copy(down_sum, down_moved, down_sent, down_arrived, (to_plane, f))
        pl.when(to_plane != s)(down_move.start)

        @pl.when(to_plane == s)
        def _():
            down_moved[...] = down_sum[...]

        same = jnp.sum(bias_ref[0], keepdims=True)
        other = jnp.sum(bias_ref[1], keepdims=True) - same
        mine = lax.broadcasted_iota(jnp.int32, (1, 128), 1) == s * own_heads + column
        bias_tile = jnp.concatenate([jnp.where(mine, same, 0.0), jnp.where(mine, other, 0.0)])

        for load in loads[3:]:
            load.wait()
        for time in range(3, S):
            layer.step(time)
        layer_own[...] = layer_ref[s]
        x = xs_ref[...].astype(F32).reshape(group, width)
        inverse = lax.rsqrt(jnp.mean(x * x, axis=1, keepdims=True) + EPSILON)
        normed_t[...] = (x * inverse * gain_ref[...]).astype(BF16).T
        for i in range(half - 1):
            to_owner(i).wait_recv()

        cosine, sine = cos_ref[...], sin_ref[...]
        gain_q, gain_k = [
            jnp.broadcast_to(ref[...], (128, dim)).T[:, :1] for ref in (gain_q_ref, gain_k_ref)
        ]

        def prepare_back(grad, raw, gain):
            front, back = grad[: dim // 2], grad[dim // 2 :]
            grad = join(front * cosine + back * sine, back * cosine - front * sine)
            inverse = lax.rsqrt(jnp.mean(raw * raw, axis=0, keepdims=True) + EPSILON)
            scaled = grad * gain
            mean = jnp.mean(scaled * raw, axis=0, keepdims=True)
            return inverse * scaled - raw * (inverse**3 * mean), grad * raw * inverse

        def gain_row(terms):
            folded = terms[:, :128]
            for n in range(1, group // 128):
                folded = folded + terms[:, n * 128 : (n + 1) * 128]
            return jnp.sum(folded.T, axis=0, keepdims=True)

        key_terms = jnp.zeros((dim, group), F32)
        for h in range(own_heads):
            kv_grad = dkvs[h * (splits // 2)].astype(F32)
            for n in range(1, splits // 2):
                kv_grad = kv_grad + dkvs[h * (splits // 2) + n].astype(F32)
            kv_grad = kv_grad.astype(BF16).astype(F32)
            back, terms = prepare_back(kv_grad[:dim], raw_ref[1, h], gain_k)
            key_terms += terms
            pg_ref[:, pl.ds(lanes + h * dim, dim)] = back.T.astype(BF16)
            pg_ref[:, pl.ds(2 * lanes + h * dim, dim)] = kv_grad[dim:].T.astype(BF16)
        for d in range(1, groups):
            dq_copy(d).wait_recv()
        query_terms = jnp.zeros((dim, group), F32)
        for h in range(own_heads):
            back, terms = prepare_back(dqs[h].astype(F32), raw_ref[0, h], gain_q)
            query_terms += terms
            pg_ref[:, pl.ds(h * dim, dim)] = back.T.astype(BF16)

        attn_gain = []
        for c in range(0, width, block):
            cs = slice(c, c + block)
            grad = nt(pg_ref[...], ws_ref[cs, :])
            scaled = xs_ref[:, :, cs].astype(F32).reshape(group, block) * inverse
            attn_gain.append(jnp.sum(grad * scaled, axis=0, keepdims=True))
            u_ref[:, :, cs] = grad.astype(BF16).reshape(S, rows, block)
        attn_gain = jnp.concatenate(attn_gain, axis=1)
        normed_sum = LineSums(u_ref, from_left, from_right, (u_sent, u_got, u_sent_, u_got_), s, f, S)
        normed_sum.step(0)

        step = 256 if 3 * lanes % 256 == 0 else 128
        for c in range(0, 3 * lanes, step):
            cs = slice(c, c + step)
            terms = nn(normed_t[...], pg_ref[:, cs]).astype(BF16)
            w_part[..., cs] = terms.reshape(S, half, 2, cut, step)
        to_other = copy(w_part.at[:, :, 1 - parity], w_other, half_sent, half_got, (s, flipped(f, 0)))
        to_other.start()
        gains = jnp.concatenate([gain_row(query_terms), gain_row(key_terms)], axis=1)
        gains = jnp.concatenate([gains, jnp.zeros((1, 256 - 2 * dim), F32)], axis=1)[:, :128]
        for n in range(chunks):
            lanes_ = slice(n * 128, (n + 1) * 128)
            vec[n] = jnp.concatenate(
                [attn_gain[:, lanes_], feed_ref[:, lanes_], gains, bias_tile, jnp.zeros((3, 128), F32)]
            )
        me = s * F + f
        vec_got[me] = vec[me * cut // 128]
        small = []
        for n, to in enumerate(everyone(s, f)):
            chunk = (to[0] * F + to[1]) * cut // 128
            small.append(copy(vec.at[chunk], vec_got.at[me], vec_sent.at[n], vec_arrived.at[n], to))
            small[-1].start()

        to_other.wait()
        w_half[...] = (w_part[:, :, parity].astype(F32) + w_other[...].astype(F32)).astype(BF16)
        w_got[f // 2] = w_half[:, f // 2]
        w_sends = []
        for d, to in enumerate(same_parity(s, f)):
            w_sends.append(copy(w_half.at[:, to[1] // 2], w_got.at[f // 2], w_sent.at[d], w_arrived.at[d], to))
            w_sends[-1].start()
        for time in range(1, S - 1):
            normed_sum.step(time)
        for send in w_sends:
            send.wait_recv()
        w_sum[...] = jnp.sum(w_got[...].astype(F32), axis=0).astype(BF16)
        w_rows[s] = w_sum[s]
        last = []
        for d in range(1, S):
            to = lax.rem(s + d, S)
            last.append(copy(w_sum.at[to], w_rows.at[s], rows_sent.at[d], rows_got.at[d], (to, f)))
            last[-1].start()
        normed_sum.step(S - 1)
        u_own[...] = u_ref[s]

        for send in swaps + small + last:
            send.wait()
        for send in w_sends:
            send.wait_send()
        pl.when(to_plane != s)(down_move.wait)
        for _, sends in spreads:
            for send in sends:
                send.wait_send()
        for i in range(half):
            to_pair(i).wait_send()
            if i < half - 1:
                to_owner(i).wait_send()
        for d in range(1, groups):
            dq_copy(d).wait_send()
        layer.drain()
        normed_sum.drain()

    u_own, w_rows, gate_rows, up_rows, out_rows, down_moved, layer_own, vec_got = pl.pallas_call(
        kernel_g,
        in_specs=[VMEM] * 13 + [ANY] * 8,
        out_specs=[VMEM] * 8,
        out_shape=[
            shape((rows, width)),
            shape((S, cut, 3 * lanes)),
            shape((S, cut, hidden)),
            shape((S, cut, hidden)),
            shape((S, cut, width)),
            shape((down_rows, width)),
            shape((rows, width)),
            shape((S * F, small_rows, 128), F32),
        ],
        scratch_shapes=[
            pltpu.VMEM((half, S, cut, width), BF16),
            pltpu.VMEM((half, down_rows, width), BF16),
            pltpu.VMEM((half, S, cut, hidden), BF16),
            pltpu.VMEM((half, S, cut, hidden), BF16),
            *[pltpu.VMEM((groups * group, 2 * dim), BF16)] * 2,
            pltpu.VMEM((groups * group, 2 * dim), F32),
            pltpu.VMEM((2 * dim, group), F32),
            pltpu.VMEM((2, half, 2 * dim, group), BF16),
            pltpu.VMEM((half, 2 * dim, group), BF16),
            pltpu.VMEM((groups, dim, group), BF16),
            pltpu.VMEM((own_heads, dim, group), BF16),
            pltpu.VMEM((half, 2 * dim, group), BF16),
            pltpu.VMEM((S, cut, hidden), BF16),
            pltpu.VMEM((S, cut, hidden), BF16),
            pltpu.VMEM((S, cut, width), BF16),
            pltpu.VMEM((down_rows, width), BF16),
            *[pltpu.VMEM((S, rows, width), BF16)] * 3,
            pltpu.VMEM((2, own_heads, dim, group), F32),
            pltpu.VMEM((width, 3 * lanes), BF16),
            pltpu.VMEM((S, rows, width), BF16),
            pltpu.VMEM((group, 3 * lanes), BF16),
            *[pltpu.VMEM((S, rows, width), BF16)] * 3,
            pltpu.VMEM((S, half, 2, cut, 3 * lanes), BF16),
            pltpu.VMEM((S, half, cut, 3 * lanes), BF16),
            pltpu.VMEM((S, half, cut, 3 * lanes), BF16),
            pltpu.VMEM((half, S, cut, 3 * lanes), BF16),
            pltpu.VMEM((S, cut, 3 * lanes), BF16),
            pltpu.VMEM((chunks, small_rows, 128), F32),
            pltpu.VMEM((width, group), BF16),
            pltpu.VMEM((2, VARIATES, QUERY_BLOCK), F32),
            dma((6,)),
            dma((2,)),
            *[dma((2, half))] * 2,
            *[dma((2, S))] * 2,
            *[dma((3, S))] * 2,
            *[dma((half,))] * 2,
            *[dma((half,))] * 2,
            *[dma((groups,))] * 2,
            *[dma((2, S))] * 4,
            dma,
            dma,
            *[dma((half,))] * 2,
            *[dma((S,))] * 2,
            *[dma((S * F,))] * 2,
            dma,
            dma,
        ],
        compiler_params=pltpu.CompilerParams(
            collective_id=1, has_side_effects=True, vmem_limit_bytes=VMEM_BYTES
        ),
    )(
        q_all, kv_all, query_marks, key_marks, grad_heads, attended, log_sum, cosine, sine, gain_query[None, :],
        gain_key[None, :], feed_gain, gain_attn[None, :], output_half, down_half, out_part, gate_got, up_got, raw, w_qkv,
        x_parts,
    )

    def kernel_z(
        x_ref, middle_ref, mid_grad_ref, u_ref, w_ref, gate_rows, up_rows, out_rows, down_ref, layer_ref, vec_ref, gain_ref,
        layer_out, tokens_out, attn_out, output_out, gate_out, up_out, down_out, attn_gain, feed_gain, gain_q, gain_k, bias,
    ):
        s, f = lax.axis_index("seq"), lax.axis_index("fsdp")
        layer_out[...] = (middle_ref[...] + layer_ref[...].astype(F32)).astype(BF16)
        x, grad = x_ref[...].astype(F32), u_ref[...].astype(F32)
        inverse = lax.rsqrt(jnp.mean(x * x, axis=1, keepdims=True) + EPSILON)
        scaled = grad * gain_ref[...]
        mean = jnp.mean(scaled * x, axis=1, keepdims=True)
        tokens_out[...] = mid_grad_ref[...] + inverse * scaled - x * (inverse**3 * mean)
        for n in range(S):
            for part in range(3):
                place = part * S * lanes + n * lanes
                attn_out[:, place : place + lanes] = w_ref[n, :, part * lanes : (part + 1) * lanes].astype(F32)
            for g in range(F):
                holder = (g % S - n) % S * per_plane + g // S
                place = (holder * S + g % S) * down_rows
                cols = slice(g * down_rows, (g + 1) * down_rows)
                gate_out[:, place : place + down_rows] = gate_rows[n, :, cols].astype(F32)
                up_out[:, place : place + down_rows] = up_rows[n, :, cols].astype(F32)
        output_out[...] = jnp.sum(out_rows[...].astype(F32), axis=0)
        down_out[...] = down_ref[...].astype(F32)
        sums = jnp.sum(vec_ref[...], axis=0)
        place = lax.rem((s * F + f) * cut, 128)
        for row, ref in ((0, attn_gain), (1, feed_gain)):
            picked = jnp.zeros((1, cut), F32)
            for n in range(0, 128, cut):
                picked = picked + jnp.where(place == n, sums[row : row + 1, n : n + cut], 0.0)
            ref[...] = picked
        gain_q[...] = sums[2:3, :dim]
        gain_k[...] = sums[2:3, dim : 2 * dim]
        bias[...] = sums[3:5, :heads]

    out = pl.pallas_call(
        kernel_z,
        in_specs=[VMEM] * 12,
        out_specs=[VMEM] * 12,
        out_shape=[
            shape((rows, width)),
            shape((rows, width), F32),
            shape((cut, 3 * S * lanes), F32),
            shape((cut, width), F32),
            shape((cut, S * hidden), F32),
            shape((cut, S * hidden), F32),
            shape((down_rows, width), F32),
            shape((1, cut), F32),
            shape((1, cut), F32),
            shape((1, dim), F32),
            shape((1, dim), F32),
            shape((2, heads), F32),
        ],
        compiler_params=pltpu.CompilerParams(vmem_limit_bytes=VMEM_BYTES),
    )(
        tokens, own_middle, middle_grad, u_own, w_rows, gate_rows, up_rows, out_rows, down_moved, layer_own, vec_got,
        gain_attn[None, :],
    )
    return (*out[:7], *[row[0] for row in out[7:11]], out[11].T)


def solution(mesh):
    by_token, by_fsdp, by_owner = P(("fsdp", "seq"), None), P("fsdp", None), P(("seq", "fsdp"), None)
    in_specs = (
        by_token,
        by_token,
        P(),
        P(),
        P(),
        P(),
        by_fsdp,
        P(),
        P(),
        P(),
        by_fsdp,
        P(),
        by_fsdp,
        by_fsdp,
        by_fsdp,
    )
    out_specs = (
        (by_token, by_token) + (by_owner,) * 5 + (P(("seq", "fsdp")),) * 2 + (P(),) * 3
    )
    return jax.shard_map(
        per_device, mesh=mesh, in_specs=in_specs, out_specs=out_specs, check_vma=False
    )
```
